32 devices in a mesh: dp: 4 (over x, core), expert: 8 (over z, y).
Axes of the slice: x: 2, y: 2, z: 4, core: 2. Of those that a mesh axis runs over, the one named last changes fastest.
Arguments:
- tokens: bfloat16 [1536, 4096], P('expert', 'dp'), may hold values from -6 to 6
- routes: int32 [1536, 2], P('expert'), may hold values from 0 to 7, all different within a row; in each aligned block of 192 rows (0 to 191, 192 to 383, ...) at most 60 rows name the same one
- route_weight: float32 [1536, 2], P('expert'), may hold values from 0.2 to 1
- cotangent: bfloat16 [1536, 4096], P('expert', 'dp'), may hold values from -4 to 4
- w_in: bfloat16 [8, 4096, 2048], P('expert', 'dp'), may hold values from -0.09375 to 0.09375
- w_out: bfloat16 [8, 1024, 4096], P('expert', None, 'dp'), may hold values from -0.1875 to 0.1875
Outputs:
- mixed: bfloat16 [1536, 4096], P('expert', 'dp')
- grad_tokens: bfloat16 [1536, 4096], P('expert', 'dp')
- grad_in: bfloat16 [8, 4096, 2048], P('expert', 'dp')
- grad_out: bfloat16 [8, 1024, 4096], P('expert', None, 'dp')
The draws below stay inside these ranges and needn't reach their ends.
Inputs may be any that keep to these rules, and one draw needn't show every extreme that they name: `routes`: each row names 2 different experts. Among the 192 rows of one index of the expert axis no expert is named more than 60 times, and in every draw some expert is named exactly 60 times by such a block.
All inputs are finite; a program needn't handle non-finite values.
Results may differ from the reference program's by a relative error of at most 0.0065.
Values may be sent and summed in bfloat16 or wider, within the bound.
No kernel may reach another device: no remote copies, remote signals or barrier semaphores. Data moves between devices by JAX's collectives and lax.ppermute only.
A program may use at most 64 MiB of HBM per device.

```python
import math
import jax
import jax.numpy as jnp
import numpy as np
from jax import lax

D = 4096
FF = 1024
TOK_DEV = 192
TOPK = 2
EXPERTS = 8
TOKENS = 1536
CAP = 60
N_EXPERT = 8


def block_levels(key, extent, shards, least, top_value):
    loudness, own = 1.0, jax.random.fold_in(key, 6)
    for position, blocks in shards:
        draws = jnp.exp(jax.random.uniform(jax.random.fold_in(own, position), (blocks,), jnp.float32, least / len(shards), top_value / len(shards)))
        loudness = loudness * jnp.repeat(draws, extent[position] // blocks).reshape([-1 if axis == position else 1 for axis in range(len(extent))])
    return loudness


def shared_out(rng, own, number, rows, count, top, bound, lean):
    ranking = jax.random.permutation(rng, count)
    crowded, common = portions_of(count, rows * top, bound, lean, True), portions_of(count, rows * top, bound, lean, False)
    places = jnp.arange(count)

    def named(lengths, offset_by):
        used = int((lengths > 0).sum())
        fixed = max(1, used // 4)
        moved = fixed + (places - fixed + offset_by * (used - fixed)) % max(1, count - fixed)
        return jnp.zeros((count,), jnp.int32).at[ranking[jnp.where(places < fixed, places, moved)]].set(jnp.asarray(lengths, jnp.int32))

    lengths = jnp.where(number % 4 == 0, named(crowded, number // 4), named(common, number - number // 4 - 1))
    mixed = jax.random.permutation(jax.random.fold_in(own, 3), count)
    giver, receiver = mixed[0:count // 2 * 2:2], mixed[1:count // 2 * 2:2]
    room = jnp.minimum(lengths[giver] - 1, bound - lengths[receiver]) // 2
    room = jnp.where((giver == ranking[0]) | (receiver == ranking[0]) | (lengths[receiver] == 0), 0, jnp.maximum(room, 0))
    moved = jax.random.randint(jax.random.fold_in(own, 4), (count // 2,), 0, 1 << 20) % (room + 1)
    lengths = lengths.at[giver].add(-moved).at[receiver].add(moved)
    items = jnp.searchsorted(jnp.cumsum(lengths), jnp.arange(rows * top), side="right").astype(jnp.int32)
    table = items.reshape(top, rows).T
    table = table[jax.random.permutation(jax.random.fold_in(own, 1), rows)]
    offset_by = jax.random.randint(jax.random.fold_in(own, 2), (rows, 1), 0, top)
    return jnp.take_along_axis(table, (jnp.arange(top)[None, :] + offset_by) % top, axis=1)


def portions_of(count, total, most, slope, full):
    portions = [(1 << 20) // math.isqrt(standing ** slope) + 1 for standing in range(1, count + 1)]
    largest = most if full else min(most, max(-(-total // count), total * portions[0] // sum(portions)))
    least = 1 if total - largest >= count - 1 else 0
    given, rest = [largest] + [least] * (count - 1), total - largest - least * (count - 1)
    while rest > 0:
        movable = [i for i in range(1, count) if given[i] < largest] or [i for i in range(1, count) if given[i] < most]
        pool, left = sum([portions[i] for i in movable]), rest
        for i in movable:
            extra = min(most - given[i], max(1, left * portions[i] // pool), rest)
            given[i] = given[i] + extra
            rest = rest - extra
    return np.array(given)


def centred(stream_key, shape, scale, reach, shards=(), held_as=jnp.bfloat16):
    result = jax.random.normal(stream_key, shape, jnp.float32) * scale
    if len(shards) > 0:
        result = block_levels(stream_key, shape, shards, -0.22, 0.18) * result
    return jnp.clip(result, min=-reach, max=reach).astype(held_as)


def setup_inputs(seed: int = 0) -> dict:
    seeds = jax.random.split(jax.random.key(seed), 7)
    tokens = centred(seeds[0], (TOKENS, D), 1.0, 6.0, ((0, 8), (1, 4)))
    routes_keys = jax.random.split(jax.random.fold_in(seeds[1], 1), TOKENS // TOK_DEV)
    routes_turns = jax.random.permutation(jax.random.fold_in(seeds[1], 3), TOKENS // TOK_DEV)
    routes = jax.vmap(lambda own, number: shared_out(jax.random.fold_in(seeds[1], 2), own, number, TOK_DEV, EXPERTS, TOPK, CAP, 2))(routes_keys, routes_turns).reshape((TOKENS, TOPK))
    route_weight = jnp.clip(0.2 + 0.8 * jax.random.uniform(seeds[2], (TOKENS, TOPK), jnp.float32) ** block_levels(seeds[2], (TOKENS, TOPK), ((0, 8),), -0.2, 0.2), 0.2, 1.0)
    cotangent = centred(seeds[3], (TOKENS, D), 0.25, 4.0, ((0, 8), (1, 4)))
    w_in = centred(seeds[4], (EXPERTS, D, 2 * FF), D ** -0.5, 0.09375, ((0, 8), (1, 4)))
    w_out = centred(seeds[5], (EXPERTS, FF, D), FF ** -0.5, 0.1875, ((0, 8), (2, 4)))
    return {"tokens": tokens, "routes": routes, "route_weight": route_weight, "cotangent": cotangent, "w_in": w_in, "w_out": w_out}


def slot_ranks(routes):
    blocks = routes.reshape(N_EXPERT, TOK_DEV * TOPK)
    onehot = (blocks[:, :, None] == jnp.arange(EXPERTS, dtype=jnp.int32)[None, None, :]).astype(jnp.int32)
    before = jnp.cumsum(onehot, axis=1) - onehot
    return jnp.sum(before * onehot, axis=-1).astype(jnp.int32)


def activate(pre_act, grad_hidden):
    gate_part = pre_act[:, :FF]
    up_part = pre_act[:, FF:]
    sigmoid_gate = jax.nn.sigmoid(gate_part)
    silu_gate = gate_part * sigmoid_gate
    hidden = (silu_gate * up_part).astype(jnp.bfloat16)
    grad_gate = grad_hidden * up_part * sigmoid_gate * (1.0 + gate_part * (1.0 - sigmoid_gate))
    grad_up = grad_hidden * silu_gate
    return hidden, jnp.concatenate([grad_gate, grad_up], axis=1).astype(jnp.bfloat16)


def expert_pass(routed_rows, routed_grads, w_in_one, w_out_one):
    pre_act = jnp.dot(routed_rows, w_in_one, preferred_element_type=jnp.float32)
    grad_hidden = jnp.dot(routed_grads, w_out_one.T, preferred_element_type=jnp.float32)
    hidden, grad_both = activate(pre_act, grad_hidden)
    out_rows = jnp.dot(hidden, w_out_one, preferred_element_type=jnp.float32).astype(jnp.bfloat16)
    grad_rows = jnp.dot(grad_both, w_in_one.T, preferred_element_type=jnp.float32).astype(jnp.bfloat16)
    grad_in_one = jnp.dot(routed_rows.T, grad_both, preferred_element_type=jnp.float32).astype(jnp.bfloat16)
    grad_out_one = jnp.dot(hidden.T, routed_grads, preferred_element_type=jnp.float32).astype(jnp.bfloat16)
    return out_rows, grad_rows, grad_in_one, grad_out_one


def reference(tokens, routes, route_weight, cotangent, w_in, w_out):
    slot_rank = slot_ranks(routes).reshape(TOKENS, TOPK)
    token_ids = jnp.broadcast_to(jnp.arange(TOKENS, dtype=jnp.int32)[:, None], (TOKENS, TOPK))
    source_dev = (token_ids // TOK_DEV).astype(jnp.int32)
    slot_place = ((routes * N_EXPERT + source_dev) * CAP + slot_rank).astype(jnp.int32)
    slot_count = EXPERTS * N_EXPERT * CAP
    slot_token = jnp.full((slot_count,), TOKENS, jnp.int32).at[slot_place.reshape(-1)].set(token_ids.reshape(-1))
    slot_weight = jnp.zeros((slot_count,), jnp.float32).at[slot_place.reshape(-1)].set(route_weight.reshape(-1))
    tokens_padded = jnp.concatenate([tokens, jnp.zeros((1, D), tokens.dtype)], axis=0)
    cotangent_padded = jnp.concatenate([cotangent, jnp.zeros((1, D), cotangent.dtype)], axis=0)
    per_slots = N_EXPERT * CAP

    def per_expert(inputs):
        expert_id, w_in_one, w_out_one = inputs
        row_index = lax.dynamic_slice_in_dim(slot_token, (expert_id * per_slots).astype(jnp.int32), per_slots)
        row_weight = lax.dynamic_slice_in_dim(slot_weight, (expert_id * per_slots).astype(jnp.int32), per_slots)
        routed_rows = tokens_padded[row_index]
        routed_grads = (row_weight[:, None] * cotangent_padded[row_index].astype(jnp.float32)).astype(jnp.bfloat16)
        return expert_pass(routed_rows, routed_grads, w_in_one, w_out_one)

    out_rows, grad_rows, grad_in, grad_out = lax.map(per_expert, (jnp.arange(EXPERTS, dtype=jnp.int32), w_in, w_out))
    route_out = out_rows.reshape(slot_count, D)[slot_place].astype(jnp.float32)
    mixed = jnp.sum(route_weight[:, :, None] * route_out, axis=1).astype(jnp.bfloat16)
    route_grad = grad_rows.reshape(slot_count, D)[slot_place].astype(jnp.float32)
    grad_tokens = jnp.sum(route_grad, axis=1).astype(jnp.bfloat16)
    return mixed, grad_tokens, grad_in, grad_out
```

```python
import jax
import jax.numpy as jnp
from jax import lax
from jax.experimental import pallas as pl
from jax.experimental.pallas import tpu as pltpu
from jax.sharding import PartitionSpec as P

BF = jnp.bfloat16
F32 = jnp.float32
VMEM_LIMIT = 48 * 1024 * 1024


def dot(a, b):
    return lax.dot_general(a, b, (((1,), (0,)), ((), ())), preferred_element_type=F32)


def dot_t(a, b):
    return lax.dot_general(a, b, (((1,), (1,)), ((), ())), preferred_element_type=F32)


def t_dot(a, b):
    return lax.dot_general(a, b, (((0,), (0,)), ((), ())), preferred_element_type=F32)


def iota(shape, dim):
    return lax.broadcasted_iota(jnp.int32, shape, dim)


def padded(capacity):
    return -(-capacity // 16) * 16


def prep_kernel(capacity, ids, tokens, routes, weight, cotangent, *outs):
    count = len(outs)
    rows = tokens.shape[0]
    me = ids[0]
    eye = iota((rows, rows), 0) == iota((rows, rows), 1)

    def lane(column, zero):
        return jnp.sum(jnp.where(eye, column, zero), axis=0, keepdims=True)

    first, second = lane(routes[:, 0:1], 0), lane(routes[:, 1:2], 0)
    w_first, w_second = lane(weight[:, 0:1], 0.0), lane(weight[:, 1:2], 0.0)
    expert = iota((count, rows), 0) ^ me
    hit_first, hit_second = first == expert, second == expert
    named = hit_first | hit_second
    w_named = jnp.where(hit_first, w_first, 0.0) + jnp.where(hit_second, w_second, 0.0)
    before = (iota((rows, rows), 0) < iota((rows, rows), 1)).astype(BF)
    rank = dot(named.astype(F32).astype(BF), before).astype(jnp.int32)
    key = jnp.where(named, rank, -2 * capacity)
    slot = iota((2 * capacity, rows), 0)
    for s, out in enumerate(outs):
        row_key = key[s : s + 1, :]
        pick_token = (row_key == slot).astype(F32)
        pick_grad = (row_key + capacity == slot).astype(F32)
        scale = jnp.sum(pick_grad * w_named[s : s + 1, :], axis=1, keepdims=True)
        scale = scale + (slot[:, 0:1] < capacity).astype(F32)
        picked = dot(pick_token.astype(BF), tokens[...]) + dot(pick_grad.astype(BF), cotangent[...])
        out[...] = (scale * picked).astype(BF)


def prep(ids, tokens, routes, weight, cotangent, count, capacity):
    rows, features = tokens.shape
    whole = pl.BlockSpec(memory_space=pltpu.VMEM)
    return pl.pallas_call(
        lambda *refs: prep_kernel(capacity, *refs),
        out_shape=[jax.ShapeDtypeStruct((2 * capacity, features), BF)] * count,
        in_specs=[pl.BlockSpec(memory_space=pltpu.SMEM)] + [whole] * 4,
        out_specs=[whole] * count,
        compiler_params=pltpu.CompilerParams(vmem_limit_bytes=VMEM_LIMIT),
        cost_estimate=pl.CostEstimate(
            flops=8 * count * capacity * rows * features,
            bytes_accessed=4 * (rows + count * capacity) * features,
            transcendentals=0,
        ),
        name="prep",
    )(ids, tokens, routes, weight, cotangent)


def up_kernel(count, capacity, ids, *refs):
    blocks, (w_gate, w_up, w_out, row_out, grad_out, send, keep) = refs[:count], refs[count:]
    step = pl.program_id(0)
    pad = padded(capacity)

    @pl.when(step == 0)
    def _():
        spot = iota((2 * pad, 2 * capacity), 0)
        col = iota((2 * pad, 2 * capacity), 1)
        target = jnp.where(col < capacity, col, col + pad - capacity)
        spread = (spot == target).astype(F32).astype(BF)
        for i, block in enumerate(blocks):
            laid = dot(spread, block[...]).astype(BF)
            row_out[pl.ds(i * pad, pad), :] = laid[:pad]
            grad_out[pl.ds(i * pad, pad), :] = laid[pad:]

    gate = dot(row_out[...], w_gate[...])
    up = dot(row_out[...], w_up[...])
    back = dot_t(grad_out[...], w_out[...])
    width = gate.shape[1]

    @pl.when(step < 2)
    def _():
        send[:, 0:width] = gate.astype(BF)
        send[:, width : 2 * width] = up.astype(BF)
        send[:, 2 * width :] = back.astype(BF)

    @pl.when(step >= 2)
    def _():
        keep[:, 0:width] = gate
        keep[:, width : 2 * width] = up
        keep[:, 2 * width :] = back


def up_step(ids, blocks, w_in, w_out, capacity):
    features, both_units = w_in.shape
    units = both_units // 2
    width = units // 4
    count = len(blocks)
    pad = padded(capacity)
    rows = count * pad

    def tile(step, ids):
        half = jnp.where(step < 2, 1 - ids[1], ids[1])
        return half * 2 + step % 2

    return pl.pallas_call(
        lambda *refs: up_kernel(count, capacity, *refs),
        grid_spec=pltpu.PrefetchScalarGridSpec(
            num_scalar_prefetch=1,
            grid=(4,),
            in_specs=[pl.BlockSpec((2 * capacity, features), lambda j, ids: (0, 0))] * count
            + [
                pl.BlockSpec((features, width), lambda j, ids: (0, tile(j, ids))),
                pl.BlockSpec((features, width), lambda j, ids: (0, 4 + tile(j, ids))),
                pl.BlockSpec((width, features), lambda j, ids: (tile(j, ids), 0)),
            ],
            out_specs=[
                pl.BlockSpec((rows, features), lambda j, ids: (0, 0)),
                pl.BlockSpec((rows, features), lambda j, ids: (0, 0)),
                pl.BlockSpec((rows, 3 * width), lambda j, ids: (0, jnp.minimum(j, 1))),
                pl.BlockSpec((rows, 3 * width), lambda j, ids: (0, jnp.maximum(j - 2, 0))),
            ],
        ),
        out_shape=[
            jax.ShapeDtypeStruct((rows, features), BF),
            jax.ShapeDtypeStruct((rows, features), BF),
            jax.ShapeDtypeStruct((rows, 6 * width), BF),
            jax.ShapeDtypeStruct((rows, 6 * width), F32),
        ],
        compiler_params=pltpu.CompilerParams(vmem_limit_bytes=VMEM_LIMIT),
        cost_estimate=pl.CostEstimate(
            flops=6 * rows * features * units,
            bytes_accessed=6 * features * units + 12 * rows * features,
            transcendentals=0,
        ),
        name="up",
    )(ids, *blocks, w_in, w_in, w_out)


def act_kernel(total, other, out):
    width = total.shape[1] // 6
    for j in range(2):
        base = 3 * width * j
        gate, up, back = (
            total[:, base + i * width : base + (i + 1) * width]
            + other[:, base + i * width : base + (i + 1) * width].astype(F32)
            for i in range(3)
        )
        sigmoid = jax.nn.sigmoid(gate)
        silu = gate * sigmoid
        out[:, base : base + width] = (silu * up).astype(BF)
        out[:, base + width : base + 2 * width] = (
            back * up * sigmoid * (1.0 + gate * (1.0 - sigmoid))
        ).astype(BF)
        out[:, base + 2 * width : base + 3 * width] = (back * silu).astype(BF)


def act_step(total, other):
    whole = pl.BlockSpec(memory_space=pltpu.VMEM)
    return pl.pallas_call(
        act_kernel,
        out_shape=jax.ShapeDtypeStruct(total.shape, BF),
        in_specs=[whole] * 2,
        out_specs=whole,
        compiler_params=pltpu.CompilerParams(vmem_limit_bytes=VMEM_LIMIT),
        cost_estimate=pl.CostEstimate(
            flops=4 * total.size, bytes_accessed=8 * total.size, transcendentals=total.size
        ),
        name="act",
    )(total, other)


def down_kernel(count, capacity, ids, own, core, w_in, w_out, *outs):
    pad = padded(capacity)
    units = w_out.shape[0]
    width = units // 4
    out_rows = grad_rows = None
    for held, half in ((own, ids[1]), (core, 1 - ids[1])):
        for j in range(2):
            base = 3 * width * j
            at = pl.multiple_of((half * 2 + j) * width, width)
            at_up = pl.multiple_of(units + (half * 2 + j) * width, width)
            a = dot(held[:, base : base + width], w_out[pl.ds(at, width), :])
            b = dot_t(held[:, base + width : base + 2 * width], w_in[:, pl.ds(at, width)])
            c = dot_t(held[:, base + 2 * width : base + 3 * width], w_in[:, pl.ds(at_up, width)])
            out_rows = a if out_rows is None else out_rows + a
            grad_rows = b + c if grad_rows is None else grad_rows + (b + c)
    spot = iota((2 * capacity, pad), 0)
    col = iota((2 * capacity, pad), 1)
    pack_out = (spot == jnp.where(col < capacity, col, -1)).astype(F32).astype(BF)
    pack_grad = (spot - capacity == jnp.where(col < capacity, col, -capacity - 1)).astype(F32).astype(BF)
    out_rows, grad_rows = out_rows.astype(BF), grad_rows.astype(BF)
    for i, out in enumerate(outs):
        out[...] = (
            dot(pack_out, out_rows[i * pad : (i + 1) * pad])
            + dot(pack_grad, grad_rows[i * pad : (i + 1) * pad])
        ).astype(BF)


def down_step(ids, own, core, w_in, w_out, count, capacity):
    features, both_units = w_in.shape
    units = both_units // 2
    rows = own.shape[0]
    width = features // 4
    return pl.pallas_call(
        lambda *refs: down_kernel(count, capacity, *refs),
        grid_spec=pltpu.PrefetchScalarGridSpec(
            num_scalar_prefetch=1,
            grid=(4,),
            in_specs=[
                pl.BlockSpec(own.shape, lambda j, ids: (0, 0)),
                pl.BlockSpec(core.shape, lambda j, ids: (0, 0)),
                pl.BlockSpec((width, both_units), lambda j, ids: (j, 0)),
                pl.BlockSpec((units, width), lambda j, ids: (0, j)),
            ],
            out_specs=[pl.BlockSpec((2 * capacity, width), lambda j, ids: (0, j))] * count,
        ),
        out_shape=[jax.ShapeDtypeStruct((2 * capacity, features), BF)] * count,
        compiler_params=pltpu.CompilerParams(vmem_limit_bytes=VMEM_LIMIT),
        cost_estimate=pl.CostEstimate(
            flops=6 * rows * features * units,
            bytes_accessed=6 * features * units + 12 * rows * features,
            transcendentals=0,
        ),
        name="down",
    )(ids, own, core, w_in, w_out)


def grads_kernel(chunks, ids, *refs):
    groups = [refs[5 * i : 5 * i + 5] for i in range(chunks)]
    grad_in, grad_out = refs[5 * chunks :]
    step = pl.program_id(0)
    width = groups[0][2].shape[1] // 6
    units = grad_in.shape[1] // 2
    for which, half in ((2, ids[1]), (3, 1 - ids[1])):
        for j in range(2):
            base = 3 * width * j
            for part in range(2):
                total = None
                for group in groups:
                    term = t_dot(
                        group[0][...],
                        group[which][:, base + (part + 1) * width : base + (part + 2) * width],
                    )
                    total = term if total is None else total + term
                at = pl.multiple_of(part * units + (half * 2 + j) * width, width)
                grad_in[:, pl.ds(at, width)] = total.astype(BF)
    for at_step in range(4):

        @pl.when(step == at_step)
        def _():
            which, j = 2 + at_step // 2, at_step % 2
            base = 3 * width * j
            total = None
            for group in groups:
                term = t_dot(group[which][:, base : base + width], group[4][...])
                total = term if total is None else total + term
            grad_out[...] = total.astype(BF)


def grads_step(ids, groups, units):
    features = groups[0][0].shape[1]
    f_tile, u_tile = features // 4, units // 4
    operands, specs = [], []
    rows_all = 0
    for rows, grads, own, core in groups:
        operands += [rows, own, core, grads]
        n = rows.shape[0]
        rows_all += n
        specs += [
            pl.BlockSpec((n, f_tile), lambda j, ids: (0, j)),
            pl.BlockSpec(own.shape, lambda j, ids: (0, 0)),
            pl.BlockSpec(core.shape, lambda j, ids: (0, 0)),
            pl.BlockSpec(grads.shape, lambda j, ids: (0, 0)),
        ]

    def unit_tile(j, ids):
        return jnp.where(j < 2, ids[1] * 2 + j, (1 - ids[1]) * 2 + j - 2)

    def kernel(ids, *refs):
        laid = []
        for i in range(len(groups)):
            rows, own, core, grads = refs[4 * i : 4 * i + 4]
            laid += [rows, rows, own, core, grads]
        grads_kernel(len(groups), ids, *laid, *refs[4 * len(groups) :])

    return pl.pallas_call(
        kernel,
        grid_spec=pltpu.PrefetchScalarGridSpec(
            num_scalar_prefetch=1,
            grid=(4,),
            in_specs=specs,
            out_specs=[
                pl.BlockSpec((f_tile, 2 * units), lambda j, ids: (j, 0)),
                pl.BlockSpec((u_tile, features), lambda j, ids: (unit_tile(j, ids), 0)),
            ],
        ),
        out_shape=[
            jax.ShapeDtypeStruct((features, 2 * units), BF),
            jax.ShapeDtypeStruct((units, features), BF),
        ],
        compiler_params=pltpu.CompilerParams(vmem_limit_bytes=VMEM_LIMIT),
        cost_estimate=pl.CostEstimate(
            flops=6 * rows_all * features * units,
            bytes_accessed=6 * features * units + 12 * rows_all * features,
            transcendentals=0,
        ),
        name="grads",
    )(ids, *operands)


def final_kernel(capacity, ids, routes, weight, *refs):
    homes, (mixed, grad_tokens) = refs[:-2], refs[-2:]
    rows = routes.shape[0]
    me = ids[0]
    count = len(homes)
    first, second = routes[:, 0:1], routes[:, 1:2]
    expert = iota((rows, count), 1) ^ me
    hit_first, hit_second = first == expert, second == expert
    named = hit_first | hit_second
    w_named = jnp.where(hit_first, weight[:, 0:1], 0.0) + jnp.where(hit_second, weight[:, 1:2], 0.0)
    before = (iota((rows, rows), 1) < iota((rows, rows), 0)).astype(BF)
    rank = dot(before, named.astype(F32).astype(BF)).astype(jnp.int32)
    key = jnp.where(named, rank, -2 * capacity)
    slot = iota((rows, 2 * capacity), 1)
    total_out = total_grad = None
    for s, home in enumerate(homes):
        column = key[:, s : s + 1]
        pick_out = (column == slot).astype(F32).astype(BF)
        pick_grad = (column + capacity == slot).astype(F32).astype(BF)
        out = w_named[:, s : s + 1] * dot(pick_out, home[...])
        grad = dot(pick_grad, home[...])
        total_out = out if total_out is None else total_out + out
        total_grad = grad if total_grad is None else total_grad + grad
    mixed[...] = total_out.astype(BF)
    grad_tokens[...] = total_grad.astype(BF)


def final(ids, routes, weight, homes, capacity):
    rows = routes.shape[0]
    features = homes[0].shape[1]
    width = features // 4
    count = len(homes)
    return pl.pallas_call(
        lambda *refs: final_kernel(capacity, *refs),
        grid_spec=pltpu.PrefetchScalarGridSpec(
            num_scalar_prefetch=1,
            grid=(4,),
            in_specs=[
                pl.BlockSpec(routes.shape, lambda j, ids: (0, 0)),
                pl.BlockSpec(weight.shape, lambda j, ids: (0, 0)),
            ]
            + [pl.BlockSpec((2 * capacity, width), lambda j, ids: (0, j))] * count,
            out_specs=[pl.BlockSpec((rows, width), lambda j, ids: (0, j))] * 2,
        ),
        out_shape=[jax.ShapeDtypeStruct((rows, features), BF)] * 2,
        compiler_params=pltpu.CompilerParams(vmem_limit_bytes=VMEM_LIMIT),
        cost_estimate=pl.CostEstimate(
            flops=8 * count * capacity * rows * features,
            bytes_accessed=4 * (rows + count * capacity) * features,
            transcendentals=0,
        ),
        name="final",
    )(ids, routes, weight, *homes)


def per_device_chunked(tokens, routes, route_weight, cotangent, w_in, w_out):
    tok_rows = tokens.shape[0]
    top_count = routes.shape[1]
    n_expert = lax.axis_size("expert")
    n_dp = lax.axis_size("dp")
    capacity = tok_rows * top_count * 5 // (4 * n_expert)
    w_in, w_out = w_in[0], w_out[0]
    units = w_out.shape[0]
    ids = jnp.stack([lax.axis_index("expert"), lax.axis_index("dp") % 2]).astype(jnp.int32)

    def across(x, s):
        return lax.ppermute(x, "expert", [(i, i ^ s) for i in range(n_expert)]) if s else x

    def beside(x, s):
        return lax.ppermute(x, "dp", [(i, i ^ s) for i in range(n_dp)])

    half, quarter = n_expert // 2, n_expert // 4
    plan = [list(range(half)), list(range(half, half + quarter)), list(range(half + quarter, n_expert))]
    sent = prep(ids, tokens, routes, route_weight, cotangent, n_expert, capacity)
    homes = [None] * n_expert
    groups = []
    for sources in plan:
        blocks = [across(sent[s], s) for s in sources]
        rows, grads, send, keep = up_step(ids, blocks, w_in, w_out, capacity)
        total = keep + beside(send, 1).astype(F32)
        own = act_step(total, beside(total.astype(BF), 2))
        core = beside(own, 1)
        groups.append((rows, grads, own, core))
        back = down_step(ids, own, core, w_in, w_out, len(sources), capacity)
        for s, block in zip(sources, back):
            homes[s] = across(block, s)
    grad_in, grad_out = grads_step(ids, groups, units)
    mixed, grad_tokens = final(ids, routes, route_weight, homes, capacity)
    return mixed, grad_tokens, grad_in[None], grad_out[None]


def activate(pre_act, grad_hidden):
    units = pre_act.shape[1] // 2
    gate_part = pre_act[:, :units]
    up_part = pre_act[:, units:]
    sigmoid_gate = jax.nn.sigmoid(gate_part)
    silu_gate = gate_part * sigmoid_gate
    hidden = (silu_gate * up_part).astype(jnp.bfloat16)
    grad_gate = grad_hidden * up_part * sigmoid_gate * (1.0 + gate_part * (1.0 - sigmoid_gate))
    grad_up = grad_hidden * silu_gate
    return (hidden, jnp.concatenate([grad_gate, grad_up], axis=1).astype(jnp.bfloat16))


def per_device(tokens, routes, route_weight, cotangent, w_in, w_out):
    tok_rows, features = tokens.shape
    top_count = routes.shape[1]
    n_expert = lax.axis_size("expert")
    local_experts = w_in.shape[0]
    hidden_units = w_out.shape[1]
    experts = n_expert * local_experts
    capacity = tok_rows * top_count * 5 // (4 * experts)
    slot_count = experts * capacity
    flat_routes = routes.reshape(-1)
    onehot = (flat_routes[:, None] == jnp.arange(experts, dtype=jnp.int32)[None, :]).astype(
        jnp.int32
    )
    slot_rank = jnp.sum((jnp.cumsum(onehot, axis=0) - onehot) * onehot, axis=1)
    target = flat_routes * capacity + slot_rank
    placing = (target[None, :] == jnp.arange(slot_count, dtype=jnp.int32)[:, None]).astype(
        jnp.bfloat16
    )
    choose_token = jnp.sum(placing.reshape(slot_count, tok_rows, top_count), axis=2)
    scaled_grads = (route_weight[:, :, None] * cotangent[:, None, :].astype(jnp.float32)).astype(
        jnp.bfloat16
    )
    scaled_grads = scaled_grads.reshape(tok_rows * top_count, features)
    send_rows = jnp.dot(choose_token, tokens, preferred_element_type=jnp.float32).astype(
        jnp.bfloat16
    )
    send_grads = jnp.dot(placing, scaled_grads, preferred_element_type=jnp.float32).astype(
        jnp.bfloat16
    )
    send_rows = send_rows.reshape(n_expert, local_experts * capacity, features)
    send_grads = send_grads.reshape(n_expert, local_experts * capacity, features)
    routed_rows, routed_grads = (
        lax.all_to_all(send_rows, "expert", split_axis=0, concat_axis=0, tiled=True),
        lax.all_to_all(send_grads, "expert", split_axis=0, concat_axis=0, tiled=True),
    )
    rows_four = routed_rows.reshape(n_expert, local_experts, capacity, features)
    grads_four = routed_grads.reshape(n_expert, local_experts, capacity, features)
    total_rows = n_expert * local_experts * capacity
    pre_part = jnp.einsum("secd,edf->secf", rows_four, w_in, preferred_element_type=jnp.float32)
    back_part = jnp.einsum("secd,efd->secf", grads_four, w_out, preferred_element_type=jnp.float32)
    pre_flat = pre_part.reshape(total_rows, 2 * hidden_units)
    back_flat = back_part.reshape(total_rows, hidden_units)
    pre_share, back_share = (
        lax.psum_scatter(pre_flat, "dp", scatter_dimension=0, tiled=True),
        lax.psum_scatter(back_flat, "dp", scatter_dimension=0, tiled=True),
    )
    hidden_share, both_share = activate(pre_share, back_share)
    hidden, grad_both = (
        lax.all_gather(hidden_share, "dp", axis=0, tiled=True),
        lax.all_gather(both_share, "dp", axis=0, tiled=True),
    )
    hidden_four = hidden.reshape(n_expert, local_experts, capacity, hidden_units)
    both_four = grad_both.reshape(n_expert, local_experts, capacity, 2 * hidden_units)
    out_rows = jnp.einsum(
        "secf,efd->secd", hidden_four, w_out, preferred_element_type=jnp.float32
    ).astype(jnp.bfloat16)
    grad_rows = jnp.einsum(
        "secf,edf->secd", both_four, w_in, preferred_element_type=jnp.float32
    ).astype(jnp.bfloat16)
    grad_out = jnp.einsum(
        "secf,secd->efd", hidden_four, grads_four, preferred_element_type=jnp.float32
    ).astype(jnp.bfloat16)
    grad_in = jnp.einsum(
        "secd,secf->edf", rows_four, both_four, preferred_element_type=jnp.float32
    ).astype(jnp.bfloat16)
    home_out, home_grad = (
        lax.all_to_all(
            out_rows.reshape(n_expert, local_experts * capacity, features),
            "expert",
            split_axis=0,
            concat_axis=0,
            tiled=True,
        ),
        lax.all_to_all(
            grad_rows.reshape(n_expert, local_experts * capacity, features),
            "expert",
            split_axis=0,
            concat_axis=0,
            tiled=True,
        ),
    )
    route_out = jnp.dot(
        placing.T, home_out.reshape(slot_count, features), preferred_element_type=jnp.float32
    )
    route_out = route_out.reshape(tok_rows, top_count, features)
    mixed = jnp.sum(route_weight[:, :, None] * route_out, axis=1).astype(jnp.bfloat16)
    grad_tokens = jnp.dot(
        choose_token.T, home_grad.reshape(slot_count, features), preferred_element_type=jnp.float32
    )
    return (mixed, grad_tokens.astype(jnp.bfloat16), grad_in, grad_out)


def solution(mesh):
    placed = (
        P("expert", "dp"),
        P("expert", None),
        P("expert", None),
        P("expert", "dp"),
        P("expert", "dp", None),
        P("expert", None, "dp"),
    )
    sizes = dict(mesh.shape)
    chunked = sizes["dp"] == 4 and sizes["expert"] in (4, 8)
    return jax.shard_map(
        per_device_chunked if chunked else per_device,
        mesh=mesh,
        in_specs=placed,
        out_specs=(
            P("expert", "dp"),
            P("expert", "dp"),
            P("expert", "dp", None),
            P("expert", None, "dp"),
        ),
        check_vma=False,
    )
```

```python
import jax
import jax.numpy as jnp
from jax import lax
from jax.experimental import pallas as pl
from jax.experimental.pallas import tpu as pltpu
from jax.sharding import PartitionSpec as P

BF = jnp.bfloat16
F32 = jnp.float32
VMEM_LIMIT = 18 * 1024 * 1024
GRADS_LIMIT = 32 * 1024 * 1024
FIRST_LIMIT = 54 * 1024 * 1024
PREP_LIMIT = 60 * 1024 * 1024
COST = pl.CostEstimate(flops=1, bytes_accessed=1, transcendentals=0)


def dot(a, b):
    return lax.dot_general(a, b, (((1,), (0,)), ((), ())), preferred_element_type=F32)


def dot_t(a, b):
    return lax.dot_general(a, b, (((1,), (1,)), ((), ())), preferred_element_type=F32)


def t_dot(a, b):
    return lax.dot_general(a, b, (((0,), (0,)), ((), ())), preferred_element_type=F32)


def iota(shape, dim):
    return lax.broadcasted_iota(jnp.int32, shape, dim)


def padded(capacity):
    return -(-capacity // 16) * 16


def prep_kernel(capacity, ids, tokens, routes, weight, cotangent, *refs):
    outs, (token_rows, grad_rows, route_lines, weight_lines, sems) = refs[:-5], refs[-5:]
    pairs = ((routes, route_lines), (weight, weight_lines), (tokens, token_rows), (cotangent, grad_rows))
    copies = [pltpu.make_async_copy(x, held, sems.at[i]) for i, (x, held) in enumerate(pairs)]
    for copy in copies:
        copy.start()
    for copy in copies[:2]:
        copy.wait()
    routes, weight = route_lines, weight_lines
    count = len(outs)
    rows = routes.shape[1]
    expert = iota((count, rows), 0) ^ ids[0]
    named, w_named = None, None
    for k in range(routes.shape[0]):
        hit = routes[k : k + 1, :] == expert
        w_hit = jnp.where(hit, weight[k : k + 1, :], 0.0)
        named = hit if named is None else named | hit
        w_named = w_hit if w_named is None else w_named + w_hit
    before = (iota((rows, rows), 0) < iota((rows, rows), 1)).astype(F32).astype(BF)
    rank = dot(named.astype(F32).astype(BF), before).astype(jnp.int32)
    key = jnp.where(named, rank, -2 * capacity)
    slot = iota((2 * capacity, rows), 0)
    picks = []
    for s in range(count):
        row_key = key[s : s + 1, :]
        pick_token = (row_key == slot).astype(F32)
        pick_grad = (row_key + capacity == slot).astype(F32)
        scale = jnp.sum(pick_grad * w_named[s : s + 1, :], axis=1, keepdims=True)
        scale = scale + (slot[:, 0:1] < capacity).astype(F32)
        picks.append((pick_token.astype(BF), pick_grad.astype(BF), scale))
    for copy in copies[2:]:
        copy.wait()
    for out, (pick_token, pick_grad, scale) in zip(outs, picks):
        out[...] = (scale * (dot(pick_token, token_rows[...]) + dot(pick_grad, grad_rows[...]))).astype(BF)


def prep(ids, tokens, routes, weight, cotangent, count, capacity):
    rows, features = tokens.shape
    whole = pl.BlockSpec(memory_space=pltpu.VMEM)
    away = pl.BlockSpec(memory_space=pltpu.HBM)
    return pl.pallas_call(
        lambda *refs: prep_kernel(capacity, *refs),
        out_shape=[jax.ShapeDtypeStruct((2 * capacity, features), BF)] * count,
        in_specs=[pl.BlockSpec(memory_space=pltpu.SMEM)] + [away] * 4,
        out_specs=[whole] * count,
        scratch_shapes=[pltpu.VMEM((rows, features), BF)] * 2
        + [pltpu.VMEM(routes.T.shape, routes.dtype), pltpu.VMEM(weight.T.shape, weight.dtype)]
        + [pltpu.SemaphoreType.DMA((4,))],
        compiler_params=pltpu.CompilerParams(vmem_limit_bytes=PREP_LIMIT),
        cost_estimate=COST,
        name="prep",
    )(ids, tokens, routes.T, weight.T, cotangent)


def call(kernel, name, out_shapes, scalars, *arrays):
    whole = pl.BlockSpec(memory_space=pltpu.VMEM)
    return pl.pallas_call(
        kernel,
        out_shape=out_shapes,
        in_specs=[pl.BlockSpec(memory_space=pltpu.SMEM)] * len(scalars) + [whole] * len(arrays),
        out_specs=jax.tree.map(lambda _: whole, out_shapes),
        compiler_params=pltpu.CompilerParams(vmem_limit_bytes=VMEM_LIMIT),
        cost_estimate=COST,
        name=name,
    )(*scalars, *arrays)


def up_kernel(capacity, held, ids, *refs):
    if held:
        blocks, (*parts, w_out, row_out, grad_out, send, keep, sent) = refs[:-8], refs[-8:]
    else:
        blocks, (far_in, far_out, row_out, grad_out, send, keep, *parts, w_out, sent, sems) = refs[:-11], refs[-11:]
    depth, both_units = parts[0].shape
    units = both_units // 2
    width = units // 4
    copies = []
    if not held:
        for k, part in enumerate(parts):
            copies.append(pltpu.make_async_copy(far_in.at[k * depth : (k + 1) * depth, :], part, sems.at[k]))
        copies.append(pltpu.make_async_copy(far_out, w_out, sems.at[len(parts)]))
        for copy in copies:
            copy.start()
    pad = padded(capacity)
    spot = iota((2 * pad, 2 * capacity), 0)
    col = iota((2 * pad, 2 * capacity), 1)
    target = jnp.where(col < capacity, col, col + pad - capacity)
    spread = (spot == target).astype(F32).astype(BF)
    for i, block in enumerate(blocks):
        laid = dot(spread, block[...]).astype(BF)
        row_out[i * pad : (i + 1) * pad, :] = laid[:pad]
        grad_out[i * pad : (i + 1) * pad, :] = laid[pad:]
    tiles = [(out, half, j) for out, half in ((sent, 1 - ids[1]), (keep, ids[1])) for j in range(2)]
    for k, w_in in enumerate(parts):
        if not held:
            copies[k].wait()
        at = slice(k * depth, (k + 1) * depth)
        for out, half, j in tiles:
            for part in range(2):
                base = (3 * j + part) * width
                column = pl.multiple_of(part * units + (half * 2 + j) * width, width)
                term = dot(row_out[:, at], w_in[:, pl.ds(column, width)])
                if k:
                    out[:, base : base + width] += term
                else:
                    out[:, base : base + width] = term
    if not held:
        copies[-1].wait()
    for out, half, j in tiles:
        row = pl.multiple_of((half * 2 + j) * width, width)
        out[:, (3 * j + 2) * width : (3 * j + 3) * width] = dot_t(grad_out[...], w_out[pl.ds(row, width), :])
    send[...] = sent[...].astype(BF)


def up_step(ids, blocks, weights, capacity, held):
    *_, w_out = weights
    units, features = w_out.shape
    rows = len(blocks) * padded(capacity)
    shape = jax.ShapeDtypeStruct
    whole = pl.BlockSpec(memory_space=pltpu.VMEM)
    away = pl.BlockSpec(memory_space=pl.ANY)
    out_shape = [
        shape((rows, features), BF),
        shape((rows, features), BF),
        shape((rows, 3 * units // 2), BF),
        shape((rows, 3 * units // 2), F32),
    ]
    scratch = [pltpu.VMEM((rows, 3 * units // 2), F32)]
    if not held:
        out_shape += [shape((features // 2, 2 * units), BF)] * 2 + [shape(w_out.shape, BF)]
        scratch += [pltpu.SemaphoreType.DMA((3,))]
    return pl.pallas_call(
        lambda *refs: up_kernel(capacity, held, *refs),
        out_shape=out_shape,
        in_specs=[pl.BlockSpec(memory_space=pltpu.SMEM)]
        + [whole] * len(blocks)
        + [whole if held else away] * len(weights),
        out_specs=[whole] * len(out_shape),
        scratch_shapes=scratch,
        compiler_params=pltpu.CompilerParams(vmem_limit_bytes=VMEM_LIMIT if held else FIRST_LIMIT),
        cost_estimate=COST,
        name="up",
    )(ids, *blocks, *weights)


def sum_kernel(keep, core, out):
    out[...] = (keep[...] + core[...].astype(F32)).astype(BF)


def sum_step(keep, core):
    return call(sum_kernel, "total", jax.ShapeDtypeStruct(keep.shape, BF), [], keep, core)


def act_kernel(keep, core, other, out):
    width = keep.shape[1] // 6
    for j in range(2):
        base = 3 * width * j
        gate, up, back = (
            keep[:, at : at + width] + core[:, at : at + width].astype(F32) + other[:, at : at + width].astype(F32)
            for at in (base, base + width, base + 2 * width)
        )
        sigmoid = jax.nn.sigmoid(gate)
        silu = gate * sigmoid
        out[:, base : base + width] = (silu * up).astype(BF)
        out[:, base + width : base + 2 * width] = (
            back * up * sigmoid * (1.0 + gate * (1.0 - sigmoid))
        ).astype(BF)
        out[:, base + 2 * width : base + 3 * width] = (back * silu).astype(BF)


def act_step(keep, core, other):
    return call(act_kernel, "act", jax.ShapeDtypeStruct(keep.shape, BF), [], keep, core, other)


def down_kernel(capacity, cuts, ids, own, core, *refs):
    *parts, w_out = refs[:3]
    outs = refs[3:]
    pad = padded(capacity)
    units = w_out.shape[0]
    width = units // 4
    out_rows, grad_parts = None, [None] * len(parts)
    for held, half in ((own, ids[1]), (core, 1 - ids[1])):
        for j in range(2):
            base = 3 * width * j
            at = pl.multiple_of((half * 2 + j) * width, width)
            at_up = pl.multiple_of(units + (half * 2 + j) * width, width)
            a = dot(held[:, base : base + width], w_out[pl.ds(at, width), :])
            out_rows = a if out_rows is None else out_rows + a
            for k, w_in in enumerate(parts):
                b = dot_t(held[:, base + width : base + 2 * width], w_in[:, pl.ds(at, width)])
                b = b + dot_t(held[:, base + 2 * width : base + 3 * width], w_in[:, pl.ds(at_up, width)])
                grad_parts[k] = b if grad_parts[k] is None else grad_parts[k] + b
    grad_rows = jnp.concatenate(grad_parts, axis=1)
    spot = iota((2 * capacity, pad), 0)
    col = iota((2 * capacity, pad), 1)
    pack_out = (spot == jnp.where(col < capacity, col, -1)).astype(F32).astype(BF)
    pack_grad = (spot - capacity == jnp.where(col < capacity, col, -capacity - 1)).astype(F32).astype(BF)
    out_rows, grad_rows = out_rows.astype(BF), grad_rows.astype(BF)
    for i in range(out_rows.shape[0] // pad):
        packed = (
            dot(pack_out, out_rows[i * pad : (i + 1) * pad])
            + dot(pack_grad, grad_rows[i * pad : (i + 1) * pad])
        ).astype(BF)
        cut = packed.shape[1] // cuts
        for j in range(cuts):
            outs[i * cuts + j][...] = packed[:, j * cut : (j + 1) * cut]


def down_step(ids, own, core, weights, count, capacity, cuts):
    features = weights[-1].shape[1]
    outs = call(
        lambda *refs: down_kernel(capacity, cuts, *refs),
        "down",
        [jax.ShapeDtypeStruct((2 * capacity, features // cuts), BF)] * (count * cuts),
        [ids],
        own,
        core,
        *weights,
    )
    return [outs[i * cuts : (i + 1) * cuts] for i in range(count)]


def grads_kernel(count, ids, *refs):
    groups = [refs[4 * i : 4 * i + 4] for i in range(count)]
    grad_in, grad_out, rows, grads, own, core, tiles_in, tiles_out, sems = refs[4 * count :]
    at = 0
    for group in groups:
        n = group[0].shape[0]
        for held, part in zip((rows, grads, own, core), group):
            held[at : at + n, :] = part[...]
        at += n
    features, units = rows.shape[1], grad_out.shape[0]
    f_tile, width = features // 4, units // 4
    copies = []
    for j in range(4):
        turned = rows[:, j * f_tile : (j + 1) * f_tile].T
        for held, half in ((own, ids[1]), (core, 1 - ids[1])):
            for i in range(2):
                both = dot(turned, held[:, (3 * i + 1) * width : (3 * i + 3) * width]).astype(BF)
                for part in range(2):
                    to = pl.multiple_of(part * units + (half * 2 + i) * width, width)
                    tiles_in[j, :, pl.ds(to, width)] = both[:, part * width : (part + 1) * width]
        copies.append(pltpu.make_async_copy(tiles_in.at[j], grad_in.at[j * f_tile : (j + 1) * f_tile, :], sems.at[j]))
        copies[-1].start()
    for j, (held, half) in enumerate(((own, ids[1]), (core, 1 - ids[1]))):
        for i in range(2):
            turned = held[:, 3 * i * width : (3 * i + 1) * width].T
            tiles_out[2 * j + i] = dot(turned, grads[...]).astype(BF)
            to = pl.multiple_of((half * 2 + i) * width, width)
            copies.append(pltpu.make_async_copy(tiles_out.at[2 * j + i], grad_out.at[pl.ds(to, width), :], sems.at[4 + 2 * j + i]))
            copies[-1].start()
    for copy in copies:
        copy.wait()


def grads_step(ids, groups, units):
    features = groups[0][0].shape[1]
    rows = sum(group[0].shape[0] for group in groups)
    whole = pl.BlockSpec(memory_space=pltpu.VMEM)
    arrays = [x for group in groups for x in group]
    return pl.pallas_call(
        lambda *refs: grads_kernel(len(groups), *refs),
        out_shape=[
            jax.ShapeDtypeStruct((features, 2 * units), BF),
            jax.ShapeDtypeStruct((units, features), BF),
        ],
        in_specs=[pl.BlockSpec(memory_space=pltpu.SMEM)] + [whole] * len(arrays),
        out_specs=[pl.BlockSpec(memory_space=pltpu.HBM)] * 2,
        scratch_shapes=[
            pltpu.VMEM((rows, features), BF),
            pltpu.VMEM((rows, features), BF),
            pltpu.VMEM((rows, units * 3 // 2), BF),
            pltpu.VMEM((rows, units * 3 // 2), BF),
            pltpu.VMEM((4, features // 4, 2 * units), BF),
            pltpu.VMEM((4, units // 4, features), BF),
            pltpu.SemaphoreType.DMA((8,)),
        ],
        compiler_params=pltpu.CompilerParams(vmem_limit_bytes=GRADS_LIMIT),
        cost_estimate=COST,
        name="grads",
    )(ids, *arrays)


def final_kernel(capacity, sources, cuts, ids, routes, weight, *refs):
    taken = cuts * len(sources)
    homes, partial, (mixed, grad_tokens) = refs[:taken], refs[taken:-2], refs[-2:]
    rows = routes.shape[1]
    me = ids[0]
    count = len(sources)
    eye = iota((rows, rows), 0) == iota((rows, rows), 1)

    def column(line, zero):
        return jnp.sum(jnp.where(eye, line, zero), axis=1, keepdims=True)

    lane = iota((rows, count), 1)
    expert = lane * 0
    for i, s in enumerate(sources):
        expert = jnp.where(lane == i, s, expert)
    expert = expert ^ me
    named, w_named = None, None
    for k in range(routes.shape[0]):
        hit = column(routes[k : k + 1, :], 0) == expert
        w_hit = jnp.where(hit, column(weight[k : k + 1, :], 0.0), 0.0)
        named = hit if named is None else named | hit
        w_named = w_hit if w_named is None else w_named + w_hit
    before = (iota((rows, rows), 1) < iota((rows, rows), 0)).astype(BF)
    rank = dot(before, named.astype(F32).astype(BF)).astype(jnp.int32)
    key = jnp.where(named, rank, -2 * capacity)
    slot = iota((rows, 2 * capacity), 1)
    width = mixed.shape[1] // cuts
    for j in range(cuts):
        at = slice(j * width, (j + 1) * width)
        total_out, total_grad = (p[:, at] for p in partial) if partial else (None, None)
        for i in range(count):
            home = homes[i * cuts + j]
            row_key = key[:, i : i + 1]
            pick_out = (row_key == slot).astype(F32).astype(BF)
            pick_grad = (row_key + capacity == slot).astype(F32).astype(BF)
            out = w_named[:, i : i + 1] * dot(pick_out, home[...])
            grad = dot(pick_grad, home[...])
            total_out = out if total_out is None else total_out + out
            total_grad = grad if total_grad is None else total_grad + grad
        mixed[:, at] = total_out.astype(mixed.dtype)
        grad_tokens[:, at] = total_grad.astype(mixed.dtype)


def final(ids, routes, weight, homes, sources, capacity, partial, dtype):
    cuts = len(homes[0])
    shape = (routes.shape[0], homes[0][0].shape[1] * cuts)
    return call(
        lambda *refs: final_kernel(capacity, sources, cuts, *refs),
        "final",
        [jax.ShapeDtypeStruct(shape, dtype)] * 2,
        [ids],
        routes.T,
        weight.T,
        *[x for home in homes for x in home],
        *partial,
    )


def per_device_chunked(tokens, routes, route_weight, cotangent, w_in, w_out):
    tok_rows = tokens.shape[0]
    top_count = routes.shape[1]
    n_expert = lax.axis_size("expert")
    n_dp = lax.axis_size("dp")
    capacity = tok_rows * top_count * 5 // (4 * n_expert)
    w_in, w_out = w_in[0], w_out[0]
    units = w_out.shape[0]
    ids = jnp.stack([lax.axis_index("expert"), lax.axis_index("dp") % 2]).astype(jnp.int32)

    def across(x, s):
        return lax.ppermute(x, "expert", [(i, i ^ s) for i in range(n_expert)]) if s else x

    def beside(x, s):
        return lax.ppermute(x, "dp", [(i, i ^ s) for i in range(n_dp)])

    def after(x, *earlier):
        return lax.optimization_barrier((x, *earlier))[0]

    def after(x, *earlier):
        return lax.optimization_barrier((x, *earlier))[0]

    inside = lax.axis_index("expert") >= 0

    def stage(body, *args):
        shapes = jax.eval_shape(body, *args)
        return lax.cond(inside, body, lambda *_: jax.tree.map(lambda x: jnp.zeros(x.shape, x.dtype), shapes), *args)

    def up_part(blocks, *earlier):
        first, *others = blocks
        rows, grads, send, keep = up_step(ids, [after(first, *earlier), *others], weights, capacity, True)
        return rows, grads, keep, beside(send, 1)

    def x_part(state, *earlier):
        rows, grads, keep, core = state
        total = sum_step(after(keep, *earlier), core)
        return (rows, grads, keep, core, beside(total, 2)), total

    def act_part(state, *earlier):
        rows, grads, keep, core, other = state
        own = act_step(after(keep, *earlier), core, other)
        return rows, grads, own, beside(own, 1)

    def down_part(group, count):
        return down_step(ids, *group[2:], weights, count, capacity, 1)

    def with_next(state, count, next_blocks):
        state, total = x_part(state)
        next_state = up_part(next_blocks, total)
        group = act_part(state)
        next_state, _ = x_part(next_state, group[2])
        return group, down_part(group, count), next_state

    def own_stage(begun, next_blocks):
        rows, grads, send, keep = begun
        return with_next((rows, grads, keep, beside(send, 1)), size, next_blocks)

    def far_stage(blocks, before):
        state, total = x_part(up_part(blocks))
        before = act_part(before, total)
        back = down_part(before, size)
        group = act_part(state, *[x for parts in back for x in parts])
        return group, down_part(group, len(blocks)), before, back

    def last_stage(blocks, next_blocks):
        return with_next(up_part(blocks), len(blocks), next_blocks)

    def rest_stage(state):
        group = act_part(state)
        return group, down_part(group, half - 2 * size)

    half, quarter = n_expert // 2, n_expert // 4
    size = half // 4
    near, rest = [list(range(size)), list(range(size, 2 * size))], list(range(2 * size, half))
    far, last = list(range(half, half + quarter)), list(range(half + quarter, n_expert))
    sent = prep(ids, tokens, routes, route_weight, cotangent, n_expert, capacity)
    came, home = {0: sent[0]}, {}

    def blocks(sources, *earlier):
        first, *others = [came[s] for s in sources]
        return [after(first, *earlier), *others]

    def start(sources, *earlier):
        came.update({s: across(after(sent[s], *earlier) if earlier else sent[s], s) for s in sources if s})

    def start_back(sources, back, *earlier):
        for s, parts in zip(sources, back):
            home[s] = [across(after(x, *earlier) if earlier else x, s) for x in parts]

    def arrived(sources):
        return [x for s in sources for x in home[s]]

    rest_first, rest_second = rest[:size], rest[size:]
    start(far + near[0] + near[1] + rest_first)
    begun = up_step(ids, blocks(near[0]), [w_in, w_out], capacity, False)
    begun, weights = begun[:4], begun[4:]
    group_0, back_0, state_1 = stage(own_stage, begun, blocks(near[1]))
    start_back(near[0], back_0)
    start(last + rest_second, *blocks(far + rest_first), group_0[3])
    group_far, back_far, group_1, back_1 = stage(far_stage, blocks(far, group_0[3]), state_1)
    start_back(far + near[1], back_far + back_1, *blocks(last))
    group_last, back_last, state_rest = stage(last_stage, blocks(last, group_far[3]), blocks(rest))
    start_back(last, back_last, *arrived(far + near[1]))
    group_rest, back_rest = stage(rest_stage, state_rest)
    start_back(rest, back_rest)

    def add(sources, partial, dtype):
        return final(ids, routes, route_weight, [home[s] for s in sources], sources, capacity, partial, dtype)

    groups = [group_0, group_far, group_1, group_last, group_rest]
    grad_in, grad_out = grads_step(ids, groups, units)
    partial = add(near[0] + near[1] + far, [], F32)
    partial = add(last, partial, F32)
    mixed, grad_tokens = add(rest, partial, BF)
    return mixed, grad_tokens, grad_in[None], grad_out[None]


def activate(pre_act, grad_hidden):
    units = pre_act.shape[1] // 2
    gate_part = pre_act[:, :units]
    up_part = pre_act[:, units:]
    sigmoid_gate = jax.nn.sigmoid(gate_part)
    silu_gate = gate_part * sigmoid_gate
    hidden = (silu_gate * up_part).astype(jnp.bfloat16)
    grad_gate = grad_hidden * up_part * sigmoid_gate * (1.0 + gate_part * (1.0 - sigmoid_gate))
    grad_up = grad_hidden * silu_gate
    return (hidden, jnp.concatenate([grad_gate, grad_up], axis=1).astype(jnp.bfloat16))


def per_device(tokens, routes, route_weight, cotangent, w_in, w_out):
    tok_rows, features = tokens.shape
    top_count = routes.shape[1]
    n_expert = lax.axis_size("expert")
    local_experts = w_in.shape[0]
    hidden_units = w_out.shape[1]
    experts = n_expert * local_experts
    capacity = tok_rows * top_count * 5 // (4 * experts)
    slot_count = experts * capacity
    flat_routes = routes.reshape(-1)
    onehot = (flat_routes[:, None] == jnp.arange(experts, dtype=jnp.int32)[None, :]).astype(
        jnp.int32
    )
    slot_rank = jnp.sum((jnp.cumsum(onehot, axis=0) - onehot) * onehot, axis=1)
    target = flat_routes * capacity + slot_rank
    placing = (target[None, :] == jnp.arange(slot_count, dtype=jnp.int32)[:, None]).astype(
        jnp.bfloat16
    )
    choose_token = jnp.sum(placing.reshape(slot_count, tok_rows, top_count), axis=2)
    scaled_grads = (route_weight[:, :, None] * cotangent[:, None, :].astype(jnp.float32)).astype(
        jnp.bfloat16
    )
    scaled_grads = scaled_grads.reshape(tok_rows * top_count, features)
    send_rows = jnp.dot(choose_token, tokens, preferred_element_type=jnp.float32).astype(
        jnp.bfloat16
    )
    send_grads = jnp.dot(placing, scaled_grads, preferred_element_type=jnp.float32).astype(
        jnp.bfloat16
    )
    send_rows = send_rows.reshape(n_expert, local_experts * capacity, features)
    send_grads = send_grads.reshape(n_expert, local_experts * capacity, features)
    routed_rows, routed_grads = (
        lax.all_to_all(send_rows, "expert", split_axis=0, concat_axis=0, tiled=True),
        lax.all_to_all(send_grads, "expert", split_axis=0, concat_axis=0, tiled=True),
    )
    rows_four = routed_rows.reshape(n_expert, local_experts, capacity, features)
    grads_four = routed_grads.reshape(n_expert, local_experts, capacity, features)
    total_rows = n_expert * local_experts * capacity
    pre_part = jnp.einsum("secd,edf->secf", rows_four, w_in, preferred_element_type=jnp.float32)
    back_part = jnp.einsum("secd,efd->secf", grads_four, w_out, preferred_element_type=jnp.float32)
    pre_flat = pre_part.reshape(total_rows, 2 * hidden_units)
    back_flat = back_part.reshape(total_rows, hidden_units)
    pre_share, back_share = (
        lax.psum_scatter(pre_flat, "dp", scatter_dimension=0, tiled=True),
        lax.psum_scatter(back_flat, "dp", scatter_dimension=0, tiled=True),
    )
    hidden_share, both_share = activate(pre_share, back_share)
    hidden, grad_both = (
        lax.all_gather(hidden_share, "dp", axis=0, tiled=True),
        lax.all_gather(both_share, "dp", axis=0, tiled=True),
    )
    hidden_four = hidden.reshape(n_expert, local_experts, capacity, hidden_units)
    both_four = grad_both.reshape(n_expert, local_experts, capacity, 2 * hidden_units)
    out_rows = jnp.einsum(
        "secf,efd->secd", hidden_four, w_out, preferred_element_type=jnp.float32
    ).astype(jnp.bfloat16)
    grad_rows = jnp.einsum(
        "secf,edf->secd", both_four, w_in, preferred_element_type=jnp.float32
    ).astype(jnp.bfloat16)
    grad_out = jnp.einsum(
        "secf,secd->efd", hidden_four, grads_four, preferred_element_type=jnp.float32
    ).astype(jnp.bfloat16)
    grad_in = jnp.einsum(
        "secd,secf->edf", rows_four, both_four, preferred_element_type=jnp.float32
    ).astype(jnp.bfloat16)
    home_out, home_grad = (
        lax.all_to_all(
            out_rows.reshape(n_expert, local_experts * capacity, features),
            "expert",
            split_axis=0,
            concat_axis=0,
            tiled=True,
        ),
        lax.all_to_all(
            grad_rows.reshape(n_expert, local_experts * capacity, features),
            "expert",
            split_axis=0,
            concat_axis=0,
            tiled=True,
        ),
    )
    route_out = jnp.dot(
        placing.T, home_out.reshape(slot_count, features), preferred_element_type=jnp.float32
    )
    route_out = route_out.reshape(tok_rows, top_count, features)
    mixed = jnp.sum(route_weight[:, :, None] * route_out, axis=1).astype(jnp.bfloat16)
    grad_tokens = jnp.dot(
        choose_token.T, home_grad.reshape(slot_count, features), preferred_element_type=jnp.float32
    )
    return (mixed, grad_tokens.astype(jnp.bfloat16), grad_in, grad_out)


def solution(mesh):
    placed = (
        P("expert", "dp"),
        P("expert", None),
        P("expert", None),
        P("expert", "dp"),
        P("expert", "dp", None),
        P("expert", None, "dp"),
    )
    sizes = dict(mesh.shape)
    chunked = sizes["dp"] == 4 and sizes["expert"] in (8, 16)
    return jax.shard_map(
        per_device_chunked if chunked else per_device,
        mesh=mesh,
        in_specs=placed,
        out_specs=(
            P("expert", "dp"),
            P("expert", "dp"),
            P("expert", "dp", None),
            P("expert", None, "dp"),
        ),
        check_vma=False,
    )
```

```python
import jax
import jax.numpy as jnp
from jax import lax
from jax.experimental import pallas as pl
from jax.experimental.pallas import tpu as pltpu
from jax.sharding import PartitionSpec as P

BF = jnp.bfloat16
F32 = jnp.float32
VMEM_LIMIT = 18 * 1024 * 1024
GRADS_LIMIT = 32 * 1024 * 1024
PREP_LIMIT = 60 * 1024 * 1024
COST = pl.CostEstimate(flops=1, bytes_accessed=1, transcendentals=0)


def dot(a, b):
    return lax.dot_general(a, b, (((1,), (0,)), ((), ())), preferred_element_type=F32)


def dot_t(a, b):
    return lax.dot_general(a, b, (((1,), (1,)), ((), ())), preferred_element_type=F32)


def t_dot(a, b):
    return lax.dot_general(a, b, (((0,), (0,)), ((), ())), preferred_element_type=F32)


def iota(shape, dim):
    return lax.broadcasted_iota(jnp.int32, shape, dim)


def padded(capacity):
    return -(-capacity // 16) * 16


def prep_kernel(capacity, ids, tokens, routes, weight, cotangent, *refs):
    outs, (token_rows, grad_rows, route_lines, weight_lines, sems) = refs[:-5], refs[-5:]
    pairs = ((routes, route_lines), (weight, weight_lines), (tokens, token_rows), (cotangent, grad_rows))
    copies = [pltpu.make_async_copy(x, held, sems.at[i]) for i, (x, held) in enumerate(pairs)]
    for copy in copies:
        copy.start()
    for copy in copies[:2]:
        copy.wait()
    routes, weight = route_lines, weight_lines
    count = len(outs)
    rows = routes.shape[1]
    expert = iota((count, rows), 0) ^ ids[0]
    named, w_named = None, None
    for k in range(routes.shape[0]):
        hit = routes[k : k + 1, :] == expert
        w_hit = jnp.where(hit, weight[k : k + 1, :], 0.0)
        named = hit if named is None else named | hit
        w_named = w_hit if w_named is None else w_named + w_hit
    before = (iota((rows, rows), 0) < iota((rows, rows), 1)).astype(F32).astype(BF)
    rank = dot(named.astype(F32).astype(BF), before).astype(jnp.int32)
    key = jnp.where(named, rank, -2 * capacity)
    slot = iota((2 * capacity, rows), 0)
    picks = []
    for s in range(count):
        row_key = key[s : s + 1, :]
        pick_token = (row_key == slot).astype(F32)
        pick_grad = (row_key + capacity == slot).astype(F32)
        scale = jnp.sum(pick_grad * w_named[s : s + 1, :], axis=1, keepdims=True)
        scale = scale + (slot[:, 0:1] < capacity).astype(F32)
        picks.append((pick_token.astype(BF), pick_grad.astype(BF), scale))
    for copy in copies[2:]:
        copy.wait()
    for out, (pick_token, pick_grad, scale) in zip(outs, picks):
        out[...] = (scale * (dot(pick_token, token_rows[...]) + dot(pick_grad, grad_rows[...]))).astype(BF)


def prep(ids, tokens, routes, weight, cotangent, count, capacity):
    rows, features = tokens.shape
    whole = pl.BlockSpec(memory_space=pltpu.VMEM)
    away = pl.BlockSpec(memory_space=pltpu.HBM)
    return pl.pallas_call(
        lambda *refs: prep_kernel(capacity, *refs),
        out_shape=[jax.ShapeDtypeStruct((2 * capacity, features), BF)] * count,
        in_specs=[pl.BlockSpec(memory_space=pltpu.SMEM)] + [away] * 4,
        out_specs=[whole] * count,
        scratch_shapes=[pltpu.VMEM((rows, features), BF)] * 2
        + [pltpu.VMEM(routes.T.shape, routes.dtype), pltpu.VMEM(weight.T.shape, weight.dtype)]
        + [pltpu.SemaphoreType.DMA((4,))],
        compiler_params=pltpu.CompilerParams(vmem_limit_bytes=PREP_LIMIT),
        cost_estimate=COST,
        name="prep",
    )(ids, tokens, routes.T, weight.T, cotangent)


def call(kernel, name, out_shapes, scalars, *arrays):
    whole = pl.BlockSpec(memory_space=pltpu.VMEM)
    return pl.pallas_call(
        kernel,
        out_shape=out_shapes,
        in_specs=[pl.BlockSpec(memory_space=pltpu.SMEM)] * len(scalars) + [whole] * len(arrays),
        out_specs=jax.tree.map(lambda _: whole, out_shapes),
        compiler_params=pltpu.CompilerParams(vmem_limit_bytes=VMEM_LIMIT),
        cost_estimate=COST,
        name=name,
    )(*scalars, *arrays)


def lay_out(capacity, blocks, row_out, grad_out):
    pad = padded(capacity)
    spot = iota((2 * pad, 2 * capacity), 0)
    col = iota((2 * pad, 2 * capacity), 1)
    target = jnp.where(col < capacity, col, col + pad - capacity)
    spread = (spot == target).astype(F32).astype(BF)
    for i, block in enumerate(blocks):
        laid = dot(spread, block[...]).astype(BF)
        row_out[i * pad : (i + 1) * pad, :] = laid[:pad]
        grad_out[i * pad : (i + 1) * pad, :] = laid[pad:]


def half_products(half, rows, grads, w_in, w_out, out):
    units = w_out.shape[0]
    width = units // 4
    for j in range(2):
        at = pl.multiple_of((half * 2 + j) * width, width)
        at_up = pl.multiple_of(units + (half * 2 + j) * width, width)
        gate = dot(rows[...], w_in[:, pl.ds(at, width)])
        up = dot(rows[...], w_in[:, pl.ds(at_up, width)])
        back = dot_t(grads[...], w_out[pl.ds(at, width), :])
        for part, term in enumerate((gate, up, back)):
            out[:, (3 * j + part) * width : (3 * j + part + 1) * width] = term.astype(out.dtype)


PIECES = 4


def weight_copies(ids, far_in, far_out, w_in, w_out, sems):
    units = far_out.shape[0]
    span, depth = units // 2, far_in.shape[0] // PIECES
    copies = []
    for half in (1 - ids[1], ids[1]):
        at = pl.ds(pl.multiple_of(half * span, span), span)
        at_up = pl.ds(pl.multiple_of(units + half * span, span), span)
        for k in range(PIECES):
            rows = slice(k * depth, (k + 1) * depth)
            step = span // PIECES
            row = pl.ds(pl.multiple_of(half * span + k * step, step), step)
            for x, y in (
                (far_in.at[rows, at], w_in.at[rows, at]),
                (far_in.at[rows, at_up], w_in.at[rows, at_up]),
                (far_out.at[row, :], w_out.at[row, :]),
            ):
                copies.append(pltpu.make_async_copy(x, y, sems.at[len(copies)]))
    for copy in copies:
        copy.start()
    return copies


def other_half(ids, blocks, w_in, w_out, capacity):
    units, features = w_out.shape
    rows = len(blocks) * padded(capacity)
    shape = jax.ShapeDtypeStruct
    whole = pl.BlockSpec(memory_space=pltpu.VMEM)
    away = pl.BlockSpec(memory_space=pl.ANY)

    def kernel(ids, *refs):
        held, (far_in, far_out, row_out, grad_out, send, near_in, near_out, sems) = refs[:-8], refs[-8:]
        copies = weight_copies(ids, far_in, far_out, near_in, near_out, sems)
        lay_out(capacity, held, row_out, grad_out)
        for copy in copies[: 3 * PIECES]:
            copy.wait()
        half_products(1 - ids[1], row_out, grad_out, near_in, near_out, send)
        for copy in copies[3 * PIECES :]:
            copy.wait()

    return pl.pallas_call(
        kernel,
        out_shape=[
            shape((rows, features), BF),
            shape((rows, features), BF),
            shape((rows, 3 * units // 2), BF),
            shape(w_in.shape, BF),
            shape(w_out.shape, BF),
        ],
        in_specs=[pl.BlockSpec(memory_space=pltpu.SMEM)] + [whole] * len(blocks) + [away] * 2,
        out_specs=[whole] * 5,
        scratch_shapes=[pltpu.SemaphoreType.DMA((6 * PIECES,))],
        compiler_params=pltpu.CompilerParams(vmem_limit_bytes=VMEM_LIMIT),
        cost_estimate=COST,
        name="up",
    )(ids, *blocks, w_in, w_out)


def own_half(ids, rows, grads, weights):
    def kernel(ids, rows, grads, w_in, w_out, keep):
        half_products(ids[1], rows, grads, w_in, w_out, keep)

    shape = jax.ShapeDtypeStruct((rows.shape[0], 3 * weights[1].shape[0] // 2), F32)
    return call(kernel, "up", shape, [ids], rows, grads, *weights)


def up_step(ids, blocks, weights, capacity):
    units, features = weights[1].shape
    rows = len(blocks) * padded(capacity)
    shape = jax.ShapeDtypeStruct

    def kernel(ids, *refs):
        held, (w_in, w_out, row_out, grad_out, send, keep) = refs[:-6], refs[-6:]
        lay_out(capacity, held, row_out, grad_out)
        half_products(1 - ids[1], row_out, grad_out, w_in, w_out, send)
        half_products(ids[1], row_out, grad_out, w_in, w_out, keep)

    return call(
        kernel,
        "up",
        [
            shape((rows, features), BF),
            shape((rows, features), BF),
            shape((rows, 3 * units // 2), BF),
            shape((rows, 3 * units // 2), F32),
        ],
        [ids],
        *blocks,
        *weights,
    )


def sum_kernel(keep, core, *outs):
    cut = keep.shape[1] // len(outs)
    for j, out in enumerate(outs):
        at = slice(j * cut, (j + 1) * cut)
        out[...] = (keep[:, at] + core[:, at].astype(F32)).astype(BF)


def sum_step(keep, core, cuts=1):
    shape = jax.ShapeDtypeStruct((keep.shape[0], keep.shape[1] // cuts), BF)
    return call(sum_kernel, "total", [shape] * cuts, [], keep, core)


def activated(keep, core, others, out):
    width = keep.shape[1] // 6
    for j in range(2):
        base = 3 * width * j
        other, skip = others[j % len(others)], base * (len(others) - 1)
        gate, up, back = (
            keep[:, at : at + width]
            + core[:, at : at + width].astype(F32)
            + other[:, at - skip : at - skip + width].astype(F32)
            for at in (base, base + width, base + 2 * width)
        )
        sigmoid = jax.nn.sigmoid(gate)
        silu = gate * sigmoid
        out[:, base : base + width] = (silu * up).astype(BF)
        out[:, base + width : base + 2 * width] = (
            back * up * sigmoid * (1.0 + gate * (1.0 - sigmoid))
        ).astype(BF)
        out[:, base + 2 * width : base + 3 * width] = (back * silu).astype(BF)


def act_step(keep, core, others):
    def kernel(keep, core, *refs):
        activated(keep, core, refs[:-1], refs[-1])

    return call(kernel, "act", jax.ShapeDtypeStruct(keep.shape, BF), [], keep, core, *others)


def act_and_sum(keep, core, other, next_keep, next_core):
    def kernel(keep, core, other, next_keep, next_core, out, total):
        activated(keep, core, [other], out)
        sum_kernel(next_keep, next_core, total)

    shapes = [jax.ShapeDtypeStruct(x.shape, BF) for x in (keep, next_keep)]
    return call(kernel, "act", shapes, [], keep, core, other, next_keep, next_core)


def act_and_load(ids, keep, core, other, w_in, w_out):
    shape = jax.ShapeDtypeStruct
    whole = pl.BlockSpec(memory_space=pltpu.VMEM)
    away = pl.BlockSpec(memory_space=pl.ANY)

    def kernel(ids, keep, core, other, far_in, far_out, out, near_in, near_out, sems):
        copies = weight_copies(ids, far_in, far_out, near_in, near_out, sems)
        activated(keep, core, [other], out)
        for copy in copies:
            copy.wait()

    return pl.pallas_call(
        kernel,
        out_shape=[shape(keep.shape, BF), shape(w_in.shape, BF), shape(w_out.shape, BF)],
        in_specs=[pl.BlockSpec(memory_space=pltpu.SMEM)] + [whole] * 3 + [away] * 2,
        out_specs=[whole] * 3,
        scratch_shapes=[pltpu.SemaphoreType.DMA((6 * PIECES,))],
        compiler_params=pltpu.CompilerParams(vmem_limit_bytes=VMEM_LIMIT),
        cost_estimate=COST,
        name="act",
    )(ids, keep, core, other, w_in, w_out)


def half_rows(half, held, w_in, w_out):
    units = w_out.shape[0]
    width = units // 4
    out_rows = grad_rows = None
    for j in range(2):
        base = 3 * width * j
        at = pl.multiple_of((half * 2 + j) * width, width)
        at_up = pl.multiple_of(units + (half * 2 + j) * width, width)
        a = dot(held[:, base : base + width], w_out[pl.ds(at, width), :])
        b = dot_t(held[:, base + width : base + 2 * width], w_in[:, pl.ds(at, width)])
        c = dot_t(held[:, base + 2 * width : base + 3 * width], w_in[:, pl.ds(at_up, width)])
        out_rows = a if out_rows is None else out_rows + a
        grad_rows = b + c if grad_rows is None else grad_rows + (b + c)
    return out_rows, grad_rows


def pack(capacity, out_rows, grad_rows, outs):
    pad = padded(capacity)
    spot = iota((2 * capacity, pad), 0)
    col = iota((2 * capacity, pad), 1)
    pack_out = (spot == jnp.where(col < capacity, col, -1)).astype(F32).astype(BF)
    pack_grad = (spot - capacity == jnp.where(col < capacity, col, -capacity - 1)).astype(F32).astype(BF)
    out_rows, grad_rows = out_rows.astype(BF), grad_rows.astype(BF)
    sources = out_rows.shape[0] // pad
    cuts = len(outs) // sources
    for i in range(sources):
        at = slice(i * pad, (i + 1) * pad)
        packed = (dot(pack_out, out_rows[at]) + dot(pack_grad, grad_rows[at])).astype(BF)
        cut = packed.shape[1] // cuts
        for j in range(cuts):
            outs[i * cuts + j][...] = packed[:, j * cut : (j + 1) * cut]


def down_step(ids, own, core, weights, count, capacity, cuts):
    def kernel(ids, own, core, w_in, w_out, *outs):
        out_rows, grad_rows = half_rows(ids[1], own, w_in, w_out)
        more_out, more_grad = half_rows(1 - ids[1], core, w_in, w_out)
        pack(capacity, out_rows + more_out, grad_rows + more_grad, outs)

    shape = jax.ShapeDtypeStruct((2 * capacity, weights[1].shape[1] // cuts), BF)
    outs = call(kernel, "down", [shape] * (count * cuts), [ids], own, core, *weights)
    return [outs[i * cuts : (i + 1) * cuts] for i in range(count)]


def down_own(ids, own, weights):
    def kernel(ids, own, w_in, w_out, out_rows, grad_rows):
        out_rows[...], grad_rows[...] = half_rows(ids[1], own, w_in, w_out)

    shape = jax.ShapeDtypeStruct((own.shape[0], weights[1].shape[1]), F32)
    return call(kernel, "down", [shape] * 2, [ids], own, *weights)


def down_other(ids, out_rows, grad_rows, core, weights, count, capacity):
    def kernel(ids, out_rows, grad_rows, core, w_in, w_out, *outs):
        more_out, more_grad = half_rows(1 - ids[1], core, w_in, w_out)
        pack(capacity, out_rows[...] + more_out, grad_rows[...] + more_grad, outs)

    shape = jax.ShapeDtypeStruct((2 * capacity, weights[1].shape[1]), BF)
    return call(kernel, "down", [shape] * count, [ids], out_rows, grad_rows, core, *weights)


def grads_kernel(count, ids, *refs):
    groups = [refs[4 * i : 4 * i + 4] for i in range(count)]
    grad_in, grad_out, rows, grads, own, core, tiles_in, tiles_out, sems = refs[4 * count :]
    at = 0
    for group in groups:
        n = group[0].shape[0]
        for held, part in zip((rows, grads, own, core), group):
            held[at : at + n, :] = part[...]
        at += n
    features, units = rows.shape[1], grad_out.shape[0]
    f_tile, width = features // 4, units // 4
    copies = []
    for j in range(4):
        turned = rows[:, j * f_tile : (j + 1) * f_tile].T
        for held, half in ((own, ids[1]), (core, 1 - ids[1])):
            for i in range(2):
                both = dot(turned, held[:, (3 * i + 1) * width : (3 * i + 3) * width]).astype(BF)
                for part in range(2):
                    to = pl.multiple_of(part * units + (half * 2 + i) * width, width)
                    tiles_in[j, :, pl.ds(to, width)] = both[:, part * width : (part + 1) * width]
        copies.append(pltpu.make_async_copy(tiles_in.at[j], grad_in.at[j * f_tile : (j + 1) * f_tile, :], sems.at[j]))
        copies[-1].start()
    for j, (held, half) in enumerate(((own, ids[1]), (core, 1 - ids[1]))):
        for i in range(2):
            turned = held[:, 3 * i * width : (3 * i + 1) * width].T
            tiles_out[2 * j + i] = dot(turned, grads[...]).astype(BF)
            to = pl.multiple_of((half * 2 + i) * width, width)
            copies.append(pltpu.make_async_copy(tiles_out.at[2 * j + i], grad_out.at[pl.ds(to, width), :], sems.at[4 + 2 * j + i]))
            copies[-1].start()
    for copy in copies:
        copy.wait()


def grads_step(ids, groups, units):
    features = groups[0][0].shape[1]
    rows = sum(group[0].shape[0] for group in groups)
    whole = pl.BlockSpec(memory_space=pltpu.VMEM)
    arrays = [x for group in groups for x in group]
    return pl.pallas_call(
        lambda *refs: grads_kernel(len(groups), *refs),
        out_shape=[
            jax.ShapeDtypeStruct((features, 2 * units), BF),
            jax.ShapeDtypeStruct((units, features), BF),
        ],
        in_specs=[pl.BlockSpec(memory_space=pltpu.SMEM)] + [whole] * len(arrays),
        out_specs=[pl.BlockSpec(memory_space=pltpu.HBM)] * 2,
        scratch_shapes=[
            pltpu.VMEM((rows, features), BF),
            pltpu.VMEM((rows, features), BF),
            pltpu.VMEM((rows, units * 3 // 2), BF),
            pltpu.VMEM((rows, units * 3 // 2), BF),
            pltpu.VMEM((4, features // 4, 2 * units), BF),
            pltpu.VMEM((4, units // 4, features), BF),
            pltpu.SemaphoreType.DMA((8,)),
        ],
        compiler_params=pltpu.CompilerParams(vmem_limit_bytes=GRADS_LIMIT),
        cost_estimate=COST,
        name="grads",
    )(ids, *arrays)


def final_kernel(capacity, sources, cuts, ids, routes, weight, *refs):
    taken = cuts * len(sources)
    homes, partial, (mixed, grad_tokens) = refs[:taken], refs[taken:-2], refs[-2:]
    rows = routes.shape[1]
    me = ids[0]
    count = len(sources)
    eye = iota((rows, rows), 0) == iota((rows, rows), 1)

    def column(line, zero):
        return jnp.sum(jnp.where(eye, line, zero), axis=1, keepdims=True)

    lane = iota((rows, count), 1)
    expert = lane * 0
    for i, s in enumerate(sources):
        expert = jnp.where(lane == i, s, expert)
    expert = expert ^ me
    named, w_named = None, None
    for k in range(routes.shape[0]):
        hit = column(routes[k : k + 1, :], 0) == expert
        w_hit = jnp.where(hit, column(weight[k : k + 1, :], 0.0), 0.0)
        named = hit if named is None else named | hit
        w_named = w_hit if w_named is None else w_named + w_hit
    before = (iota((rows, rows), 1) < iota((rows, rows), 0)).astype(BF)
    rank = dot(before, named.astype(F32).astype(BF)).astype(jnp.int32)
    key = jnp.where(named, rank, -2 * capacity)
    slot = iota((rows, 2 * capacity), 1)
    width = mixed.shape[1] // cuts
    for j in range(cuts):
        at = slice(j * width, (j + 1) * width)
        total_out, total_grad = (p[:, at] for p in partial) if partial else (None, None)
        for i in range(count):
            home = homes[i * cuts + j]
            row_key = key[:, i : i + 1]
            pick_out = (row_key == slot).astype(F32).astype(BF)
            pick_grad = (row_key + capacity == slot).astype(F32).astype(BF)
            out = w_named[:, i : i + 1] * dot(pick_out, home[...])
            grad = dot(pick_grad, home[...])
            total_out = out if total_out is None else total_out + out
            total_grad = grad if total_grad is None else total_grad + grad
        mixed[:, at] = total_out.astype(mixed.dtype)
        grad_tokens[:, at] = total_grad.astype(mixed.dtype)


def final(ids, routes, weight, homes, sources, capacity, partial, dtype):
    cuts = len(homes[0])
    shape = (routes.shape[0], homes[0][0].shape[1] * cuts)
    return call(
        lambda *refs: final_kernel(capacity, sources, cuts, *refs),
        "final",
        [jax.ShapeDtypeStruct(shape, dtype)] * 2,
        [ids],
        routes.T,
        weight.T,
        *[x for home in homes for x in home],
        *partial,
    )


def per_device_chunked(tokens, routes, route_weight, cotangent, w_in, w_out):
    tok_rows = tokens.shape[0]
    top_count = routes.shape[1]
    n_expert = lax.axis_size("expert")
    n_dp = lax.axis_size("dp")
    capacity = tok_rows * top_count * 5 // (4 * n_expert)
    w_in, w_out = w_in[0], w_out[0]
    units = w_out.shape[0]
    ids = jnp.stack([lax.axis_index("expert"), lax.axis_index("dp") % 2]).astype(jnp.int32)

    def across(x, s):
        return lax.ppermute(x, "expert", [(i, i ^ s) for i in range(n_expert)]) if s else x

    def beside(x, s):
        return lax.ppermute(x, "dp", [(i, i ^ s) for i in range(n_dp)])

    def after(x, *earlier):
        return lax.optimization_barrier((x, *earlier))[0]

    def after(x, *earlier):
        return lax.optimization_barrier((x, *earlier))[0]

    inside = lax.axis_index("expert") >= 0

    def stage(body, *args):
        shapes = jax.eval_shape(body, *args)
        return lax.cond(inside, body, lambda *_: jax.tree.map(lambda x: jnp.zeros(x.shape, x.dtype), shapes), *args)

    def up_part(blocks, weights, *earlier):
        first, *others = blocks
        return up_step(ids, [after(first, *earlier), *others], weights, capacity)

    def core_part(state, *earlier):
        rows, grads, send, keep = state
        return rows, grads, keep, beside(after(send, *earlier) if earlier else send, 1)

    def up_in_halves(blocks):
        rows, grads, send, *weights = other_half(ids, blocks, w_in, w_out, capacity)
        core = beside(send, 1)
        return (rows, grads, own_half(ids, after(rows, send), grads, weights), core), weights

    def sum_part(state, *earlier, cuts=1):
        rows, grads, keep, core = state
        return rows, grads, keep, core, sum_step(after(keep, *earlier), core, cuts)

    def x_part(state):
        rows, grads, keep, core, totals = state
        return rows, grads, keep, core, [beside(total, 2) for total in totals]

    def act_part(state, *earlier):
        rows, grads, keep, core, others = state
        own = act_step(after(keep, *earlier), core, others)
        return rows, grads, own, beside(own, 1)

    def down_part(group, weights, count, cuts=1):
        return down_step(ids, *group[2:], weights, count, capacity, cuts)

    def down_in_halves(group, weights, count):
        _, _, own, core = group
        sums = down_own(ids, own, weights)
        return [[x] for x in down_other(ids, *sums, after(core, *sums), weights, count, capacity)]

    def act_both(state, next_state, *earlier):
        rows, grads, keep, core, (other,) = state
        own, next_total = act_and_sum(after(keep, *earlier), core, other, *next_state[2:])
        return (rows, grads, own, beside(own, 1)), (*next_state, [next_total])

    def first_stage(blocks):
        state, _ = up_in_halves(blocks)
        return sum_part(state, cuts=2)

    def far_stage(blocks, before, before_count, next_blocks):
        state, held = up_in_halves(blocks)
        state = sum_part(state)
        before = act_part(before, *state[4])
        next_state = up_part(next_blocks, held, before[2])
        back = down_part((*before[:2], after(before[2], next_state[2]), before[3]), held, before_count)
        ends = [x for parts in back for x in parts]
        group, next_state = act_both(x_part(state), core_part(next_state, *ends), *ends)
        return group, down_in_halves(group, held, len(blocks)), next_state, before, back

    def rest_stage(state):
        rows, grads, keep, core, (other,) = state
        own, *weights = act_and_load(ids, keep, core, other, w_in, w_out)
        group = rows, grads, own, beside(own, 1)
        return group, down_part(group, weights, size, 2)

    half, quarter = n_expert // 2, n_expert // 4
    size = quarter // 2
    near = [list(range(quarter)), list(range(quarter, quarter + size)), list(range(quarter + size, half))]
    far, last = list(range(half, half + quarter)), list(range(half + quarter, n_expert))
    sent = prep(ids, tokens, routes, route_weight, cotangent, n_expert, capacity)
    came, home = {0: sent[0]}, {}

    def blocks(sources, *earlier):
        first, *others = [came[s] for s in sources]
        return [after(first, *earlier), *others]

    def start(sources, *earlier):
        came.update({s: across(after(sent[s], *earlier) if earlier else sent[s], s) for s in sources if s})

    def start_back(sources, back, *earlier):
        for s, parts in zip(sources, back):
            home[s] = [across(after(x, *earlier) if earlier else x, s) for x in parts]

    def arrived(sources):
        return [x for s in sources for x in home[s]]

    start(far + near[0] + near[1])
    state_0 = stage(first_stage, blocks(near[0]))
    start(last, *blocks(far + near[1]), *state_0[4])
    state_0 = x_part(state_0)
    start(near[2], *blocks(far), *state_0[4])
    group_far, back_far, state_1, group_0, back_0 = stage(
        lambda a, b, c: far_stage(a, b, quarter, c), blocks(far), state_0, blocks(near[1])
    )
    start_back(far + near[0], back_far + back_0, *blocks(last))
    group_last, back_last, state_2, group_1, back_1 = stage(
        lambda a, b, c: far_stage(a, b, size, c), blocks(last, group_far[3]), x_part(state_1), blocks(near[2])
    )
    start_back(last, back_last, *arrived(far + near[0]))
    start_back(near[1], back_1)
    group_2, back_2 = stage(rest_stage, x_part(state_2))
    start_back(near[2], back_2)

    def add(sources, partial, dtype):
        return final(ids, routes, route_weight, [home[s] for s in sources], sources, capacity, partial, dtype)

    groups = [group_0, group_far, group_1, group_last, group_2]
    grad_in, grad_out = grads_step(ids, groups, units)
    partial = add(near[0] + near[1] + far, [], F32)
    partial = add(near[2], partial, F32)
    mixed, grad_tokens = add(last, partial, BF)
    return mixed, grad_tokens, grad_in[None], grad_out[None]


def activate(pre_act, grad_hidden):
    units = pre_act.shape[1] // 2
    gate_part = pre_act[:, :units]
    up_part = pre_act[:, units:]
    sigmoid_gate = jax.nn.sigmoid(gate_part)
    silu_gate = gate_part * sigmoid_gate
    hidden = (silu_gate * up_part).astype(jnp.bfloat16)
    grad_gate = grad_hidden * up_part * sigmoid_gate * (1.0 + gate_part * (1.0 - sigmoid_gate))
    grad_up = grad_hidden * silu_gate
    return (hidden, jnp.concatenate([grad_gate, grad_up], axis=1).astype(jnp.bfloat16))


def per_device(tokens, routes, route_weight, cotangent, w_in, w_out):
    tok_rows, features = tokens.shape
    top_count = routes.shape[1]
    n_expert = lax.axis_size("expert")
    local_experts = w_in.shape[0]
    hidden_units = w_out.shape[1]
    experts = n_expert * local_experts
    capacity = tok_rows * top_count * 5 // (4 * experts)
    slot_count = experts * capacity
    flat_routes = routes.reshape(-1)
    onehot = (flat_routes[:, None] == jnp.arange(experts, dtype=jnp.int32)[None, :]).astype(
        jnp.int32
    )
    slot_rank = jnp.sum((jnp.cumsum(onehot, axis=0) - onehot) * onehot, axis=1)
    target = flat_routes * capacity + slot_rank
    placing = (target[None, :] == jnp.arange(slot_count, dtype=jnp.int32)[:, None]).astype(
        jnp.bfloat16
    )
    choose_token = jnp.sum(placing.reshape(slot_count, tok_rows, top_count), axis=2)
    scaled_grads = (route_weight[:, :, None] * cotangent[:, None, :].astype(jnp.float32)).astype(
        jnp.bfloat16
    )
    scaled_grads = scaled_grads.reshape(tok_rows * top_count, features)
    send_rows = jnp.dot(choose_token, tokens, preferred_element_type=jnp.float32).astype(
        jnp.bfloat16
    )
    send_grads = jnp.dot(placing, scaled_grads, preferred_element_type=jnp.float32).astype(
        jnp.bfloat16
    )
    send_rows = send_rows.reshape(n_expert, local_experts * capacity, features)
    send_grads = send_grads.reshape(n_expert, local_experts * capacity, features)
    routed_rows, routed_grads = (
        lax.all_to_all(send_rows, "expert", split_axis=0, concat_axis=0, tiled=True),
        lax.all_to_all(send_grads, "expert", split_axis=0, concat_axis=0, tiled=True),
    )
    rows_four = routed_rows.reshape(n_expert, local_experts, capacity, features)
    grads_four = routed_grads.reshape(n_expert, local_experts, capacity, features)
    total_rows = n_expert * local_experts * capacity
    pre_part = jnp.einsum("secd,edf->secf", rows_four, w_in, preferred_element_type=jnp.float32)
    back_part = jnp.einsum("secd,efd->secf", grads_four, w_out, preferred_element_type=jnp.float32)
    pre_flat = pre_part.reshape(total_rows, 2 * hidden_units)
    back_flat = back_part.reshape(total_rows, hidden_units)
    pre_share, back_share = (
        lax.psum_scatter(pre_flat, "dp", scatter_dimension=0, tiled=True),
        lax.psum_scatter(back_flat, "dp", scatter_dimension=0, tiled=True),
    )
    hidden_share, both_share = activate(pre_share, back_share)
    hidden, grad_both = (
        lax.all_gather(hidden_share, "dp", axis=0, tiled=True),
        lax.all_gather(both_share, "dp", axis=0, tiled=True),
    )
    hidden_four = hidden.reshape(n_expert, local_experts, capacity, hidden_units)
    both_four = grad_both.reshape(n_expert, local_experts, capacity, 2 * hidden_units)
    out_rows = jnp.einsum(
        "secf,efd->secd", hidden_four, w_out, preferred_element_type=jnp.float32
    ).astype(jnp.bfloat16)
    grad_rows = jnp.einsum(
        "secf,edf->secd", both_four, w_in, preferred_element_type=jnp.float32
    ).astype(jnp.bfloat16)
    grad_out = jnp.einsum(
        "secf,secd->efd", hidden_four, grads_four, preferred_element_type=jnp.float32
    ).astype(jnp.bfloat16)
    grad_in = jnp.einsum(
        "secd,secf->edf", rows_four, both_four, preferred_element_type=jnp.float32
    ).astype(jnp.bfloat16)
    home_out, home_grad = (
        lax.all_to_all(
            out_rows.reshape(n_expert, local_experts * capacity, features),
            "expert",
            split_axis=0,
            concat_axis=0,
            tiled=True,
        ),
        lax.all_to_all(
            grad_rows.reshape(n_expert, local_experts * capacity, features),
            "expert",
            split_axis=0,
            concat_axis=0,
            tiled=True,
        ),
    )
    route_out = jnp.dot(
        placing.T, home_out.reshape(slot_count, features), preferred_element_type=jnp.float32
    )
    route_out = route_out.reshape(tok_rows, top_count, features)
    mixed = jnp.sum(route_weight[:, :, None] * route_out, axis=1).astype(jnp.bfloat16)
    grad_tokens = jnp.dot(
        choose_token.T, home_grad.reshape(slot_count, features), preferred_element_type=jnp.float32
    )
    return (mixed, grad_tokens.astype(jnp.bfloat16), grad_in, grad_out)


def solution(mesh):
    placed = (
        P("expert", "dp"),
        P("expert", None),
        P("expert", None),
        P("expert", "dp"),
        P("expert", "dp", None),
        P("expert", None, "dp"),
    )
    sizes = dict(mesh.shape)
    chunked = sizes["dp"] == 4 and sizes["expert"] in (8, 16)
    return jax.shard_map(
        per_device_chunked if chunked else per_device,
        mesh=mesh,
        in_specs=placed,
        out_specs=(
            P("expert", "dp"),
            P("expert", "dp"),
            P("expert", "dp", None),
            P("expert", None, "dp"),
        ),
        check_vma=False,
    )
```

```python
import jax
import jax.numpy as jnp
from jax import lax
from jax.experimental import pallas as pl
from jax.experimental.pallas import tpu as pltpu
from jax.sharding import PartitionSpec as P

BF = jnp.bfloat16
F32 = jnp.float32
VMEM_LIMIT = 18 * 1024 * 1024
GRADS_LIMIT = 32 * 1024 * 1024
PREP_LIMIT = 60 * 1024 * 1024
COST = pl.CostEstimate(flops=1, bytes_accessed=1, transcendentals=0)


def dot(a, b):
    return lax.dot_general(a, b, (((1,), (0,)), ((), ())), preferred_element_type=F32)


def dot_t(a, b):
    return lax.dot_general(a, b, (((1,), (1,)), ((), ())), preferred_element_type=F32)


def t_dot(a, b):
    return lax.dot_general(a, b, (((0,), (0,)), ((), ())), preferred_element_type=F32)


def iota(shape, dim):
    return lax.broadcasted_iota(jnp.int32, shape, dim)


def padded(capacity):
    return -(-capacity // 16) * 16


def prep_kernel(capacity, ids, tokens, routes, weight, cotangent, *refs):
    outs, (token_rows, grad_rows, route_lines, weight_lines, sems) = refs[:-5], refs[-5:]
    pairs = ((routes, route_lines), (weight, weight_lines), (tokens, token_rows), (cotangent, grad_rows))
    copies = [pltpu.make_async_copy(x, held, sems.at[i]) for i, (x, held) in enumerate(pairs)]
    for copy in copies:
        copy.start()
    for copy in copies[:2]:
        copy.wait()
    routes, weight = route_lines, weight_lines
    count = len(outs)
    rows = routes.shape[1]
    expert = iota((count, rows), 0) ^ ids[0]
    named, w_named = None, None
    for k in range(routes.shape[0]):
        hit = routes[k : k + 1, :] == expert
        w_hit = jnp.where(hit, weight[k : k + 1, :], 0.0)
        named = hit if named is None else named | hit
        w_named = w_hit if w_named is None else w_named + w_hit
    before = (iota((rows, rows), 0) < iota((rows, rows), 1)).astype(F32).astype(BF)
    rank = dot(named.astype(F32).astype(BF), before).astype(jnp.int32)
    key = jnp.where(named, rank, -2 * capacity)
    slot = iota((2 * capacity, rows), 0)
    picks = []
    for s in range(count):
        row_key = key[s : s + 1, :]
        pick_token = (row_key == slot).astype(F32)
        pick_grad = (row_key + capacity == slot).astype(F32)
        scale = jnp.sum(pick_grad * w_named[s : s + 1, :], axis=1, keepdims=True)
        scale = scale + (slot[:, 0:1] < capacity).astype(F32)
        picks.append((pick_token.astype(BF), pick_grad.astype(BF), scale))
    for copy in copies[2:]:
        copy.wait()
    for out, (pick_token, pick_grad, scale) in zip(outs, picks):
        out[...] = (scale * (dot(pick_token, token_rows[...]) + dot(pick_grad, grad_rows[...]))).astype(BF)


def prep(ids, tokens, routes, weight, cotangent, count, capacity):
    rows, features = tokens.shape
    whole = pl.BlockSpec(memory_space=pltpu.VMEM)
    away = pl.BlockSpec(memory_space=pltpu.HBM)
    return pl.pallas_call(
        lambda *refs: prep_kernel(capacity, *refs),
        out_shape=[jax.ShapeDtypeStruct((2 * capacity, features), BF)] * count,
        in_specs=[pl.BlockSpec(memory_space=pltpu.SMEM)] + [away] * 4,
        out_specs=[whole] * count,
        scratch_shapes=[pltpu.VMEM((rows, features), BF)] * 2
        + [pltpu.VMEM(routes.T.shape, routes.dtype), pltpu.VMEM(weight.T.shape, weight.dtype)]
        + [pltpu.SemaphoreType.DMA((4,))],
        compiler_params=pltpu.CompilerParams(vmem_limit_bytes=PREP_LIMIT),
        cost_estimate=COST,
        name="prep",
    )(ids, tokens, routes.T, weight.T, cotangent)


def call(kernel, name, out_shapes, scalars, *arrays):
    whole = pl.BlockSpec(memory_space=pltpu.VMEM)
    return pl.pallas_call(
        kernel,
        out_shape=out_shapes,
        in_specs=[pl.BlockSpec(memory_space=pltpu.SMEM)] * len(scalars) + [whole] * len(arrays),
        out_specs=jax.tree.map(lambda _: whole, out_shapes),
        compiler_params=pltpu.CompilerParams(vmem_limit_bytes=VMEM_LIMIT),
        cost_estimate=COST,
        name=name,
    )(*scalars, *arrays)


def lay_out(capacity, blocks, row_out, grad_out):
    pad = padded(capacity)
    spot = iota((2 * pad, 2 * capacity), 0)
    col = iota((2 * pad, 2 * capacity), 1)
    target = jnp.where(col < capacity, col, col + pad - capacity)
    spread = (spot == target).astype(F32).astype(BF)
    for i, block in enumerate(blocks):
        laid = dot(spread, block[...]).astype(BF)
        row_out[i * pad : (i + 1) * pad, :] = laid[:pad]
        grad_out[i * pad : (i + 1) * pad, :] = laid[pad:]


def half_products(half, rows, grads, w_in, w_out, out):
    units = w_out.shape[0]
    width = units // 4
    for j in range(2):
        at = pl.multiple_of((half * 2 + j) * width, width)
        at_up = pl.multiple_of(units + (half * 2 + j) * width, width)
        gate = dot(rows[...], w_in[:, pl.ds(at, width)])
        up = dot(rows[...], w_in[:, pl.ds(at_up, width)])
        back = dot_t(grads[...], w_out[pl.ds(at, width), :])
        for part, term in enumerate((gate, up, back)):
            out[:, (3 * j + part) * width : (3 * j + part + 1) * width] = term.astype(out.dtype)


PIECES = 4


def weight_copies(halves, far_in, far_out, w_in, w_out, sems):
    units = far_out.shape[0]
    span, depth = units // 2, far_in.shape[0] // PIECES
    copies = []
    for half in halves:
        at = pl.ds(pl.multiple_of(half * span, span), span)
        at_up = pl.ds(pl.multiple_of(units + half * span, span), span)
        for k in range(PIECES):
            rows = slice(k * depth, (k + 1) * depth)
            step = span // PIECES
            row = pl.ds(pl.multiple_of(half * span + k * step, step), step)
            for x, y in (
                (far_in.at[rows, at], w_in.at[rows, at]),
                (far_in.at[rows, at_up], w_in.at[rows, at_up]),
                (far_out.at[row, :], w_out.at[row, :]),
            ):
                copies.append(pltpu.make_async_copy(x, y, sems.at[len(copies)]))
    for copy in copies:
        copy.start()
    return copies


def other_half(ids, blocks, w_in, w_out, capacity):
    units, features = w_out.shape
    rows = len(blocks) * padded(capacity)
    shape = jax.ShapeDtypeStruct
    whole = pl.BlockSpec(memory_space=pltpu.VMEM)
    away = pl.BlockSpec(memory_space=pl.ANY)

    def kernel(ids, *refs):
        held, (far_in, far_out, row_out, grad_out, send, near_in, near_out, sems) = refs[:-8], refs[-8:]
        copies = weight_copies((1 - ids[1], ids[1]), far_in, far_out, near_in, near_out, sems)
        lay_out(capacity, held, row_out, grad_out)
        for copy in copies[: 3 * PIECES]:
            copy.wait()
        half_products(1 - ids[1], row_out, grad_out, near_in, near_out, send)
        for copy in copies[3 * PIECES :]:
            copy.wait()

    return pl.pallas_call(
        kernel,
        out_shape=[
            shape((rows, features), BF),
            shape((rows, features), BF),
            shape((rows, 3 * units // 2), BF),
            shape(w_in.shape, BF),
            shape(w_out.shape, BF),
        ],
        in_specs=[pl.BlockSpec(memory_space=pltpu.SMEM)] + [whole] * len(blocks) + [away] * 2,
        out_specs=[whole] * 5,
        scratch_shapes=[pltpu.SemaphoreType.DMA((6 * PIECES,))],
        compiler_params=pltpu.CompilerParams(vmem_limit_bytes=VMEM_LIMIT),
        cost_estimate=COST,
        name="up",
    )(ids, *blocks, w_in, w_out)


def own_half(ids, rows, grads, weights):
    def kernel(ids, rows, grads, w_in, w_out, keep):
        half_products(ids[1], rows, grads, w_in, w_out, keep)

    shape = jax.ShapeDtypeStruct((rows.shape[0], 3 * weights[1].shape[0] // 2), F32)
    return call(kernel, "up", shape, [ids], rows, grads, *weights)


def up_step(ids, blocks, weights, capacity):
    units, features = weights[1].shape
    rows = len(blocks) * padded(capacity)
    shape = jax.ShapeDtypeStruct

    def kernel(ids, *refs):
        held, (w_in, w_out, row_out, grad_out, send, keep) = refs[:-6], refs[-6:]
        lay_out(capacity, held, row_out, grad_out)
        half_products(1 - ids[1], row_out, grad_out, w_in, w_out, send)
        half_products(ids[1], row_out, grad_out, w_in, w_out, keep)

    return call(
        kernel,
        "up",
        [
            shape((rows, features), BF),
            shape((rows, features), BF),
            shape((rows, 3 * units // 2), BF),
            shape((rows, 3 * units // 2), F32),
        ],
        [ids],
        *blocks,
        *weights,
    )


def sum_kernel(keep, core, *outs):
    cut = keep.shape[1] // len(outs)
    for j, out in enumerate(outs):
        at = slice(j * cut, (j + 1) * cut)
        out[...] = (keep[:, at] + core[:, at].astype(F32)).astype(BF)


def sum_step(keep, core, cuts=1):
    shape = jax.ShapeDtypeStruct((keep.shape[0], keep.shape[1] // cuts), BF)
    return call(sum_kernel, "total", [shape] * cuts, [], keep, core)


def activated(keep, core, others, out):
    width = keep.shape[1] // 6
    for j in range(2):
        base = 3 * width * j
        other, skip = others[j % len(others)], base * (len(others) - 1)
        gate, up, back = (
            keep[:, at : at + width]
            + core[:, at : at + width].astype(F32)
            + other[:, at - skip : at - skip + width].astype(F32)
            for at in (base, base + width, base + 2 * width)
        )
        sigmoid = jax.nn.sigmoid(gate)
        silu = gate * sigmoid
        out[:, base : base + width] = (silu * up).astype(BF)
        out[:, base + width : base + 2 * width] = (
            back * up * sigmoid * (1.0 + gate * (1.0 - sigmoid))
        ).astype(BF)
        out[:, base + 2 * width : base + 3 * width] = (back * silu).astype(BF)


def act_step(keep, core, others):
    def kernel(keep, core, *refs):
        activated(keep, core, refs[:-1], refs[-1])

    return call(kernel, "act", jax.ShapeDtypeStruct(keep.shape, BF), [], keep, core, *others)


def act_and_sum(keep, core, other, next_keep, next_core):
    def kernel(keep, core, other, next_keep, next_core, out, total):
        activated(keep, core, [other], out)
        sum_kernel(next_keep, next_core, total)

    shapes = [jax.ShapeDtypeStruct(x.shape, BF) for x in (keep, next_keep)]
    return call(kernel, "act", shapes, [], keep, core, other, next_keep, next_core)


def half_rows(half, held, w_in, w_out):
    units = w_out.shape[0]
    width = units // 4
    out_rows = grad_rows = None
    for j in range(2):
        base = 3 * width * j
        at = pl.multiple_of((half * 2 + j) * width, width)
        at_up = pl.multiple_of(units + (half * 2 + j) * width, width)
        a = dot(held[:, base : base + width], w_out[pl.ds(at, width), :])
        b = dot_t(held[:, base + width : base + 2 * width], w_in[:, pl.ds(at, width)])
        c = dot_t(held[:, base + 2 * width : base + 3 * width], w_in[:, pl.ds(at_up, width)])
        out_rows = a if out_rows is None else out_rows + a
        grad_rows = b + c if grad_rows is None else grad_rows + (b + c)
    return out_rows, grad_rows


def pack(capacity, out_rows, grad_rows, outs):
    pad = padded(capacity)
    spot = iota((2 * capacity, pad), 0)
    col = iota((2 * capacity, pad), 1)
    pack_out = (spot == jnp.where(col < capacity, col, -1)).astype(F32).astype(BF)
    pack_grad = (spot - capacity == jnp.where(col < capacity, col, -capacity - 1)).astype(F32).astype(BF)
    out_rows, grad_rows = out_rows.astype(BF), grad_rows.astype(BF)
    sources = out_rows.shape[0] // pad
    cuts = len(outs) // sources
    for i in range(sources):
        at = slice(i * pad, (i + 1) * pad)
        packed = (dot(pack_out, out_rows[at]) + dot(pack_grad, grad_rows[at])).astype(BF)
        cut = packed.shape[1] // cuts
        for j in range(cuts):
            outs[i * cuts + j][...] = packed[:, j * cut : (j + 1) * cut]


def down_step(ids, own, core, weights, count, capacity):
    def kernel(ids, own, core, w_in, w_out, *outs):
        out_rows, grad_rows = half_rows(ids[1], own, w_in, w_out)
        more_out, more_grad = half_rows(1 - ids[1], core, w_in, w_out)
        pack(capacity, out_rows + more_out, grad_rows + more_grad, outs)

    shape = jax.ShapeDtypeStruct((2 * capacity, weights[1].shape[1]), BF)
    return [[x] for x in call(kernel, "down", [shape] * count, [ids], own, core, *weights)]


def down_own(ids, own, weights):
    def kernel(ids, own, w_in, w_out, out_rows, grad_rows):
        out_rows[...], grad_rows[...] = half_rows(ids[1], own, w_in, w_out)

    shape = jax.ShapeDtypeStruct((own.shape[0], weights[1].shape[1]), F32)
    return call(kernel, "down", [shape] * 2, [ids], own, *weights)


def down_own_alone(ids, own, w_in, w_out):
    shape = jax.ShapeDtypeStruct
    whole = pl.BlockSpec(memory_space=pltpu.VMEM)
    away = pl.BlockSpec(memory_space=pl.ANY)

    def kernel(ids, own, far_in, far_out, out_rows, grad_rows, near_in, near_out, sems):
        copies = weight_copies((ids[1], 1 - ids[1]), far_in, far_out, near_in, near_out, sems)
        for copy in copies[: 3 * PIECES]:
            copy.wait()
        out_rows[...], grad_rows[...] = half_rows(ids[1], own, near_in, near_out)
        for copy in copies[3 * PIECES :]:
            copy.wait()

    sums = shape((own.shape[0], w_out.shape[1]), F32)
    return pl.pallas_call(
        kernel,
        out_shape=[sums, sums, shape(w_in.shape, BF), shape(w_out.shape, BF)],
        in_specs=[pl.BlockSpec(memory_space=pltpu.SMEM), whole] + [away] * 2,
        out_specs=[whole] * 4,
        scratch_shapes=[pltpu.SemaphoreType.DMA((6 * PIECES,))],
        compiler_params=pltpu.CompilerParams(vmem_limit_bytes=VMEM_LIMIT),
        cost_estimate=COST,
        name="down",
    )(ids, own, w_in, w_out)


def down_other(ids, out_rows, grad_rows, core, weights, count, capacity, cuts=1):
    def kernel(ids, out_rows, grad_rows, core, w_in, w_out, *outs):
        more_out, more_grad = half_rows(1 - ids[1], core, w_in, w_out)
        pack(capacity, out_rows[...] + more_out, grad_rows[...] + more_grad, outs)

    shape = jax.ShapeDtypeStruct((2 * capacity, weights[1].shape[1] // cuts), BF)
    outs = call(kernel, "down", [shape] * (count * cuts), [ids], out_rows, grad_rows, core, *weights)
    return [outs[i * cuts : (i + 1) * cuts] for i in range(count)]


def grads_kernel(count, ids, *refs):
    groups = [refs[4 * i : 4 * i + 4] for i in range(count)]
    grad_in, grad_out, rows, grads, own, core, tiles_in, tiles_out, sems = refs[4 * count :]
    at = 0
    for group in groups:
        n = group[0].shape[0]
        for held, part in zip((rows, grads, own, core), group):
            held[at : at + n, :] = part[...]
        at += n
    features, units = rows.shape[1], grad_out.shape[0]
    f_tile, width = features // 4, units // 4
    copies = []
    for j in range(4):
        turned = rows[:, j * f_tile : (j + 1) * f_tile].T
        for held, half in ((own, ids[1]), (core, 1 - ids[1])):
            for i in range(2):
                both = dot(turned, held[:, (3 * i + 1) * width : (3 * i + 3) * width]).astype(BF)
                for part in range(2):
                    to = pl.multiple_of(part * units + (half * 2 + i) * width, width)
                    tiles_in[j, :, pl.ds(to, width)] = both[:, part * width : (part + 1) * width]
        copies.append(pltpu.make_async_copy(tiles_in.at[j], grad_in.at[j * f_tile : (j + 1) * f_tile, :], sems.at[j]))
        copies[-1].start()
    for j, (held, half) in enumerate(((own, ids[1]), (core, 1 - ids[1]))):
        for i in range(2):
            turned = held[:, 3 * i * width : (3 * i + 1) * width].T
            tiles_out[2 * j + i] = dot(turned, grads[...]).astype(BF)
            to = pl.multiple_of((half * 2 + i) * width, width)
            copies.append(pltpu.make_async_copy(tiles_out.at[2 * j + i], grad_out.at[pl.ds(to, width), :], sems.at[4 + 2 * j + i]))
            copies[-1].start()
    for copy in copies:
        copy.wait()


def grads_step(ids, groups, units):
    features = groups[0][0].shape[1]
    rows = sum(group[0].shape[0] for group in groups)
    whole = pl.BlockSpec(memory_space=pltpu.VMEM)
    arrays = [x for group in groups for x in group]
    return pl.pallas_call(
        lambda *refs: grads_kernel(len(groups), *refs),
        out_shape=[
            jax.ShapeDtypeStruct((features, 2 * units), BF),
            jax.ShapeDtypeStruct((units, features), BF),
        ],
        in_specs=[pl.BlockSpec(memory_space=pltpu.SMEM)] + [whole] * len(arrays),
        out_specs=[pl.BlockSpec(memory_space=pltpu.HBM)] * 2,
        scratch_shapes=[
            pltpu.VMEM((rows, features), BF),
            pltpu.VMEM((rows, features), BF),
            pltpu.VMEM((rows, units * 3 // 2), BF),
            pltpu.VMEM((rows, units * 3 // 2), BF),
            pltpu.VMEM((4, features // 4, 2 * units), BF),
            pltpu.VMEM((4, units // 4, features), BF),
            pltpu.SemaphoreType.DMA((8,)),
        ],
        compiler_params=pltpu.CompilerParams(vmem_limit_bytes=GRADS_LIMIT),
        cost_estimate=COST,
        name="grads",
    )(ids, *arrays)


def final_kernel(capacity, sources, parts, ids, routes, weight, *refs):
    taken, cuts = sum(parts), max(parts)
    partial, (mixed, grad_tokens) = refs[taken:-2], refs[-2:]
    homes = [refs[sum(parts[:i]) : sum(parts[: i + 1])] for i in range(len(parts))]
    rows = routes.shape[1]
    me = ids[0]
    count = len(sources)
    eye = iota((rows, rows), 0) == iota((rows, rows), 1)

    def column(line, zero):
        return jnp.sum(jnp.where(eye, line, zero), axis=1, keepdims=True)

    lane = iota((rows, count), 1)
    expert = lane * 0
    for i, s in enumerate(sources):
        expert = jnp.where(lane == i, s, expert)
    expert = expert ^ me
    named, w_named = None, None
    for k in range(routes.shape[0]):
        hit = column(routes[k : k + 1, :], 0) == expert
        w_hit = jnp.where(hit, column(weight[k : k + 1, :], 0.0), 0.0)
        named = hit if named is None else named | hit
        w_named = w_hit if w_named is None else w_named + w_hit
    before = (iota((rows, rows), 1) < iota((rows, rows), 0)).astype(BF)
    rank = dot(before, named.astype(F32).astype(BF)).astype(jnp.int32)
    key = jnp.where(named, rank, -2 * capacity)
    slot = iota((rows, 2 * capacity), 1)
    width = mixed.shape[1] // cuts
    for j in range(cuts):
        at = slice(j * width, (j + 1) * width)
        total_out, total_grad = (p[:, at] for p in partial) if partial else (None, None)
        for i in range(count):
            home = homes[i][j][...] if len(homes[i]) == cuts else homes[i][0][:, at]
            row_key = key[:, i : i + 1]
            pick_out = (row_key == slot).astype(F32).astype(BF)
            pick_grad = (row_key + capacity == slot).astype(F32).astype(BF)
            out = w_named[:, i : i + 1] * dot(pick_out, home)
            grad = dot(pick_grad, home)
            total_out = out if total_out is None else total_out + out
            total_grad = grad if total_grad is None else total_grad + grad
        mixed[:, at] = total_out.astype(mixed.dtype)
        grad_tokens[:, at] = total_grad.astype(mixed.dtype)


def final(ids, routes, weight, homes, sources, capacity, partial, dtype):
    parts = [len(home) for home in homes]
    shape = (routes.shape[0], homes[0][0].shape[1] * parts[0])
    return call(
        lambda *refs: final_kernel(capacity, sources, parts, *refs),
        "final",
        [jax.ShapeDtypeStruct(shape, dtype)] * 2,
        [ids],
        routes.T,
        weight.T,
        *[x for home in homes for x in home],
        *partial,
    )


def per_device_chunked(tokens, routes, route_weight, cotangent, w_in, w_out):
    tok_rows = tokens.shape[0]
    top_count = routes.shape[1]
    n_expert = lax.axis_size("expert")
    n_dp = lax.axis_size("dp")
    capacity = tok_rows * top_count * 5 // (4 * n_expert)
    w_in, w_out = w_in[0], w_out[0]
    units = w_out.shape[0]
    ids = jnp.stack([lax.axis_index("expert"), lax.axis_index("dp") % 2]).astype(jnp.int32)

    def across(x, s):
        return lax.ppermute(x, "expert", [(i, i ^ s) for i in range(n_expert)]) if s else x

    def beside(x, s):
        return lax.ppermute(x, "dp", [(i, i ^ s) for i in range(n_dp)])

    def after(x, *earlier):
        return lax.optimization_barrier((x, *earlier))[0]

    def after(x, *earlier):
        return lax.optimization_barrier((x, *earlier))[0]

    inside = lax.axis_index("expert") >= 0

    def stage(body, *args):
        shapes = jax.eval_shape(body, *args)
        return lax.cond(inside, body, lambda *_: jax.tree.map(lambda x: jnp.zeros(x.shape, x.dtype), shapes), *args)

    def up_part(blocks, weights, *earlier):
        first, *others = blocks
        return up_step(ids, [after(first, *earlier), *others], weights, capacity)

    def core_part(state, *earlier):
        rows, grads, send, keep = state
        return rows, grads, keep, beside(after(send, *earlier) if earlier else send, 1)

    def up_in_halves(blocks):
        rows, grads, send, *weights = other_half(ids, blocks, w_in, w_out, capacity)
        core = beside(send, 1)
        return (rows, grads, own_half(ids, after(rows, send), grads, weights), core), weights

    def sum_part(state, *earlier, cuts=1):
        rows, grads, keep, core = state
        return rows, grads, keep, core, sum_step(after(keep, *earlier), core, cuts)

    def x_part(state):
        rows, grads, keep, core, totals = state
        return rows, grads, keep, core, [beside(total, 2) for total in totals]

    def act_part(state, *earlier):
        rows, grads, keep, core, others = state
        own = act_step(after(keep, *earlier), core, others)
        return rows, grads, own, beside(own, 1)

    def down_part(group, weights, count):
        return down_step(ids, *group[2:], weights, count, capacity)

    def down_in_halves(group, weights, count):
        _, _, own, core = group
        sums = down_own(ids, own, weights)
        return down_other(ids, *sums, after(core, *sums), weights, count, capacity)

    def act_both(state, next_state, *earlier):
        rows, grads, keep, core, (other,) = state
        own, next_total = act_and_sum(after(keep, *earlier), core, other, *next_state[2:])
        return (rows, grads, own, beside(own, 1)), (*next_state, [next_total])

    def first_stage(blocks):
        state, _ = up_in_halves(blocks)
        return sum_part(state, cuts=2)

    def far_stage(blocks, before, before_count, next_blocks):
        state, held = up_in_halves(blocks)
        state = sum_part(state)
        before = act_part(before, *state[4])
        next_state = up_part(next_blocks, held, before[2])
        back = down_part((*before[:2], after(before[2], next_state[2]), before[3]), held, before_count)
        ends = [x for parts in back for x in parts]
        group, next_state = act_both(x_part(state), core_part(next_state, *ends), *ends)
        return group, down_in_halves(group, held, len(blocks)), next_state, before, back

    def rest_stage(state):
        group = act_part(state)
        _, _, own, core = group
        *sums, held_in, held_out = down_own_alone(ids, own, w_in, w_out)
        return group, down_other(ids, *sums, after(core, *sums), (held_in, held_out), size, capacity, 2)

    half, quarter = n_expert // 2, n_expert // 4
    size = quarter // 2
    near = [list(range(quarter)), list(range(quarter, quarter + size)), list(range(quarter + size, half))]
    far, last = list(range(half, half + quarter)), list(range(half + quarter, n_expert))
    sent = prep(ids, tokens, routes, route_weight, cotangent, n_expert, capacity)
    came, home = {0: sent[0]}, {}

    def blocks(sources, *earlier):
        first, *others = [came[s] for s in sources]
        return [after(first, *earlier), *others]

    def start(sources, *earlier):
        came.update({s: across(after(sent[s], *earlier) if earlier else sent[s], s) for s in sources if s})

    def start_back(sources, back, *earlier):
        for s, parts in zip(sources, back):
            home[s] = [across(after(x, *earlier) if earlier else x, s) for x in parts]

    def arrived(sources):
        return [x for s in sources for x in home[s]]

    start(far + near[0] + near[1])
    state_0 = stage(first_stage, blocks(near[0]))
    start(last, *blocks(far + near[1]), *state_0[4])
    state_0 = x_part(state_0)
    start(near[2], *blocks(far), *state_0[4])
    group_far, back_far, state_1, group_0, back_0 = stage(
        lambda a, b, c: far_stage(a, b, quarter, c), blocks(far), state_0, blocks(near[1])
    )
    start_back(far + near[0], back_far + back_0, *blocks(last))
    group_last, back_last, state_2, group_1, back_1 = stage(
        lambda a, b, c: far_stage(a, b, size, c), blocks(last, group_far[3]), x_part(state_1), blocks(near[2])
    )
    start_back(last, back_last, *arrived(far + near[0]))
    start_back(near[1], back_1)
    group_2, back_2 = stage(rest_stage, x_part(state_2))
    start_back(near[2], back_2)

    def add(sources, partial, dtype):
        return final(ids, routes, route_weight, [home[s] for s in sources], sources, capacity, partial, dtype)

    groups = [group_0, group_far, group_1, group_last, group_2]
    grad_in, grad_out = grads_step(ids, groups, units)
    partial = add(near[0] + far, [], F32)
    partial = add(last, partial, F32)
    mixed, grad_tokens = add(near[1] + near[2], partial, BF)
    return mixed, grad_tokens, grad_in[None], grad_out[None]


def activate(pre_act, grad_hidden):
    units = pre_act.shape[1] // 2
    gate_part = pre_act[:, :units]
    up_part = pre_act[:, units:]
    sigmoid_gate = jax.nn.sigmoid(gate_part)
    silu_gate = gate_part * sigmoid_gate
    hidden = (silu_gate * up_part).astype(jnp.bfloat16)
    grad_gate = grad_hidden * up_part * sigmoid_gate * (1.0 + gate_part * (1.0 - sigmoid_gate))
    grad_up = grad_hidden * silu_gate
    return (hidden, jnp.concatenate([grad_gate, grad_up], axis=1).astype(jnp.bfloat16))


def per_device(tokens, routes, route_weight, cotangent, w_in, w_out):
    tok_rows, features = tokens.shape
    top_count = routes.shape[1]
    n_expert = lax.axis_size("expert")
    local_experts = w_in.shape[0]
    hidden_units = w_out.shape[1]
    experts = n_expert * local_experts
    capacity = tok_rows * top_count * 5 // (4 * experts)
    slot_count = experts * capacity
    flat_routes = routes.reshape(-1)
    onehot = (flat_routes[:, None] == jnp.arange(experts, dtype=jnp.int32)[None, :]).astype(
        jnp.int32
    )
    slot_rank = jnp.sum((jnp.cumsum(onehot, axis=0) - onehot) * onehot, axis=1)
    target = flat_routes * capacity + slot_rank
    placing = (target[None, :] == jnp.arange(slot_count, dtype=jnp.int32)[:, None]).astype(
        jnp.bfloat16
    )
    choose_token = jnp.sum(placing.reshape(slot_count, tok_rows, top_count), axis=2)
    scaled_grads = (route_weight[:, :, None] * cotangent[:, None, :].astype(jnp.float32)).astype(
        jnp.bfloat16
    )
    scaled_grads = scaled_grads.reshape(tok_rows * top_count, features)
    send_rows = jnp.dot(choose_token, tokens, preferred_element_type=jnp.float32).astype(
        jnp.bfloat16
    )
    send_grads = jnp.dot(placing, scaled_grads, preferred_element_type=jnp.float32).astype(
        jnp.bfloat16
    )
    send_rows = send_rows.reshape(n_expert, local_experts * capacity, features)
    send_grads = send_grads.reshape(n_expert, local_experts * capacity, features)
    routed_rows, routed_grads = (
        lax.all_to_all(send_rows, "expert", split_axis=0, concat_axis=0, tiled=True),
        lax.all_to_all(send_grads, "expert", split_axis=0, concat_axis=0, tiled=True),
    )
    rows_four = routed_rows.reshape(n_expert, local_experts, capacity, features)
    grads_four = routed_grads.reshape(n_expert, local_experts, capacity, features)
    total_rows = n_expert * local_experts * capacity
    pre_part = jnp.einsum("secd,edf->secf", rows_four, w_in, preferred_element_type=jnp.float32)
    back_part = jnp.einsum("secd,efd->secf", grads_four, w_out, preferred_element_type=jnp.float32)
    pre_flat = pre_part.reshape(total_rows, 2 * hidden_units)
    back_flat = back_part.reshape(total_rows, hidden_units)
    pre_share, back_share = (
        lax.psum_scatter(pre_flat, "dp", scatter_dimension=0, tiled=True),
        lax.psum_scatter(back_flat, "dp", scatter_dimension=0, tiled=True),
    )
    hidden_share, both_share = activate(pre_share, back_share)
    hidden, grad_both = (
        lax.all_gather(hidden_share, "dp", axis=0, tiled=True),
        lax.all_gather(both_share, "dp", axis=0, tiled=True),
    )
    hidden_four = hidden.reshape(n_expert, local_experts, capacity, hidden_units)
    both_four = grad_both.reshape(n_expert, local_experts, capacity, 2 * hidden_units)
    out_rows = jnp.einsum(
        "secf,efd->secd", hidden_four, w_out, preferred_element_type=jnp.float32
    ).astype(jnp.bfloat16)
    grad_rows = jnp.einsum(
        "secf,edf->secd", both_four, w_in, preferred_element_type=jnp.float32
    ).astype(jnp.bfloat16)
    grad_out = jnp.einsum(
        "secf,secd->efd", hidden_four, grads_four, preferred_element_type=jnp.float32
    ).astype(jnp.bfloat16)
    grad_in = jnp.einsum(
        "secd,secf->edf", rows_four, both_four, preferred_element_type=jnp.float32
    ).astype(jnp.bfloat16)
    home_out, home_grad = (
        lax.all_to_all(
            out_rows.reshape(n_expert, local_experts * capacity, features),
            "expert",
            split_axis=0,
            concat_axis=0,
            tiled=True,
        ),
        lax.all_to_all(
            grad_rows.reshape(n_expert, local_experts * capacity, features),
            "expert",
            split_axis=0,
            concat_axis=0,
            tiled=True,
        ),
    )
    route_out = jnp.dot(
        placing.T, home_out.reshape(slot_count, features), preferred_element_type=jnp.float32
    )
    route_out = route_out.reshape(tok_rows, top_count, features)
    mixed = jnp.sum(route_weight[:, :, None] * route_out, axis=1).astype(jnp.bfloat16)
    grad_tokens = jnp.dot(
        choose_token.T, home_grad.reshape(slot_count, features), preferred_element_type=jnp.float32
    )
    return (mixed, grad_tokens.astype(jnp.bfloat16), grad_in, grad_out)


def solution(mesh):
    placed = (
        P("expert", "dp"),
        P("expert", None),
        P("expert", None),
        P("expert", "dp"),
        P("expert", "dp", None),
        P("expert", None, "dp"),
    )
    sizes = dict(mesh.shape)
    chunked = sizes["dp"] == 4 and sizes["expert"] in (8, 16)
    return jax.shard_map(
        per_device_chunked if chunked else per_device,
        mesh=mesh,
        in_specs=placed,
        out_specs=(
            P("expert", "dp"),
            P("expert", "dp"),
            P("expert", "dp", None),
            P("expert", None, "dp"),
        ),
        check_vma=False,
    )
```

```python
import jax
import jax.numpy as jnp
from jax import lax
from jax.experimental import pallas as pl
from jax.experimental.pallas import tpu as pltpu
from jax.sharding import PartitionSpec as P

BF = jnp.bfloat16
F32 = jnp.float32
VMEM_LIMIT = 18 * 1024 * 1024
GRADS_LIMIT = 32 * 1024 * 1024
PREP_LIMIT = 60 * 1024 * 1024
COST = pl.CostEstimate(flops=1, bytes_accessed=1, transcendentals=0)


def dot(a, b):
    return lax.dot_general(a, b, (((1,), (0,)), ((), ())), preferred_element_type=F32)


def dot_t(a, b):
    return lax.dot_general(a, b, (((1,), (1,)), ((), ())), preferred_element_type=F32)


def t_dot(a, b):
    return lax.dot_general(a, b, (((0,), (0,)), ((), ())), preferred_element_type=F32)


def iota(shape, dim):
    return lax.broadcasted_iota(jnp.int32, shape, dim)


def padded(capacity):
    return -(-capacity // 16) * 16


def prep_kernel(capacity, ids, tokens, routes, weight, cotangent, *refs):
    outs, (token_rows, grad_rows, route_lines, weight_lines, sems) = refs[:-5], refs[-5:]
    pairs = ((routes, route_lines), (weight, weight_lines), (tokens, token_rows), (cotangent, grad_rows))
    copies = [pltpu.make_async_copy(x, held, sems.at[i]) for i, (x, held) in enumerate(pairs)]
    for copy in copies:
        copy.start()
    for copy in copies[:2]:
        copy.wait()
    routes, weight = route_lines, weight_lines
    count = len(outs)
    rows = routes.shape[1]
    expert = iota((count, rows), 0) ^ ids[0]
    named, w_named = None, None
    for k in range(routes.shape[0]):
        hit = routes[k : k + 1, :] == expert
        w_hit = jnp.where(hit, weight[k : k + 1, :], 0.0)
        named = hit if named is None else named | hit
        w_named = w_hit if w_named is None else w_named + w_hit
    before = (iota((rows, rows), 0) < iota((rows, rows), 1)).astype(F32).astype(BF)
    rank = dot(named.astype(F32).astype(BF), before).astype(jnp.int32)
    key = jnp.where(named, rank, -2 * capacity)
    slot = iota((2 * capacity, rows), 0)
    picks = []
    for s in range(count):
        row_key = key[s : s + 1, :]
        pick_token = (row_key == slot).astype(F32)
        pick_grad = (row_key + capacity == slot).astype(F32)
        scale = jnp.sum(pick_grad * w_named[s : s + 1, :], axis=1, keepdims=True)
        scale = scale + (slot[:, 0:1] < capacity).astype(F32)
        picks.append((pick_token.astype(BF), pick_grad.astype(BF), scale))
    for copy in copies[2:]:
        copy.wait()
    for out, (pick_token, pick_grad, scale) in zip(outs, picks):
        out[...] = (scale * (dot(pick_token, token_rows[...]) + dot(pick_grad, grad_rows[...]))).astype(BF)


def prep(ids, tokens, routes, weight, cotangent, count, capacity):
    rows, features = tokens.shape
    whole = pl.BlockSpec(memory_space=pltpu.VMEM)
    away = pl.BlockSpec(memory_space=pltpu.HBM)
    return pl.pallas_call(
        lambda *refs: prep_kernel(capacity, *refs),
        out_shape=[jax.ShapeDtypeStruct((2 * capacity, features), BF)] * count,
        in_specs=[pl.BlockSpec(memory_space=pltpu.SMEM)] + [away] * 4,
        out_specs=[whole] * count,
        scratch_shapes=[pltpu.VMEM((rows, features), BF)] * 2
        + [pltpu.VMEM(routes.T.shape, routes.dtype), pltpu.VMEM(weight.T.shape, weight.dtype)]
        + [pltpu.SemaphoreType.DMA((4,))],
        compiler_params=pltpu.CompilerParams(vmem_limit_bytes=PREP_LIMIT),
        cost_estimate=COST,
        name="prep",
    )(ids, tokens, routes.T, weight.T, cotangent)


def call(kernel, name, out_shapes, scalars, *arrays):
    whole = pl.BlockSpec(memory_space=pltpu.VMEM)
    return pl.pallas_call(
        kernel,
        out_shape=out_shapes,
        in_specs=[pl.BlockSpec(memory_space=pltpu.SMEM)] * len(scalars) + [whole] * len(arrays),
        out_specs=jax.tree.map(lambda _: whole, out_shapes),
        compiler_params=pltpu.CompilerParams(vmem_limit_bytes=VMEM_LIMIT),
        cost_estimate=COST,
        name=name,
    )(*scalars, *arrays)


def lay_out(capacity, blocks, row_out, grad_out):
    pad = padded(capacity)
    spot = iota((2 * pad, 2 * capacity), 0)
    col = iota((2 * pad, 2 * capacity), 1)
    target = jnp.where(col < capacity, col, col + pad - capacity)
    spread = (spot == target).astype(F32).astype(BF)
    for i, block in enumerate(blocks):
        laid = dot(spread, block[...]).astype(BF)
        row_out[i * pad : (i + 1) * pad, :] = laid[:pad]
        grad_out[i * pad : (i + 1) * pad, :] = laid[pad:]


def half_products(half, rows, grads, w_in, w_out, out):
    units = w_out.shape[0]
    width = units // 4
    for j in range(2):
        at = pl.multiple_of((half * 2 + j) * width, width)
        at_up = pl.multiple_of(units + (half * 2 + j) * width, width)
        gate = dot(rows[...], w_in[:, pl.ds(at, width)])
        up = dot(rows[...], w_in[:, pl.ds(at_up, width)])
        back = dot_t(grads[...], w_out[pl.ds(at, width), :])
        for part, term in enumerate((gate, up, back)):
            out[:, (3 * j + part) * width : (3 * j + part + 1) * width] = term.astype(out.dtype)


PIECES = 1


def weight_copies(halves, far_in, far_out, w_in, w_out, sems):
    units = far_out.shape[0]
    span, depth = units // 2, far_in.shape[0] // PIECES
    copies = []
    for half in halves:
        at = pl.ds(pl.multiple_of(half * span, span), span)
        at_up = pl.ds(pl.multiple_of(units + half * span, span), span)
        for k in range(PIECES):
            rows = slice(k * depth, (k + 1) * depth)
            step = span // PIECES
            row = pl.ds(pl.multiple_of(half * span + k * step, step), step)
            for x, y in (
                (far_in.at[rows, at], w_in.at[rows, at]),
                (far_in.at[rows, at_up], w_in.at[rows, at_up]),
                (far_out.at[row, :], w_out.at[row, :]),
            ):
                copies.append(pltpu.make_async_copy(x, y, sems.at[len(copies)]))
    for copy in copies:
        copy.start()
    return copies


def other_half(ids, blocks, w_in, w_out, capacity):
    units, features = w_out.shape
    rows = len(blocks) * padded(capacity)
    shape = jax.ShapeDtypeStruct
    whole = pl.BlockSpec(memory_space=pltpu.VMEM)
    away = pl.BlockSpec(memory_space=pl.ANY)

    def kernel(ids, *refs):
        held, (far_in, far_out, row_out, grad_out, send, near_in, near_out, sems) = refs[:-8], refs[-8:]
        copies = weight_copies((1 - ids[1], ids[1]), far_in, far_out, near_in, near_out, sems)
        lay_out(capacity, held, row_out, grad_out)
        for copy in copies[: 3 * PIECES]:
            copy.wait()
        half_products(1 - ids[1], row_out, grad_out, near_in, near_out, send)
        for copy in copies[3 * PIECES :]:
            copy.wait()

    return pl.pallas_call(
        kernel,
        out_shape=[
            shape((rows, features), BF),
            shape((rows, features), BF),
            shape((rows, 3 * units // 2), BF),
            shape(w_in.shape, BF),
            shape(w_out.shape, BF),
        ],
        in_specs=[pl.BlockSpec(memory_space=pltpu.SMEM)] + [whole] * len(blocks) + [away] * 2,
        out_specs=[whole] * 5,
        scratch_shapes=[pltpu.SemaphoreType.DMA((6 * PIECES,))],
        compiler_params=pltpu.CompilerParams(vmem_limit_bytes=VMEM_LIMIT),
        cost_estimate=COST,
        name="up",
    )(ids, *blocks, w_in, w_out)


def own_half(ids, rows, grads, weights):
    def kernel(ids, rows, grads, w_in, w_out, keep):
        half_products(ids[1], rows, grads, w_in, w_out, keep)

    shape = jax.ShapeDtypeStruct((rows.shape[0], 3 * weights[1].shape[0] // 2), F32)
    return call(kernel, "up", shape, [ids], rows, grads, *weights)


def up_step(ids, blocks, weights, capacity):
    units, features = weights[1].shape
    rows = len(blocks) * padded(capacity)
    shape = jax.ShapeDtypeStruct

    def kernel(ids, *refs):
        held, (w_in, w_out, row_out, grad_out, send, keep) = refs[:-6], refs[-6:]
        lay_out(capacity, held, row_out, grad_out)
        half_products(1 - ids[1], row_out, grad_out, w_in, w_out, send)
        half_products(ids[1], row_out, grad_out, w_in, w_out, keep)

    return call(
        kernel,
        "up",
        [
            shape((rows, features), BF),
            shape((rows, features), BF),
            shape((rows, 3 * units // 2), BF),
            shape((rows, 3 * units // 2), F32),
        ],
        [ids],
        *blocks,
        *weights,
    )


def sum_kernel(keep, core, *outs):
    cut = keep.shape[1] // len(outs)
    for j, out in enumerate(outs):
        at = slice(j * cut, (j + 1) * cut)
        out[...] = (keep[:, at] + core[:, at].astype(F32)).astype(BF)


def sum_step(keep, core, cuts=1):
    shape = jax.ShapeDtypeStruct((keep.shape[0], keep.shape[1] // cuts), BF)
    return call(sum_kernel, "total", [shape] * cuts, [], keep, core)


def activated(keep, core, others, out):
    width = keep.shape[1] // 6
    for j in range(2):
        base = 3 * width * j
        other, skip = others[j % len(others)], base * (len(others) - 1)
        gate, up, back = (
            keep[:, at : at + width]
            + core[:, at : at + width].astype(F32)
            + other[:, at - skip : at - skip + width].astype(F32)
            for at in (base, base + width, base + 2 * width)
        )
        sigmoid = jax.nn.sigmoid(gate)
        silu = gate * sigmoid
        out[:, base : base + width] = (silu * up).astype(BF)
        out[:, base + width : base + 2 * width] = (
            back * up * sigmoid * (1.0 + gate * (1.0 - sigmoid))
        ).astype(BF)
        out[:, base + 2 * width : base + 3 * width] = (back * silu).astype(BF)


def act_step(keep, core, others):
    def kernel(keep, core, *refs):
        activated(keep, core, refs[:-1], refs[-1])

    return call(kernel, "act", jax.ShapeDtypeStruct(keep.shape, BF), [], keep, core, *others)


def act_and_sum(keep, core, other, next_keep, next_core):
    def kernel(keep, core, other, next_keep, next_core, out, total):
        activated(keep, core, [other], out)
        sum_kernel(next_keep, next_core, total)

    shapes = [jax.ShapeDtypeStruct(x.shape, BF) for x in (keep, next_keep)]
    return call(kernel, "act", shapes, [], keep, core, other, next_keep, next_core)


def half_rows(half, held, w_in, w_out):
    units = w_out.shape[0]
    width = units // 4
    out_rows = grad_rows = None
    for j in range(2):
        base = 3 * width * j
        at = pl.multiple_of((half * 2 + j) * width, width)
        at_up = pl.multiple_of(units + (half * 2 + j) * width, width)
        a = dot(held[:, base : base + width], w_out[pl.ds(at, width), :])
        b = dot_t(held[:, base + width : base + 2 * width], w_in[:, pl.ds(at, width)])
        c = dot_t(held[:, base + 2 * width : base + 3 * width], w_in[:, pl.ds(at_up, width)])
        out_rows = a if out_rows is None else out_rows + a
        grad_rows = b + c if grad_rows is None else grad_rows + (b + c)
    return out_rows, grad_rows


def pack(capacity, out_rows, grad_rows, outs):
    pad = padded(capacity)
    spot = iota((2 * capacity, pad), 0)
    col = iota((2 * capacity, pad), 1)
    pack_out = (spot == jnp.where(col < capacity, col, -1)).astype(F32).astype(BF)
    pack_grad = (spot - capacity == jnp.where(col < capacity, col, -capacity - 1)).astype(F32).astype(BF)
    out_rows, grad_rows = out_rows.astype(BF), grad_rows.astype(BF)
    sources = out_rows.shape[0] // pad
    cuts = len(outs) // sources
    for i in range(sources):
        at = slice(i * pad, (i + 1) * pad)
        packed = (dot(pack_out, out_rows[at]) + dot(pack_grad, grad_rows[at])).astype(BF)
        cut = packed.shape[1] // cuts
        for j in range(cuts):
            outs[i * cuts + j][...] = packed[:, j * cut : (j + 1) * cut]


def down_step(ids, own, core, weights, count, capacity):
    def kernel(ids, own, core, w_in, w_out, *outs):
        out_rows, grad_rows = half_rows(ids[1], own, w_in, w_out)
        more_out, more_grad = half_rows(1 - ids[1], core, w_in, w_out)
        pack(capacity, out_rows + more_out, grad_rows + more_grad, outs)

    shape = jax.ShapeDtypeStruct((2 * capacity, weights[1].shape[1]), BF)
    return [[x] for x in call(kernel, "down", [shape] * count, [ids], own, core, *weights)]


def down_own(ids, own, weights):
    def kernel(ids, own, w_in, w_out, out_rows, grad_rows):
        out_rows[...], grad_rows[...] = half_rows(ids[1], own, w_in, w_out)

    shape = jax.ShapeDtypeStruct((own.shape[0], weights[1].shape[1]), F32)
    return call(kernel, "down", [shape] * 2, [ids], own, *weights)


def down_own_alone(ids, own, w_in, w_out):
    shape = jax.ShapeDtypeStruct
    whole = pl.BlockSpec(memory_space=pltpu.VMEM)
    away = pl.BlockSpec(memory_space=pl.ANY)

    def kernel(ids, own, far_in, far_out, out_rows, grad_rows, near_in, near_out, sems):
        copies = weight_copies((ids[1], 1 - ids[1]), far_in, far_out, near_in, near_out, sems)
        for copy in copies[: 3 * PIECES]:
            copy.wait()
        out_rows[...], grad_rows[...] = half_rows(ids[1], own, near_in, near_out)
        for copy in copies[3 * PIECES :]:
            copy.wait()

    sums = shape((own.shape[0], w_out.shape[1]), F32)
    return pl.pallas_call(
        kernel,
        out_shape=[sums, sums, shape(w_in.shape, BF), shape(w_out.shape, BF)],
        in_specs=[pl.BlockSpec(memory_space=pltpu.SMEM), whole] + [away] * 2,
        out_specs=[whole] * 4,
        scratch_shapes=[pltpu.SemaphoreType.DMA((6 * PIECES,))],
        compiler_params=pltpu.CompilerParams(vmem_limit_bytes=VMEM_LIMIT),
        cost_estimate=COST,
        name="down",
    )(ids, own, w_in, w_out)


def down_other(ids, out_rows, grad_rows, core, weights, count, capacity, cuts=1):
    def kernel(ids, out_rows, grad_rows, core, w_in, w_out, *outs):
        more_out, more_grad = half_rows(1 - ids[1], core, w_in, w_out)
        pack(capacity, out_rows[...] + more_out, grad_rows[...] + more_grad, outs)

    shape = jax.ShapeDtypeStruct((2 * capacity, weights[1].shape[1] // cuts), BF)
    outs = call(kernel, "down", [shape] * (count * cuts), [ids], out_rows, grad_rows, core, *weights)
    return [outs[i * cuts : (i + 1) * cuts] for i in range(count)]


def grads_kernel(count, ids, *refs):
    groups = [refs[4 * i : 4 * i + 4] for i in range(count)]
    grad_in, grad_out, rows, grads, own, core, tiles_in, tiles_out, sems = refs[4 * count :]
    at = 0
    for group in groups:
        n = group[0].shape[0]
        for held, part in zip((rows, grads, own, core), group):
            held[at : at + n, :] = part[...]
        at += n
    features, units = rows.shape[1], grad_out.shape[0]
    f_tile, width = features // 4, units // 4
    copies = []
    for j in range(4):
        turned = rows[:, j * f_tile : (j + 1) * f_tile].T
        for held, half in ((own, ids[1]), (core, 1 - ids[1])):
            for i in range(2):
                both = dot(turned, held[:, (3 * i + 1) * width : (3 * i + 3) * width]).astype(BF)
                for part in range(2):
                    to = pl.multiple_of(part * units + (half * 2 + i) * width, width)
                    tiles_in[j, :, pl.ds(to, width)] = both[:, part * width : (part + 1) * width]
        copies.append(pltpu.make_async_copy(tiles_in.at[j], grad_in.at[j * f_tile : (j + 1) * f_tile, :], sems.at[j]))
        copies[-1].start()
    for j, (held, half) in enumerate(((own, ids[1]), (core, 1 - ids[1]))):
        for i in range(2):
            turned = held[:, 3 * i * width : (3 * i + 1) * width].T
            tiles_out[2 * j + i] = dot(turned, grads[...]).astype(BF)
            to = pl.multiple_of((half * 2 + i) * width, width)
            copies.append(pltpu.make_async_copy(tiles_out.at[2 * j + i], grad_out.at[pl.ds(to, width), :], sems.at[4 + 2 * j + i]))
            copies[-1].start()
    for copy in copies:
        copy.wait()


def grads_step(ids, groups, units):
    features = groups[0][0].shape[1]
    rows = sum(group[0].shape[0] for group in groups)
    whole = pl.BlockSpec(memory_space=pltpu.VMEM)
    arrays = [x for group in groups for x in group]
    return pl.pallas_call(
        lambda *refs: grads_kernel(len(groups), *refs),
        out_shape=[
            jax.ShapeDtypeStruct((features, 2 * units), BF),
            jax.ShapeDtypeStruct((units, features), BF),
        ],
        in_specs=[pl.BlockSpec(memory_space=pltpu.SMEM)] + [whole] * len(arrays),
        out_specs=[pl.BlockSpec(memory_space=pltpu.HBM)] * 2,
        scratch_shapes=[
            pltpu.VMEM((rows, features), BF),
            pltpu.VMEM((rows, features), BF),
            pltpu.VMEM((rows, units * 3 // 2), BF),
            pltpu.VMEM((rows, units * 3 // 2), BF),
            pltpu.VMEM((4, features // 4, 2 * units), BF),
            pltpu.VMEM((4, units // 4, features), BF),
            pltpu.SemaphoreType.DMA((8,)),
        ],
        compiler_params=pltpu.CompilerParams(vmem_limit_bytes=GRADS_LIMIT),
        cost_estimate=COST,
        name="grads",
    )(ids, *arrays)


def final_kernel(capacity, sources, parts, ids, routes, weight, *refs):
    taken, cuts = sum(parts), max(parts)
    partial, (mixed, grad_tokens) = refs[taken:-2], refs[-2:]
    homes = [refs[sum(parts[:i]) : sum(parts[: i + 1])] for i in range(len(parts))]
    rows = routes.shape[1]
    me = ids[0]
    count = len(sources)
    eye = iota((rows, rows), 0) == iota((rows, rows), 1)

    def column(line, zero):
        return jnp.sum(jnp.where(eye, line, zero), axis=1, keepdims=True)

    lane = iota((rows, count), 1)
    expert = lane * 0
    for i, s in enumerate(sources):
        expert = jnp.where(lane == i, s, expert)
    expert = expert ^ me
    named, w_named = None, None
    for k in range(routes.shape[0]):
        hit = column(routes[k : k + 1, :], 0) == expert
        w_hit = jnp.where(hit, column(weight[k : k + 1, :], 0.0), 0.0)
        named = hit if named is None else named | hit
        w_named = w_hit if w_named is None else w_named + w_hit
    before = (iota((rows, rows), 1) < iota((rows, rows), 0)).astype(BF)
    rank = dot(before, named.astype(F32).astype(BF)).astype(jnp.int32)
    key = jnp.where(named, rank, -2 * capacity)
    slot = iota((rows, 2 * capacity), 1)
    width = mixed.shape[1] // cuts
    for j in range(cuts):
        at = slice(j * width, (j + 1) * width)
        total_out, total_grad = (p[:, at] for p in partial) if partial else (None, None)
        for i in range(count):
            home = homes[i][j][...] if len(homes[i]) == cuts else homes[i][0][:, at]
            row_key = key[:, i : i + 1]
            pick_out = (row_key == slot).astype(F32).astype(BF)
            pick_grad = (row_key + capacity == slot).astype(F32).astype(BF)
            out = w_named[:, i : i + 1] * dot(pick_out, home)
            grad = dot(pick_grad, home)
            total_out = out if total_out is None else total_out + out
            total_grad = grad if total_grad is None else total_grad + grad
        mixed[:, at] = total_out.astype(mixed.dtype)
        grad_tokens[:, at] = total_grad.astype(mixed.dtype)


def final(ids, routes, weight, homes, sources, capacity, partial, dtype):
    parts = [len(home) for home in homes]
    shape = (routes.shape[0], homes[0][0].shape[1] * parts[0])
    return call(
        lambda *refs: final_kernel(capacity, sources, parts, *refs),
        "final",
        [jax.ShapeDtypeStruct(shape, dtype)] * 2,
        [ids],
        routes.T,
        weight.T,
        *[x for home in homes for x in home],
        *partial,
    )


def per_device_chunked(tokens, routes, route_weight, cotangent, w_in, w_out):
    tok_rows = tokens.shape[0]
    top_count = routes.shape[1]
    n_expert = lax.axis_size("expert")
    n_dp = lax.axis_size("dp")
    capacity = tok_rows * top_count * 5 // (4 * n_expert)
    w_in, w_out = w_in[0], w_out[0]
    units = w_out.shape[0]
    ids = jnp.stack([lax.axis_index("expert"), lax.axis_index("dp") % 2]).astype(jnp.int32)

    def across(x, s):
        return lax.ppermute(x, "expert", [(i, i ^ s) for i in range(n_expert)]) if s else x

    def beside(x, s):
        return lax.ppermute(x, "dp", [(i, i ^ s) for i in range(n_dp)])

    def after(x, *earlier):
        return lax.optimization_barrier((x, *earlier))[0]

    def after(x, *earlier):
        return lax.optimization_barrier((x, *earlier))[0]

    inside = lax.axis_index("expert") >= 0

    def stage(body, *args):
        shapes = jax.eval_shape(body, *args)
        return lax.cond(inside, body, lambda *_: jax.tree.map(lambda x: jnp.zeros(x.shape, x.dtype), shapes), *args)

    def up_part(blocks, weights, *earlier):
        first, *others = blocks
        return up_step(ids, [after(first, *earlier), *others], weights, capacity)

    def core_part(state, *earlier):
        rows, grads, send, keep = state
        return rows, grads, keep, beside(after(send, *earlier) if earlier else send, 1)

    def up_in_halves(blocks):
        rows, grads, send, *weights = other_half(ids, blocks, w_in, w_out, capacity)
        core = beside(send, 1)
        return (rows, grads, own_half(ids, after(rows, send), grads, weights), core), weights

    def sum_part(state, *earlier, cuts=1):
        rows, grads, keep, core = state
        return rows, grads, keep, core, sum_step(after(keep, *earlier), core, cuts)

    def x_part(state):
        rows, grads, keep, core, totals = state
        return rows, grads, keep, core, [beside(total, 2) for total in totals]

    def act_part(state, *earlier):
        rows, grads, keep, core, others = state
        own = act_step(after(keep, *earlier), core, others)
        return rows, grads, own, beside(own, 1)

    def down_part(group, weights, count):
        return down_step(ids, *group[2:], weights, count, capacity)

    def down_in_halves(group, weights, count):
        _, _, own, core = group
        sums = down_own(ids, own, weights)
        return down_other(ids, *sums, after(core, *sums), weights, count, capacity)

    def act_both(state, next_state, *earlier):
        rows, grads, keep, core, (other,) = state
        own, next_total = act_and_sum(after(keep, *earlier), core, other, *next_state[2:])
        return (rows, grads, own, beside(own, 1)), (*next_state, [next_total])

    def first_stage(blocks):
        state, _ = up_in_halves(blocks)
        return sum_part(state, cuts=2)

    def far_stage(blocks, before, before_count, next_blocks):
        state, held = up_in_halves(blocks)
        state = sum_part(state)
        before = act_part(before, *state[4])
        next_state = up_part(next_blocks, held, before[2])
        back = down_part((*before[:2], after(before[2], next_state[2]), before[3]), held, before_count)
        ends = [x for parts in back for x in parts]
        group, next_state = act_both(x_part(state), core_part(next_state, *ends), *ends)
        return group, down_in_halves(group, held, len(blocks)), next_state, before, back

    def rest_stage(state):
        group = act_part(state)
        _, _, own, core = group
        *sums, held_in, held_out = down_own_alone(ids, own, w_in, w_out)
        return group, down_other(ids, *sums, after(core, *sums), (held_in, held_out), size, capacity, 2)

    half, quarter = n_expert // 2, n_expert // 4
    size = quarter // 2
    near = [list(range(quarter)), list(range(quarter, quarter + size)), list(range(quarter + size, half))]
    far, last = list(range(half, half + quarter)), list(range(half + quarter, n_expert))
    sent = prep(ids, tokens, routes, route_weight, cotangent, n_expert, capacity)
    came, home = {0: sent[0]}, {}

    def blocks(sources, *earlier):
        first, *others = [came[s] for s in sources]
        return [after(first, *earlier), *others]

    def start(sources, *earlier):
        came.update({s: across(after(sent[s], *earlier) if earlier else sent[s], s) for s in sources if s})

    def start_back(sources, back, *earlier):
        for s, parts in zip(sources, back):
            home[s] = [across(after(x, *earlier) if earlier else x, s) for x in parts]

    def arrived(sources):
        return [x for s in sources for x in home[s]]

    start(far + near[0] + near[1])
    state_0 = stage(first_stage, blocks(near[0]))
    start(last, *blocks(far + near[1]), *state_0[4])
    state_0 = x_part(state_0)
    start(near[2], *blocks(far), *state_0[4])
    group_far, back_far, state_1, group_0, back_0 = stage(
        lambda a, b, c: far_stage(a, b, quarter, c), blocks(far), state_0, blocks(near[1])
    )
    start_back(far + near[0], back_far + back_0, *blocks(last))
    group_last, back_last, state_2, group_1, back_1 = stage(
        lambda a, b, c: far_stage(a, b, size, c), blocks(last, group_far[3]), x_part(state_1), blocks(near[2])
    )
    start_back(last, back_last, *arrived(far + near[0]))
    start_back(near[1], back_1)
    group_2, back_2 = stage(rest_stage, x_part(state_2))
    start_back(near[2], back_2)

    def add(sources, partial, dtype):
        return final(ids, routes, route_weight, [home[s] for s in sources], sources, capacity, partial, dtype)

    groups = [group_0, group_far, group_1, group_last, group_2]
    grad_in, grad_out = grads_step(ids, groups, units)
    partial = add(near[0] + far, [], F32)
    partial = add(last, partial, F32)
    mixed, grad_tokens = add(near[1] + near[2], partial, BF)
    return mixed, grad_tokens, grad_in[None], grad_out[None]


def activate(pre_act, grad_hidden):
    units = pre_act.shape[1] // 2
    gate_part = pre_act[:, :units]
    up_part = pre_act[:, units:]
    sigmoid_gate = jax.nn.sigmoid(gate_part)
    silu_gate = gate_part * sigmoid_gate
    hidden = (silu_gate * up_part).astype(jnp.bfloat16)
    grad_gate = grad_hidden * up_part * sigmoid_gate * (1.0 + gate_part * (1.0 - sigmoid_gate))
    grad_up = grad_hidden * silu_gate
    return (hidden, jnp.concatenate([grad_gate, grad_up], axis=1).astype(jnp.bfloat16))


def per_device(tokens, routes, route_weight, cotangent, w_in, w_out):
    tok_rows, features = tokens.shape
    top_count = routes.shape[1]
    n_expert = lax.axis_size("expert")
    local_experts = w_in.shape[0]
    hidden_units = w_out.shape[1]
    experts = n_expert * local_experts
    capacity = tok_rows * top_count * 5 // (4 * experts)
    slot_count = experts * capacity
    flat_routes = routes.reshape(-1)
    onehot = (flat_routes[:, None] == jnp.arange(experts, dtype=jnp.int32)[None, :]).astype(
        jnp.int32
    )
    slot_rank = jnp.sum((jnp.cumsum(onehot, axis=0) - onehot) * onehot, axis=1)
    target = flat_routes * capacity + slot_rank
    placing = (target[None, :] == jnp.arange(slot_count, dtype=jnp.int32)[:, None]).astype(
        jnp.bfloat16
    )
    choose_token = jnp.sum(placing.reshape(slot_count, tok_rows, top_count), axis=2)
    scaled_grads = (route_weight[:, :, None] * cotangent[:, None, :].astype(jnp.float32)).astype(
        jnp.bfloat16
    )
    scaled_grads = scaled_grads.reshape(tok_rows * top_count, features)
    send_rows = jnp.dot(choose_token, tokens, preferred_element_type=jnp.float32).astype(
        jnp.bfloat16
    )
    send_grads = jnp.dot(placing, scaled_grads, preferred_element_type=jnp.float32).astype(
        jnp.bfloat16
    )
    send_rows = send_rows.reshape(n_expert, local_experts * capacity, features)
    send_grads = send_grads.reshape(n_expert, local_experts * capacity, features)
    routed_rows, routed_grads = (
        lax.all_to_all(send_rows, "expert", split_axis=0, concat_axis=0, tiled=True),
        lax.all_to_all(send_grads, "expert", split_axis=0, concat_axis=0, tiled=True),
    )
    rows_four = routed_rows.reshape(n_expert, local_experts, capacity, features)
    grads_four = routed_grads.reshape(n_expert, local_experts, capacity, features)
    total_rows = n_expert * local_experts * capacity
    pre_part = jnp.einsum("secd,edf->secf", rows_four, w_in, preferred_element_type=jnp.float32)
    back_part = jnp.einsum("secd,efd->secf", grads_four, w_out, preferred_element_type=jnp.float32)
    pre_flat = pre_part.reshape(total_rows, 2 * hidden_units)
    back_flat = back_part.reshape(total_rows, hidden_units)
    pre_share, back_share = (
        lax.psum_scatter(pre_flat, "dp", scatter_dimension=0, tiled=True),
        lax.psum_scatter(back_flat, "dp", scatter_dimension=0, tiled=True),
    )
    hidden_share, both_share = activate(pre_share, back_share)
    hidden, grad_both = (
        lax.all_gather(hidden_share, "dp", axis=0, tiled=True),
        lax.all_gather(both_share, "dp", axis=0, tiled=True),
    )
    hidden_four = hidden.reshape(n_expert, local_experts, capacity, hidden_units)
    both_four = grad_both.reshape(n_expert, local_experts, capacity, 2 * hidden_units)
    out_rows = jnp.einsum(
        "secf,efd->secd", hidden_four, w_out, preferred_element_type=jnp.float32
    ).astype(jnp.bfloat16)
    grad_rows = jnp.einsum(
        "secf,edf->secd", both_four, w_in, preferred_element_type=jnp.float32
    ).astype(jnp.bfloat16)
    grad_out = jnp.einsum(
        "secf,secd->efd", hidden_four, grads_four, preferred_element_type=jnp.float32
    ).astype(jnp.bfloat16)
    grad_in = jnp.einsum(
        "secd,secf->edf", rows_four, both_four, preferred_element_type=jnp.float32
    ).astype(jnp.bfloat16)
    home_out, home_grad = (
        lax.all_to_all(
            out_rows.reshape(n_expert, local_experts * capacity, features),
            "expert",
            split_axis=0,
            concat_axis=0,
            tiled=True,
        ),
        lax.all_to_all(
            grad_rows.reshape(n_expert, local_experts * capacity, features),
            "expert",
            split_axis=0,
            concat_axis=0,
            tiled=True,
        ),
    )
    route_out = jnp.dot(
        placing.T, home_out.reshape(slot_count, features), preferred_element_type=jnp.float32
    )
    route_out = route_out.reshape(tok_rows, top_count, features)
    mixed = jnp.sum(route_weight[:, :, None] * route_out, axis=1).astype(jnp.bfloat16)
    grad_tokens = jnp.dot(
        choose_token.T, home_grad.reshape(slot_count, features), preferred_element_type=jnp.float32
    )
    return (mixed, grad_tokens.astype(jnp.bfloat16), grad_in, grad_out)


def solution(mesh):
    placed = (
        P("expert", "dp"),
        P("expert", None),
        P("expert", None),
        P("expert", "dp"),
        P("expert", "dp", None),
        P("expert", None, "dp"),
    )
    sizes = dict(mesh.shape)
    chunked = sizes["dp"] == 4 and sizes["expert"] in (8, 16)
    return jax.shard_map(
        per_device_chunked if chunked else per_device,
        mesh=mesh,
        in_specs=placed,
        out_specs=(
            P("expert", "dp"),
            P("expert", "dp"),
            P("expert", "dp", None),
            P("expert", None, "dp"),
        ),
        check_vma=False,
    )
```

```python
import jax
import jax.numpy as jnp
from jax import lax
from jax.experimental import pallas as pl
from jax.experimental.pallas import tpu as pltpu
from jax.sharding import PartitionSpec as P

BF = jnp.bfloat16
F32 = jnp.float32
VMEM_LIMIT = 18 * 1024 * 1024
GRADS_LIMIT = 32 * 1024 * 1024
PREP_LIMIT = 60 * 1024 * 1024
COST = pl.CostEstimate(flops=1, bytes_accessed=1, transcendentals=0)
LONG = pl.CostEstimate(flops=2 * 10**10, bytes_accessed=1, transcendentals=0)


def dot(a, b):
    return lax.dot_general(a, b, (((1,), (0,)), ((), ())), preferred_element_type=F32)


def dot_t(a, b):
    return lax.dot_general(a, b, (((1,), (1,)), ((), ())), preferred_element_type=F32)


def t_dot(a, b):
    return lax.dot_general(a, b, (((0,), (0,)), ((), ())), preferred_element_type=F32)


def iota(shape, dim):
    return lax.broadcasted_iota(jnp.int32, shape, dim)


def padded(capacity):
    return -(-capacity // 16) * 16


def prep_kernel(capacity, ids, tokens, routes, weight, cotangent, *refs):
    outs, (token_rows, grad_rows, route_lines, weight_lines, sems) = refs[:-5], refs[-5:]
    pairs = ((routes, route_lines), (weight, weight_lines), (tokens, token_rows), (cotangent, grad_rows))
    copies = [pltpu.make_async_copy(x, held, sems.at[i]) for i, (x, held) in enumerate(pairs)]
    for copy in copies:
        copy.start()
    for copy in copies[:2]:
        copy.wait()
    routes, weight = route_lines, weight_lines
    count = len(outs)
    rows = routes.shape[1]
    expert = iota((count, rows), 0) ^ ids[0]
    named, w_named = None, None
    for k in range(routes.shape[0]):
        hit = routes[k : k + 1, :] == expert
        w_hit = jnp.where(hit, weight[k : k + 1, :], 0.0)
        named = hit if named is None else named | hit
        w_named = w_hit if w_named is None else w_named + w_hit
    before = (iota((rows, rows), 0) < iota((rows, rows), 1)).astype(F32).astype(BF)
    rank = dot(named.astype(F32).astype(BF), before).astype(jnp.int32)
    key = jnp.where(named, rank, -2 * capacity)
    slot = iota((2 * capacity, rows), 0)
    picks = []
    for s in range(count):
        row_key = key[s : s + 1, :]
        pick_token = (row_key == slot).astype(F32)
        pick_grad = (row_key + capacity == slot).astype(F32)
        scale = jnp.sum(pick_grad * w_named[s : s + 1, :], axis=1, keepdims=True)
        scale = scale + (slot[:, 0:1] < capacity).astype(F32)
        picks.append((pick_token.astype(BF), pick_grad.astype(BF), scale))
    for copy in copies[2:]:
        copy.wait()
    for out, (pick_token, pick_grad, scale) in zip(outs, picks):
        out[...] = (scale * (dot(pick_token, token_rows[...]) + dot(pick_grad, grad_rows[...]))).astype(BF)


def prep(ids, tokens, routes, weight, cotangent, count, capacity):
    rows, features = tokens.shape
    whole = pl.BlockSpec(memory_space=pltpu.VMEM)
    away = pl.BlockSpec(memory_space=pltpu.HBM)
    return pl.pallas_call(
        lambda *refs: prep_kernel(capacity, *refs),
        out_shape=[jax.ShapeDtypeStruct((2 * capacity, features), BF)] * count,
        in_specs=[pl.BlockSpec(memory_space=pltpu.SMEM)] + [away] * 4,
        out_specs=[whole] * count,
        scratch_shapes=[pltpu.VMEM((rows, features), BF)] * 2
        + [pltpu.VMEM(routes.T.shape, routes.dtype), pltpu.VMEM(weight.T.shape, weight.dtype)]
        + [pltpu.SemaphoreType.DMA((4,))],
        compiler_params=pltpu.CompilerParams(vmem_limit_bytes=PREP_LIMIT),
        cost_estimate=COST,
        name="prep",
    )(ids, tokens, routes.T, weight.T, cotangent)


def call(kernel, name, out_shapes, scalars, *arrays, cost=COST):
    whole = pl.BlockSpec(memory_space=pltpu.VMEM)
    return pl.pallas_call(
        kernel,
        out_shape=out_shapes,
        in_specs=[pl.BlockSpec(memory_space=pltpu.SMEM)] * len(scalars) + [whole] * len(arrays),
        out_specs=jax.tree.map(lambda _: whole, out_shapes),
        compiler_params=pltpu.CompilerParams(vmem_limit_bytes=VMEM_LIMIT),
        cost_estimate=cost,
        name=name,
    )(*scalars, *arrays)


def lay_out(capacity, blocks, row_out, grad_out):
    pad = padded(capacity)
    spot = iota((2 * pad, 2 * capacity), 0)
    col = iota((2 * pad, 2 * capacity), 1)
    target = jnp.where(col < capacity, col, col + pad - capacity)
    spread = (spot == target).astype(F32).astype(BF)
    for i, block in enumerate(blocks):
        laid = dot(spread, block[...]).astype(BF)
        row_out[i * pad : (i + 1) * pad, :] = laid[:pad]
        grad_out[i * pad : (i + 1) * pad, :] = laid[pad:]


def half_products(half, rows, grads, w_in, w_out, out):
    units = w_out.shape[0]
    width = units // 4
    for j in range(2):
        at = pl.multiple_of((half * 2 + j) * width, width)
        at_up = pl.multiple_of(units + (half * 2 + j) * width, width)
        gate = dot(rows[...], w_in[:, pl.ds(at, width)])
        up = dot(rows[...], w_in[:, pl.ds(at_up, width)])
        back = dot_t(grads[...], w_out[pl.ds(at, width), :])
        for part, term in enumerate((gate, up, back)):
            out[:, (3 * j + part) * width : (3 * j + part + 1) * width] = term.astype(out.dtype)


PIECES = 1


def weight_copies(halves, far_in, far_out, w_in, w_out, sems):
    units = far_out.shape[0]
    span, depth = units // 2, far_in.shape[0] // PIECES
    copies = []
    for half in halves:
        at = pl.ds(pl.multiple_of(half * span, span), span)
        at_up = pl.ds(pl.multiple_of(units + half * span, span), span)
        for k in range(PIECES):
            rows = slice(k * depth, (k + 1) * depth)
            step = span // PIECES
            row = pl.ds(pl.multiple_of(half * span + k * step, step), step)
            for x, y in (
                (far_in.at[rows, at], w_in.at[rows, at]),
                (far_in.at[rows, at_up], w_in.at[rows, at_up]),
                (far_out.at[row, :], w_out.at[row, :]),
            ):
                copies.append(pltpu.make_async_copy(x, y, sems.at[len(copies)]))
    for copy in copies:
        copy.start()
    return copies


def other_half(ids, blocks, w_in, w_out, capacity):
    units, features = w_out.shape
    rows = len(blocks) * padded(capacity)
    shape = jax.ShapeDtypeStruct
    whole = pl.BlockSpec(memory_space=pltpu.VMEM)
    away = pl.BlockSpec(memory_space=pl.ANY)

    def kernel(ids, *refs):
        held, (far_in, far_out, row_out, grad_out, send, near_in, near_out, sems) = refs[:-8], refs[-8:]
        copies = weight_copies((1 - ids[1], ids[1]), far_in, far_out, near_in, near_out, sems)
        lay_out(capacity, held, row_out, grad_out)
        for copy in copies[: 3 * PIECES]:
            copy.wait()
        half_products(1 - ids[1], row_out, grad_out, near_in, near_out, send)
        for copy in copies[3 * PIECES :]:
            copy.wait()

    return pl.pallas_call(
        kernel,
        out_shape=[
            shape((rows, features), BF),
            shape((rows, features), BF),
            shape((rows, 3 * units // 2), BF),
            shape(w_in.shape, BF),
            shape(w_out.shape, BF),
        ],
        in_specs=[pl.BlockSpec(memory_space=pltpu.SMEM)] + [whole] * len(blocks) + [away] * 2,
        out_specs=[whole] * 5,
        scratch_shapes=[pltpu.SemaphoreType.DMA((6 * PIECES,))],
        compiler_params=pltpu.CompilerParams(vmem_limit_bytes=VMEM_LIMIT),
        cost_estimate=COST,
        name="up",
    )(ids, *blocks, w_in, w_out)


def own_half(ids, rows, grads, weights):
    def kernel(ids, rows, grads, w_in, w_out, keep):
        half_products(ids[1], rows, grads, w_in, w_out, keep)

    shape = jax.ShapeDtypeStruct((rows.shape[0], 3 * weights[1].shape[0] // 2), F32)
    return call(kernel, "up", shape, [ids], rows, grads, *weights)


def up_step(ids, blocks, weights, capacity):
    units, features = weights[1].shape
    rows = len(blocks) * padded(capacity)
    shape = jax.ShapeDtypeStruct

    def kernel(ids, *refs):
        held, (w_in, w_out, row_out, grad_out, send, keep) = refs[:-6], refs[-6:]
        lay_out(capacity, held, row_out, grad_out)
        half_products(1 - ids[1], row_out, grad_out, w_in, w_out, send)
        half_products(ids[1], row_out, grad_out, w_in, w_out, keep)

    return call(
        kernel,
        "up",
        [
            shape((rows, features), BF),
            shape((rows, features), BF),
            shape((rows, 3 * units // 2), BF),
            shape((rows, 3 * units // 2), F32),
        ],
        [ids],
        *blocks,
        *weights,
        cost=LONG,
    )


def sum_kernel(keep, core, *outs):
    cut = keep.shape[1] // len(outs)
    for j, out in enumerate(outs):
        at = slice(j * cut, (j + 1) * cut)
        out[...] = (keep[:, at] + core[:, at].astype(F32)).astype(BF)


def sum_step(keep, core, cuts=1):
    shape = jax.ShapeDtypeStruct((keep.shape[0], keep.shape[1] // cuts), BF)
    return call(sum_kernel, "total", [shape] * cuts, [], keep, core)


def activated(keep, core, others, out):
    width = keep.shape[1] // 6
    for j in range(2):
        base = 3 * width * j
        other, skip = others[j % len(others)], base * (len(others) - 1)
        gate, up, back = (
            keep[:, at : at + width]
            + core[:, at : at + width].astype(F32)
            + other[:, at - skip : at - skip + width].astype(F32)
            for at in (base, base + width, base + 2 * width)
        )
        sigmoid = jax.nn.sigmoid(gate)
        silu = gate * sigmoid
        out[:, base : base + width] = (silu * up).astype(BF)
        out[:, base + width : base + 2 * width] = (
            back * up * sigmoid * (1.0 + gate * (1.0 - sigmoid))
        ).astype(BF)
        out[:, base + 2 * width : base + 3 * width] = (back * silu).astype(BF)


def act_step(keep, core, others):
    def kernel(keep, core, *refs):
        activated(keep, core, refs[:-1], refs[-1])

    return call(kernel, "act", jax.ShapeDtypeStruct(keep.shape, BF), [], keep, core, *others)


def act_and_sum(keep, core, other, next_keep, next_core):
    def kernel(keep, core, other, next_keep, next_core, out, total):
        activated(keep, core, [other], out)
        sum_kernel(next_keep, next_core, total)

    shapes = [jax.ShapeDtypeStruct(x.shape, BF) for x in (keep, next_keep)]
    return call(kernel, "act", shapes, [], keep, core, other, next_keep, next_core)


def half_rows(half, held, w_in, w_out):
    units = w_out.shape[0]
    width = units // 4
    out_rows = grad_rows = None
    for j in range(2):
        base = 3 * width * j
        at = pl.multiple_of((half * 2 + j) * width, width)
        at_up = pl.multiple_of(units + (half * 2 + j) * width, width)
        a = dot(held[:, base : base + width], w_out[pl.ds(at, width), :])
        b = dot_t(held[:, base + width : base + 2 * width], w_in[:, pl.ds(at, width)])
        c = dot_t(held[:, base + 2 * width : base + 3 * width], w_in[:, pl.ds(at_up, width)])
        out_rows = a if out_rows is None else out_rows + a
        grad_rows = b + c if grad_rows is None else grad_rows + (b + c)
    return out_rows, grad_rows


def pack(capacity, out_rows, grad_rows, outs):
    pad = padded(capacity)
    spot = iota((2 * capacity, pad), 0)
    col = iota((2 * capacity, pad), 1)
    pack_out = (spot == jnp.where(col < capacity, col, -1)).astype(F32).astype(BF)
    pack_grad = (spot - capacity == jnp.where(col < capacity, col, -capacity - 1)).astype(F32).astype(BF)
    out_rows, grad_rows = out_rows.astype(BF), grad_rows.astype(BF)
    sources = out_rows.shape[0] // pad
    cuts = len(outs) // sources
    for i in range(sources):
        at = slice(i * pad, (i + 1) * pad)
        packed = (dot(pack_out, out_rows[at]) + dot(pack_grad, grad_rows[at])).astype(BF)
        cut = packed.shape[1] // cuts
        for j in range(cuts):
            outs[i * cuts + j][...] = packed[:, j * cut : (j + 1) * cut]


def down_step(ids, own, core, weights, count, capacity):
    def kernel(ids, own, core, w_in, w_out, *outs):
        out_rows, grad_rows = half_rows(ids[1], own, w_in, w_out)
        more_out, more_grad = half_rows(1 - ids[1], core, w_in, w_out)
        pack(capacity, out_rows + more_out, grad_rows + more_grad, outs)

    shape = jax.ShapeDtypeStruct((2 * capacity, weights[1].shape[1]), BF)
    return [[x] for x in call(kernel, "down", [shape] * count, [ids], own, core, *weights)]


def down_own(ids, own, weights):
    def kernel(ids, own, w_in, w_out, out_rows, grad_rows):
        out_rows[...], grad_rows[...] = half_rows(ids[1], own, w_in, w_out)

    shape = jax.ShapeDtypeStruct((own.shape[0], weights[1].shape[1]), F32)
    return call(kernel, "down", [shape] * 2, [ids], own, *weights)


def down_own_alone(ids, own, w_in, w_out):
    shape = jax.ShapeDtypeStruct
    whole = pl.BlockSpec(memory_space=pltpu.VMEM)
    away = pl.BlockSpec(memory_space=pl.ANY)

    def kernel(ids, own, far_in, far_out, out_rows, grad_rows, near_in, near_out, sems):
        copies = weight_copies((ids[1], 1 - ids[1]), far_in, far_out, near_in, near_out, sems)
        for copy in copies[: 3 * PIECES]:
            copy.wait()
        out_rows[...], grad_rows[...] = half_rows(ids[1], own, near_in, near_out)
        for copy in copies[3 * PIECES :]:
            copy.wait()

    sums = shape((own.shape[0], w_out.shape[1]), F32)
    return pl.pallas_call(
        kernel,
        out_shape=[sums, sums, shape(w_in.shape, BF), shape(w_out.shape, BF)],
        in_specs=[pl.BlockSpec(memory_space=pltpu.SMEM), whole] + [away] * 2,
        out_specs=[whole] * 4,
        scratch_shapes=[pltpu.SemaphoreType.DMA((6 * PIECES,))],
        compiler_params=pltpu.CompilerParams(vmem_limit_bytes=VMEM_LIMIT),
        cost_estimate=COST,
        name="down",
    )(ids, own, w_in, w_out)


def down_other(ids, out_rows, grad_rows, core, weights, count, capacity, cuts=1):
    def kernel(ids, out_rows, grad_rows, core, w_in, w_out, *outs):
        more_out, more_grad = half_rows(1 - ids[1], core, w_in, w_out)
        pack(capacity, out_rows[...] + more_out, grad_rows[...] + more_grad, outs)

    shape = jax.ShapeDtypeStruct((2 * capacity, weights[1].shape[1] // cuts), BF)
    outs = call(kernel, "down", [shape] * (count * cuts), [ids], out_rows, grad_rows, core, *weights)
    return [outs[i * cuts : (i + 1) * cuts] for i in range(count)]


def grads_kernel(count, ids, *refs):
    groups = [refs[4 * i : 4 * i + 4] for i in range(count)]
    grad_in, grad_out, rows, grads, own, core, tiles_in, tiles_out, sems = refs[4 * count :]
    at = 0
    for group in groups:
        n = group[0].shape[0]
        for held, part in zip((rows, grads, own, core), group):
            held[at : at + n, :] = part[...]
        at += n
    features, units = rows.shape[1], grad_out.shape[0]
    f_tile, width = features // 4, units // 4
    copies = []
    for j in range(4):
        turned = rows[:, j * f_tile : (j + 1) * f_tile].T
        for held, half in ((own, ids[1]), (core, 1 - ids[1])):
            for i in range(2):
                both = dot(turned, held[:, (3 * i + 1) * width : (3 * i + 3) * width]).astype(BF)
                for part in range(2):
                    to = pl.multiple_of(part * units + (half * 2 + i) * width, width)
                    tiles_in[j, :, pl.ds(to, width)] = both[:, part * width : (part + 1) * width]
        copies.append(pltpu.make_async_copy(tiles_in.at[j], grad_in.at[j * f_tile : (j + 1) * f_tile, :], sems.at[j]))
        copies[-1].start()
    for j, (held, half) in enumerate(((own, ids[1]), (core, 1 - ids[1]))):
        for i in range(2):
            turned = held[:, 3 * i * width : (3 * i + 1) * width].T
            tiles_out[2 * j + i] = dot(turned, grads[...]).astype(BF)
            to = pl.multiple_of((half * 2 + i) * width, width)
            copies.append(pltpu.make_async_copy(tiles_out.at[2 * j + i], grad_out.at[pl.ds(to, width), :], sems.at[4 + 2 * j + i]))
            copies[-1].start()
    for copy in copies:
        copy.wait()


def grads_step(ids, groups, units):
    features = groups[0][0].shape[1]
    rows = sum(group[0].shape[0] for group in groups)
    whole = pl.BlockSpec(memory_space=pltpu.VMEM)
    arrays = [x for group in groups for x in group]
    return pl.pallas_call(
        lambda *refs: grads_kernel(len(groups), *refs),
        out_shape=[
            jax.ShapeDtypeStruct((features, 2 * units), BF),
            jax.ShapeDtypeStruct((units, features), BF),
        ],
        in_specs=[pl.BlockSpec(memory_space=pltpu.SMEM)] + [whole] * len(arrays),
        out_specs=[pl.BlockSpec(memory_space=pltpu.HBM)] * 2,
        scratch_shapes=[
            pltpu.VMEM((rows, features), BF),
            pltpu.VMEM((rows, features), BF),
            pltpu.VMEM((rows, units * 3 // 2), BF),
            pltpu.VMEM((rows, units * 3 // 2), BF),
            pltpu.VMEM((4, features // 4, 2 * units), BF),
            pltpu.VMEM((4, units // 4, features), BF),
            pltpu.SemaphoreType.DMA((8,)),
        ],
        compiler_params=pltpu.CompilerParams(vmem_limit_bytes=GRADS_LIMIT),
        cost_estimate=COST,
        name="grads",
    )(ids, *arrays)


def final_kernel(capacity, sources, parts, ids, routes, weight, *refs):
    taken, cuts = sum(parts), max(parts)
    partial, (mixed, grad_tokens) = refs[taken:-2], refs[-2:]
    homes = [refs[sum(parts[:i]) : sum(parts[: i + 1])] for i in range(len(parts))]
    rows = routes.shape[1]
    me = ids[0]
    count = len(sources)
    eye = iota((rows, rows), 0) == iota((rows, rows), 1)

    def column(line, zero):
        return jnp.sum(jnp.where(eye, line, zero), axis=1, keepdims=True)

    lane = iota((rows, count), 1)
    expert = lane * 0
    for i, s in enumerate(sources):
        expert = jnp.where(lane == i, s, expert)
    expert = expert ^ me
    named, w_named = None, None
    for k in range(routes.shape[0]):
        hit = column(routes[k : k + 1, :], 0) == expert
        w_hit = jnp.where(hit, column(weight[k : k + 1, :], 0.0), 0.0)
        named = hit if named is None else named | hit
        w_named = w_hit if w_named is None else w_named + w_hit
    before = (iota((rows, rows), 1) < iota((rows, rows), 0)).astype(BF)
    rank = dot(before, named.astype(F32).astype(BF)).astype(jnp.int32)
    key = jnp.where(named, rank, -2 * capacity)
    slot = iota((rows, 2 * capacity), 1)
    width = mixed.shape[1] // cuts
    for j in range(cuts):
        at = slice(j * width, (j + 1) * width)
        total_out, total_grad = (p[:, at] for p in partial) if partial else (None, None)
        for i in range(count):
            home = homes[i][j][...] if len(homes[i]) == cuts else homes[i][0][:, at]
            row_key = key[:, i : i + 1]
            pick_out = (row_key == slot).astype(F32).astype(BF)
            pick_grad = (row_key + capacity == slot).astype(F32).astype(BF)
            out = w_named[:, i : i + 1] * dot(pick_out, home)
            grad = dot(pick_grad, home)
            total_out = out if total_out is None else total_out + out
            total_grad = grad if total_grad is None else total_grad + grad
        mixed[:, at] = total_out.astype(mixed.dtype)
        grad_tokens[:, at] = total_grad.astype(mixed.dtype)


def final(ids, routes, weight, homes, sources, capacity, partial, dtype):
    parts = [len(home) for home in homes]
    shape = (routes.shape[0], homes[0][0].shape[1] * parts[0])
    return call(
        lambda *refs: final_kernel(capacity, sources, parts, *refs),
        "final",
        [jax.ShapeDtypeStruct(shape, dtype)] * 2,
        [ids],
        routes.T,
        weight.T,
        *[x for home in homes for x in home],
        *partial,
    )


def per_device_chunked(tokens, routes, route_weight, cotangent, w_in, w_out):
    tok_rows = tokens.shape[0]
    top_count = routes.shape[1]
    n_expert = lax.axis_size("expert")
    n_dp = lax.axis_size("dp")
    capacity = tok_rows * top_count * 5 // (4 * n_expert)
    w_in, w_out = w_in[0], w_out[0]
    units = w_out.shape[0]
    ids = jnp.stack([lax.axis_index("expert"), lax.axis_index("dp") % 2]).astype(jnp.int32)

    def across(x, s):
        return lax.ppermute(x, "expert", [(i, i ^ s) for i in range(n_expert)]) if s else x

    def beside(x, s):
        return lax.ppermute(x, "dp", [(i, i ^ s) for i in range(n_dp)])

    def after(x, *earlier):
        return lax.optimization_barrier((x, *earlier))[0]

    def after(x, *earlier):
        return lax.optimization_barrier((x, *earlier))[0]

    inside = lax.axis_index("expert") >= 0

    def stage(body, *args):
        shapes = jax.eval_shape(body, *args)
        return lax.cond(inside, body, lambda *_: jax.tree.map(lambda x: jnp.zeros(x.shape, x.dtype), shapes), *args)

    def up_part(blocks, weights, *earlier):
        first, *others = blocks
        return up_step(ids, [after(first, *earlier), *others], weights, capacity)

    def core_part(state, *earlier):
        rows, grads, send, keep = state
        return rows, grads, keep, beside(after(send, *earlier) if earlier else send, 1)

    def up_in_halves(blocks):
        rows, grads, send, *weights = other_half(ids, blocks, w_in, w_out, capacity)
        core = beside(send, 1)
        return (rows, grads, own_half(ids, after(rows, send), grads, weights), core), weights

    def sum_part(state, *earlier, cuts=1):
        rows, grads, keep, core = state
        return rows, grads, keep, core, sum_step(after(keep, *earlier), core, cuts)

    def x_part(state):
        rows, grads, keep, core, totals = state
        return rows, grads, keep, core, [beside(total, 2) for total in totals]

    def act_part(state, *earlier):
        rows, grads, keep, core, others = state
        own = act_step(after(keep, *earlier), core, others)
        return rows, grads, own, beside(own, 1)

    def down_part(group, weights, count):
        return down_step(ids, *group[2:], weights, count, capacity)

    def down_in_halves(group, weights, count):
        _, _, own, core = group
        sums = down_own(ids, own, weights)
        return down_other(ids, *sums, after(core, *sums), weights, count, capacity)

    def act_both(state, next_state, *earlier):
        rows, grads, keep, core, (other,) = state
        own, next_total = act_and_sum(after(keep, *earlier), core, other, *next_state[2:])
        return (rows, grads, own, beside(own, 1)), (*next_state, [next_total])

    def first_stage(blocks):
        state, _ = up_in_halves(blocks)
        return sum_part(state, cuts=2)

    def far_stage(blocks, before, before_count, next_blocks):
        state, held = up_in_halves(blocks)
        state = sum_part(state)
        before = act_part(before, *state[4])
        next_state = up_part(next_blocks, held, before[2])
        back = down_part((*before[:2], after(before[2], next_state[2]), before[3]), held, before_count)
        ends = [x for parts in back for x in parts]
        group, next_state = act_both(x_part(state), core_part(next_state, *ends), *ends)
        return group, down_in_halves(group, held, len(blocks)), next_state, before, back

    def rest_stage(state):
        group = act_part(state)
        _, _, own, core = group
        *sums, held_in, held_out = down_own_alone(ids, own, w_in, w_out)
        return group, down_other(ids, *sums, after(core, *sums), (held_in, held_out), size, capacity, 2)

    half, quarter = n_expert // 2, n_expert // 4
    size = quarter // 2
    near = [list(range(quarter)), list(range(quarter, quarter + size)), list(range(quarter + size, half))]
    far, last = list(range(half, half + quarter)), list(range(half + quarter, n_expert))
    sent = prep(ids, tokens, routes, route_weight, cotangent, n_expert, capacity)
    came, home = {0: sent[0]}, {}

    def blocks(sources, *earlier):
        first, *others = [came[s] for s in sources]
        return [after(first, *earlier), *others]

    def start(sources, *earlier):
        came.update({s: across(after(sent[s], *earlier) if earlier else sent[s], s) for s in sources if s})

    def start_back(sources, back, *earlier):
        for s, parts in zip(sources, back):
            home[s] = [across(after(x, *earlier) if earlier else x, s) for x in parts]

    def arrived(sources):
        return [x for s in sources for x in home[s]]

    start(far + near[0] + near[1])
    state_0 = stage(first_stage, blocks(near[0]))
    start(last, *blocks(far + near[1]), *state_0[4])
    state_0 = x_part(state_0)
    start(near[2], *blocks(far), *state_0[4])
    group_far, back_far, state_1, group_0, back_0 = stage(
        lambda a, b, c: far_stage(a, b, quarter, c), blocks(far), state_0, blocks(near[1])
    )
    start_back(far + near[0], back_far + back_0, *blocks(last))
    group_last, back_last, state_2, group_1, back_1 = stage(
        lambda a, b, c: far_stage(a, b, size, c), blocks(last, group_far[3]), x_part(state_1), blocks(near[2])
    )
    start_back(last, back_last, *arrived(far + near[0]))
    start_back(near[1], back_1)
    group_2, back_2 = stage(rest_stage, x_part(state_2))
    start_back(near[2], back_2)

    def add(sources, partial, dtype):
        return final(ids, routes, route_weight, [home[s] for s in sources], sources, capacity, partial, dtype)

    groups = [group_0, group_far, group_1, group_last, group_2]
    grad_in, grad_out = grads_step(ids, groups, units)
    partial = add(near[0] + far, [], F32)
    partial = add(last, partial, F32)
    mixed, grad_tokens = add(near[1] + near[2], partial, BF)
    return mixed, grad_tokens, grad_in[None], grad_out[None]


def activate(pre_act, grad_hidden):
    units = pre_act.shape[1] // 2
    gate_part = pre_act[:, :units]
    up_part = pre_act[:, units:]
    sigmoid_gate = jax.nn.sigmoid(gate_part)
    silu_gate = gate_part * sigmoid_gate
    hidden = (silu_gate * up_part).astype(jnp.bfloat16)
    grad_gate = grad_hidden * up_part * sigmoid_gate * (1.0 + gate_part * (1.0 - sigmoid_gate))
    grad_up = grad_hidden * silu_gate
    return (hidden, jnp.concatenate([grad_gate, grad_up], axis=1).astype(jnp.bfloat16))


def per_device(tokens, routes, route_weight, cotangent, w_in, w_out):
    tok_rows, features = tokens.shape
    top_count = routes.shape[1]
    n_expert = lax.axis_size("expert")
    local_experts = w_in.shape[0]
    hidden_units = w_out.shape[1]
    experts = n_expert * local_experts
    capacity = tok_rows * top_count * 5 // (4 * experts)
    slot_count = experts * capacity
    flat_routes = routes.reshape(-1)
    onehot = (flat_routes[:, None] == jnp.arange(experts, dtype=jnp.int32)[None, :]).astype(
        jnp.int32
    )
    slot_rank = jnp.sum((jnp.cumsum(onehot, axis=0) - onehot) * onehot, axis=1)
    target = flat_routes * capacity + slot_rank
    placing = (target[None, :] == jnp.arange(slot_count, dtype=jnp.int32)[:, None]).astype(
        jnp.bfloat16
    )
    choose_token = jnp.sum(placing.reshape(slot_count, tok_rows, top_count), axis=2)
    scaled_grads = (route_weight[:, :, None] * cotangent[:, None, :].astype(jnp.float32)).astype(
        jnp.bfloat16
    )
    scaled_grads = scaled_grads.reshape(tok_rows * top_count, features)
    send_rows = jnp.dot(choose_token, tokens, preferred_element_type=jnp.float32).astype(
        jnp.bfloat16
    )
    send_grads = jnp.dot(placing, scaled_grads, preferred_element_type=jnp.float32).astype(
        jnp.bfloat16
    )
    send_rows = send_rows.reshape(n_expert, local_experts * capacity, features)
    send_grads = send_grads.reshape(n_expert, local_experts * capacity, features)
    routed_rows, routed_grads = (
        lax.all_to_all(send_rows, "expert", split_axis=0, concat_axis=0, tiled=True),
        lax.all_to_all(send_grads, "expert", split_axis=0, concat_axis=0, tiled=True),
    )
    rows_four = routed_rows.reshape(n_expert, local_experts, capacity, features)
    grads_four = routed_grads.reshape(n_expert, local_experts, capacity, features)
    total_rows = n_expert * local_experts * capacity
    pre_part = jnp.einsum("secd,edf->secf", rows_four, w_in, preferred_element_type=jnp.float32)
    back_part = jnp.einsum("secd,efd->secf", grads_four, w_out, preferred_element_type=jnp.float32)
    pre_flat = pre_part.reshape(total_rows, 2 * hidden_units)
    back_flat = back_part.reshape(total_rows, hidden_units)
    pre_share, back_share = (
        lax.psum_scatter(pre_flat, "dp", scatter_dimension=0, tiled=True),
        lax.psum_scatter(back_flat, "dp", scatter_dimension=0, tiled=True),
    )
    hidden_share, both_share = activate(pre_share, back_share)
    hidden, grad_both = (
        lax.all_gather(hidden_share, "dp", axis=0, tiled=True),
        lax.all_gather(both_share, "dp", axis=0, tiled=True),
    )
    hidden_four = hidden.reshape(n_expert, local_experts, capacity, hidden_units)
    both_four = grad_both.reshape(n_expert, local_experts, capacity, 2 * hidden_units)
    out_rows = jnp.einsum(
        "secf,efd->secd", hidden_four, w_out, preferred_element_type=jnp.float32
    ).astype(jnp.bfloat16)
    grad_rows = jnp.einsum(
        "secf,edf->secd", both_four, w_in, preferred_element_type=jnp.float32
    ).astype(jnp.bfloat16)
    grad_out = jnp.einsum(
        "secf,secd->efd", hidden_four, grads_four, preferred_element_type=jnp.float32
    ).astype(jnp.bfloat16)
    grad_in = jnp.einsum(
        "secd,secf->edf", rows_four, both_four, preferred_element_type=jnp.float32
    ).astype(jnp.bfloat16)
    home_out, home_grad = (
        lax.all_to_all(
            out_rows.reshape(n_expert, local_experts * capacity, features),
            "expert",
            split_axis=0,
            concat_axis=0,
            tiled=True,
        ),
        lax.all_to_all(
            grad_rows.reshape(n_expert, local_experts * capacity, features),
            "expert",
            split_axis=0,
            concat_axis=0,
            tiled=True,
        ),
    )
    route_out = jnp.dot(
        placing.T, home_out.reshape(slot_count, features), preferred_element_type=jnp.float32
    )
    route_out = route_out.reshape(tok_rows, top_count, features)
    mixed = jnp.sum(route_weight[:, :, None] * route_out, axis=1).astype(jnp.bfloat16)
    grad_tokens = jnp.dot(
        choose_token.T, home_grad.reshape(slot_count, features), preferred_element_type=jnp.float32
    )
    return (mixed, grad_tokens.astype(jnp.bfloat16), grad_in, grad_out)


def solution(mesh):
    placed = (
        P("expert", "dp"),
        P("expert", None),
        P("expert", None),
        P("expert", "dp"),
        P("expert", "dp", None),
        P("expert", None, "dp"),
    )
    sizes = dict(mesh.shape)
    chunked = sizes["dp"] == 4 and sizes["expert"] in (8, 16)
    return jax.shard_map(
        per_device_chunked if chunked else per_device,
        mesh=mesh,
        in_specs=placed,
        out_specs=(
            P("expert", "dp"),
            P("expert", "dp"),
            P("expert", "dp", None),
            P("expert", None, "dp"),
        ),
        check_vma=False,
    )
```

```python
import jax
import jax.numpy as jnp
from jax import lax
from jax.experimental import pallas as pl
from jax.experimental.pallas import tpu as pltpu
from jax.sharding import PartitionSpec as P

BF = jnp.bfloat16
F32 = jnp.float32
VMEM_LIMIT = 18 * 1024 * 1024
GRADS_LIMIT = 32 * 1024 * 1024
PREP_LIMIT = 60 * 1024 * 1024
COST = pl.CostEstimate(flops=1, bytes_accessed=1, transcendentals=0)
LONG = pl.CostEstimate(flops=2 * 10**10, bytes_accessed=1, transcendentals=0)


def dot(a, b):
    return lax.dot_general(a, b, (((1,), (0,)), ((), ())), preferred_element_type=F32)


def dot_t(a, b):
    return lax.dot_general(a, b, (((1,), (1,)), ((), ())), preferred_element_type=F32)


def t_dot(a, b):
    return lax.dot_general(a, b, (((0,), (0,)), ((), ())), preferred_element_type=F32)


def iota(shape, dim):
    return lax.broadcasted_iota(jnp.int32, shape, dim)


def padded(capacity):
    return -(-capacity // 16) * 16


def prep_kernel(capacity, ids, tokens, routes, weight, cotangent, *refs):
    outs, (token_rows, grad_rows, route_lines, weight_lines, sems) = refs[:-5], refs[-5:]
    pairs = ((routes, route_lines), (weight, weight_lines), (tokens, token_rows), (cotangent, grad_rows))
    copies = [pltpu.make_async_copy(x, held, sems.at[i]) for i, (x, held) in enumerate(pairs)]
    for copy in copies:
        copy.start()
    for copy in copies[:2]:
        copy.wait()
    routes, weight = route_lines, weight_lines
    count = len(outs)
    rows = routes.shape[1]
    expert = iota((count, rows), 0) ^ ids[0]
    named, w_named = None, None
    for k in range(routes.shape[0]):
        hit = routes[k : k + 1, :] == expert
        w_hit = jnp.where(hit, weight[k : k + 1, :], 0.0)
        named = hit if named is None else named | hit
        w_named = w_hit if w_named is None else w_named + w_hit
    before = (iota((rows, rows), 0) < iota((rows, rows), 1)).astype(F32).astype(BF)
    rank = dot(named.astype(F32).astype(BF), before).astype(jnp.int32)
    key = jnp.where(named, rank, -2 * capacity)
    slot = iota((2 * capacity, rows), 0)
    picks = []
    for s in range(count):
        row_key = key[s : s + 1, :]
        pick_token = (row_key == slot).astype(F32)
        pick_grad = (row_key + capacity == slot).astype(F32)
        scale = jnp.sum(pick_grad * w_named[s : s + 1, :], axis=1, keepdims=True)
        scale = scale + (slot[:, 0:1] < capacity).astype(F32)
        picks.append((pick_token.astype(BF), pick_grad.astype(BF), scale))
    for copy in copies[2:]:
        copy.wait()
    for out, (pick_token, pick_grad, scale) in zip(outs, picks):
        out[...] = (scale * (dot(pick_token, token_rows[...]) + dot(pick_grad, grad_rows[...]))).astype(BF)


def prep(ids, tokens, routes, weight, cotangent, count, capacity):
    rows, features = tokens.shape
    whole = pl.BlockSpec(memory_space=pltpu.VMEM)
    away = pl.BlockSpec(memory_space=pltpu.HBM)
    return pl.pallas_call(
        lambda *refs: prep_kernel(capacity, *refs),
        out_shape=[jax.ShapeDtypeStruct((2 * capacity, features), BF)] * count,
        in_specs=[pl.BlockSpec(memory_space=pltpu.SMEM)] + [away] * 4,
        out_specs=[whole] * count,
        scratch_shapes=[pltpu.VMEM((rows, features), BF)] * 2
        + [pltpu.VMEM(routes.T.shape, routes.dtype), pltpu.VMEM(weight.T.shape, weight.dtype)]
        + [pltpu.SemaphoreType.DMA((4,))],
        compiler_params=pltpu.CompilerParams(vmem_limit_bytes=PREP_LIMIT),
        cost_estimate=COST,
        name="prep",
    )(ids, tokens, routes.T, weight.T, cotangent)


def call(kernel, name, out_shapes, scalars, *arrays, cost=COST):
    whole = pl.BlockSpec(memory_space=pltpu.VMEM)
    return pl.pallas_call(
        kernel,
        out_shape=out_shapes,
        in_specs=[pl.BlockSpec(memory_space=pltpu.SMEM)] * len(scalars) + [whole] * len(arrays),
        out_specs=jax.tree.map(lambda _: whole, out_shapes),
        compiler_params=pltpu.CompilerParams(vmem_limit_bytes=VMEM_LIMIT),
        cost_estimate=cost,
        name=name,
    )(*scalars, *arrays)


def lay_out(capacity, blocks, row_out, grad_out):
    pad = padded(capacity)
    spot = iota((2 * pad, 2 * capacity), 0)
    col = iota((2 * pad, 2 * capacity), 1)
    target = jnp.where(col < capacity, col, col + pad - capacity)
    spread = (spot == target).astype(F32).astype(BF)
    for i, block in enumerate(blocks):
        laid = dot(spread, block[...]).astype(BF)
        row_out[i * pad : (i + 1) * pad, :] = laid[:pad]
        grad_out[i * pad : (i + 1) * pad, :] = laid[pad:]


def half_products(half, rows, grads, w_in, w_out, out):
    units = w_out.shape[0]
    width = units // 4
    for j in range(2):
        at = pl.multiple_of((half * 2 + j) * width, width)
        at_up = pl.multiple_of(units + (half * 2 + j) * width, width)
        gate = dot(rows[...], w_in[:, pl.ds(at, width)])
        up = dot(rows[...], w_in[:, pl.ds(at_up, width)])
        back = dot_t(grads[...], w_out[pl.ds(at, width), :])
        for part, term in enumerate((gate, up, back)):
            out[:, (3 * j + part) * width : (3 * j + part + 1) * width] = term.astype(out.dtype)


PIECES = 1


def weight_copies(halves, far_in, far_out, w_in, w_out, sems):
    units = far_out.shape[0]
    span, depth = units // 2, far_in.shape[0] // PIECES
    copies = []
    for half in halves:
        at = pl.ds(pl.multiple_of(half * span, span), span)
        at_up = pl.ds(pl.multiple_of(units + half * span, span), span)
        for k in range(PIECES):
            rows = slice(k * depth, (k + 1) * depth)
            step = span // PIECES
            row = pl.ds(pl.multiple_of(half * span + k * step, step), step)
            for x, y in (
                (far_in.at[rows, at], w_in.at[rows, at]),
                (far_in.at[rows, at_up], w_in.at[rows, at_up]),
                (far_out.at[row, :], w_out.at[row, :]),
            ):
                copies.append(pltpu.make_async_copy(x, y, sems.at[len(copies)]))
    for copy in copies:
        copy.start()
    return copies


def other_half(ids, blocks, w_in, w_out, capacity):
    units, features = w_out.shape
    rows = len(blocks) * padded(capacity)
    shape = jax.ShapeDtypeStruct
    whole = pl.BlockSpec(memory_space=pltpu.VMEM)
    away = pl.BlockSpec(memory_space=pl.ANY)

    def kernel(ids, *refs):
        held, (far_in, far_out, row_out, grad_out, send, near_in, near_out, sems) = refs[:-8], refs[-8:]
        copies = weight_copies((1 - ids[1], ids[1]), far_in, far_out, near_in, near_out, sems)
        lay_out(capacity, held, row_out, grad_out)
        for copy in copies[: 3 * PIECES]:
            copy.wait()
        half_products(1 - ids[1], row_out, grad_out, near_in, near_out, send)
        for copy in copies[3 * PIECES :]:
            copy.wait()

    return pl.pallas_call(
        kernel,
        out_shape=[
            shape((rows, features), BF),
            shape((rows, features), BF),
            shape((rows, 3 * units // 2), BF),
            shape(w_in.shape, BF),
            shape(w_out.shape, BF),
        ],
        in_specs=[pl.BlockSpec(memory_space=pltpu.SMEM)] + [whole] * len(blocks) + [away] * 2,
        out_specs=[whole] * 5,
        scratch_shapes=[pltpu.SemaphoreType.DMA((6 * PIECES,))],
        compiler_params=pltpu.CompilerParams(vmem_limit_bytes=VMEM_LIMIT),
        cost_estimate=COST,
        name="up",
    )(ids, *blocks, w_in, w_out)


def own_half(ids, rows, grads, weights):
    def kernel(ids, rows, grads, w_in, w_out, keep):
        half_products(ids[1], rows, grads, w_in, w_out, keep)

    shape = jax.ShapeDtypeStruct((rows.shape[0], 3 * weights[1].shape[0] // 2), F32)
    return call(kernel, "up", shape, [ids], rows, grads, *weights)


def up_step(ids, blocks, weights, capacity):
    units, features = weights[1].shape
    rows = len(blocks) * padded(capacity)
    shape = jax.ShapeDtypeStruct

    def kernel(ids, *refs):
        held, (w_in, w_out, row_out, grad_out, send, keep) = refs[:-6], refs[-6:]
        lay_out(capacity, held, row_out, grad_out)
        half_products(1 - ids[1], row_out, grad_out, w_in, w_out, send)
        half_products(ids[1], row_out, grad_out, w_in, w_out, keep)

    return call(
        kernel,
        "up",
        [
            shape((rows, features), BF),
            shape((rows, features), BF),
            shape((rows, 3 * units // 2), BF),
            shape((rows, 3 * units // 2), F32),
        ],
        [ids],
        *blocks,
        *weights,
        cost=LONG,
    )


def sum_kernel(keep, core, *outs):
    cut = keep.shape[1] // len(outs)
    for j, out in enumerate(outs):
        at = slice(j * cut, (j + 1) * cut)
        out[...] = (keep[:, at] + core[:, at].astype(F32)).astype(BF)


def sum_step(keep, core, cuts=1):
    shape = jax.ShapeDtypeStruct((keep.shape[0], keep.shape[1] // cuts), BF)
    return call(sum_kernel, "total", [shape] * cuts, [], keep, core)


def activated(keep, core, others, out):
    width = keep.shape[1] // 6
    for j in range(2):
        base = 3 * width * j
        other, skip = others[j % len(others)], base * (len(others) - 1)
        gate, up, back = (
            keep[:, at : at + width]
            + core[:, at : at + width].astype(F32)
            + other[:, at - skip : at - skip + width].astype(F32)
            for at in (base, base + width, base + 2 * width)
        )
        sigmoid = jax.nn.sigmoid(gate)
        silu = gate * sigmoid
        out[:, base : base + width] = (silu * up).astype(BF)
        out[:, base + width : base + 2 * width] = (
            back * up * sigmoid * (1.0 + gate * (1.0 - sigmoid))
        ).astype(BF)
        out[:, base + 2 * width : base + 3 * width] = (back * silu).astype(BF)


def act_step(keep, core, others):
    def kernel(keep, core, *refs):
        activated(keep, core, refs[:-1], refs[-1])

    return call(kernel, "act", jax.ShapeDtypeStruct(keep.shape, BF), [], keep, core, *others)


def act_and_sum(keep, core, other, next_keep, next_core):
    def kernel(keep, core, other, next_keep, next_core, out, total):
        activated(keep, core, [other], out)
        sum_kernel(next_keep, next_core, total)

    shapes = [jax.ShapeDtypeStruct(x.shape, BF) for x in (keep, next_keep)]
    return call(kernel, "act", shapes, [], keep, core, other, next_keep, next_core)


def half_rows(half, held, w_in, w_out):
    units = w_out.shape[0]
    width = units // 4
    out_rows = grad_rows = None
    for j in range(2):
        base = 3 * width * j
        at = pl.multiple_of((half * 2 + j) * width, width)
        at_up = pl.multiple_of(units + (half * 2 + j) * width, width)
        a = dot(held[:, base : base + width], w_out[pl.ds(at, width), :])
        b = dot_t(held[:, base + width : base + 2 * width], w_in[:, pl.ds(at, width)])
        c = dot_t(held[:, base + 2 * width : base + 3 * width], w_in[:, pl.ds(at_up, width)])
        out_rows = a if out_rows is None else out_rows + a
        grad_rows = b + c if grad_rows is None else grad_rows + (b + c)
    return out_rows, grad_rows


def pack(capacity, out_rows, grad_rows, outs):
    pad = padded(capacity)
    spot = iota((2 * capacity, pad), 0)
    col = iota((2 * capacity, pad), 1)
    pack_out = (spot == jnp.where(col < capacity, col, -1)).astype(F32).astype(BF)
    pack_grad = (spot - capacity == jnp.where(col < capacity, col, -capacity - 1)).astype(F32).astype(BF)
    out_rows, grad_rows = out_rows.astype(BF), grad_rows.astype(BF)
    sources = out_rows.shape[0] // pad
    cuts = len(outs) // sources
    for i in range(sources):
        at = slice(i * pad, (i + 1) * pad)
        packed = (dot(pack_out, out_rows[at]) + dot(pack_grad, grad_rows[at])).astype(BF)
        cut = packed.shape[1] // cuts
        for j in range(cuts):
            outs[i * cuts + j][...] = packed[:, j * cut : (j + 1) * cut]


def down_step(ids, own, core, weights, count, capacity):
    def kernel(ids, own, core, w_in, w_out, *outs):
        out_rows, grad_rows = half_rows(ids[1], own, w_in, w_out)
        more_out, more_grad = half_rows(1 - ids[1], core, w_in, w_out)
        pack(capacity, out_rows + more_out, grad_rows + more_grad, outs)

    shape = jax.ShapeDtypeStruct((2 * capacity, weights[1].shape[1]), BF)
    return [[x] for x in call(kernel, "down", [shape] * count, [ids], own, core, *weights)]


def down_own(ids, own, weights):
    def kernel(ids, own, w_in, w_out, out_rows, grad_rows):
        out_rows[...], grad_rows[...] = half_rows(ids[1], own, w_in, w_out)

    shape = jax.ShapeDtypeStruct((own.shape[0], weights[1].shape[1]), F32)
    return call(kernel, "down", [shape] * 2, [ids], own, *weights)


def down_own_alone(ids, own, w_in, w_out):
    shape = jax.ShapeDtypeStruct
    whole = pl.BlockSpec(memory_space=pltpu.VMEM)
    away = pl.BlockSpec(memory_space=pl.ANY)

    def kernel(ids, own, far_in, far_out, out_rows, grad_rows, near_in, near_out, sems):
        copies = weight_copies((ids[1], 1 - ids[1]), far_in, far_out, near_in, near_out, sems)
        for copy in copies[: 3 * PIECES]:
            copy.wait()
        out_rows[...], grad_rows[...] = half_rows(ids[1], own, near_in, near_out)
        for copy in copies[3 * PIECES :]:
            copy.wait()

    sums = shape((own.shape[0], w_out.shape[1]), F32)
    return pl.pallas_call(
        kernel,
        out_shape=[sums, sums, shape(w_in.shape, BF), shape(w_out.shape, BF)],
        in_specs=[pl.BlockSpec(memory_space=pltpu.SMEM), whole] + [away] * 2,
        out_specs=[whole] * 4,
        scratch_shapes=[pltpu.SemaphoreType.DMA((6 * PIECES,))],
        compiler_params=pltpu.CompilerParams(vmem_limit_bytes=VMEM_LIMIT),
        cost_estimate=COST,
        name="down",
    )(ids, own, w_in, w_out)


def down_other(ids, out_rows, grad_rows, core, weights, count, capacity, cuts=1):
    def kernel(ids, out_rows, grad_rows, core, w_in, w_out, *outs):
        more_out, more_grad = half_rows(1 - ids[1], core, w_in, w_out)
        pack(capacity, out_rows[...] + more_out, grad_rows[...] + more_grad, outs)

    shape = jax.ShapeDtypeStruct((2 * capacity, weights[1].shape[1] // cuts), BF)
    outs = call(kernel, "down", [shape] * (count * cuts), [ids], out_rows, grad_rows, core, *weights)
    return [outs[i * cuts : (i + 1) * cuts] for i in range(count)]


def grads_kernel(count, ids, *refs):
    groups = [refs[4 * i : 4 * i + 4] for i in range(count)]
    grad_in, grad_out, rows, grads, own, core, tiles_in, tiles_out, sems = refs[4 * count :]
    at = 0
    for group in groups:
        n = group[0].shape[0]
        for held, part in zip((rows, grads, own, core), group):
            held[at : at + n, :] = part[...]
        at += n
    features, units = rows.shape[1], grad_out.shape[0]
    f_tile, width = features // 4, units // 4
    copies = []
    for j in range(4):
        turned = rows[:, j * f_tile : (j + 1) * f_tile].T
        for held, half in ((own, ids[1]), (core, 1 - ids[1])):
            for i in range(2):
                both = dot(turned, held[:, (3 * i + 1) * width : (3 * i + 3) * width]).astype(BF)
                for part in range(2):
                    to = pl.multiple_of(part * units + (half * 2 + i) * width, width)
                    tiles_in[j, :, pl.ds(to, width)] = both[:, part * width : (part + 1) * width]
        copies.append(pltpu.make_async_copy(tiles_in.at[j], grad_in.at[j * f_tile : (j + 1) * f_tile, :], sems.at[j]))
        copies[-1].start()
    for j, (held, half) in enumerate(((own, ids[1]), (core, 1 - ids[1]))):
        for i in range(2):
            turned = held[:, 3 * i * width : (3 * i + 1) * width].T
            tiles_out[2 * j + i] = dot(turned, grads[...]).astype(BF)
            to = pl.multiple_of((half * 2 + i) * width, width)
            copies.append(pltpu.make_async_copy(tiles_out.at[2 * j + i], grad_out.at[pl.ds(to, width), :], sems.at[4 + 2 * j + i]))
            copies[-1].start()
    for copy in copies:
        copy.wait()


def grads_step(ids, groups, units):
    features = groups[0][0].shape[1]
    rows = sum(group[0].shape[0] for group in groups)
    whole = pl.BlockSpec(memory_space=pltpu.VMEM)
    arrays = [x for group in groups for x in group]
    return pl.pallas_call(
        lambda *refs: grads_kernel(len(groups), *refs),
        out_shape=[
            jax.ShapeDtypeStruct((features, 2 * units), BF),
            jax.ShapeDtypeStruct((units, features), BF),
        ],
        in_specs=[pl.BlockSpec(memory_space=pltpu.SMEM)] + [whole] * len(arrays),
        out_specs=[pl.BlockSpec(memory_space=pltpu.HBM)] * 2,
        scratch_shapes=[
            pltpu.VMEM((rows, features), BF),
            pltpu.VMEM((rows, features), BF),
            pltpu.VMEM((rows, units * 3 // 2), BF),
            pltpu.VMEM((rows, units * 3 // 2), BF),
            pltpu.VMEM((4, features // 4, 2 * units), BF),
            pltpu.VMEM((4, units // 4, features), BF),
            pltpu.SemaphoreType.DMA((8,)),
        ],
        compiler_params=pltpu.CompilerParams(vmem_limit_bytes=GRADS_LIMIT),
        cost_estimate=COST,
        name="grads",
    )(ids, *arrays)


def final_kernel(capacity, sources, parts, ids, routes, weight, *refs):
    taken, cuts = sum(parts), max(parts)
    partial, (mixed, grad_tokens) = refs[taken:-2], refs[-2:]
    homes = [refs[sum(parts[:i]) : sum(parts[: i + 1])] for i in range(len(parts))]
    rows = routes.shape[1]
    me = ids[0]
    count = len(sources)
    eye = iota((rows, rows), 0) == iota((rows, rows), 1)

    def column(line, zero):
        return jnp.sum(jnp.where(eye, line, zero), axis=1, keepdims=True)

    lane = iota((rows, count), 1)
    expert = lane * 0
    for i, s in enumerate(sources):
        expert = jnp.where(lane == i, s, expert)
    expert = expert ^ me
    named, w_named = None, None
    for k in range(routes.shape[0]):
        hit = column(routes[k : k + 1, :], 0) == expert
        w_hit = jnp.where(hit, column(weight[k : k + 1, :], 0.0), 0.0)
        named = hit if named is None else named | hit
        w_named = w_hit if w_named is None else w_named + w_hit
    before = (iota((rows, rows), 1) < iota((rows, rows), 0)).astype(BF)
    rank = dot(before, named.astype(F32).astype(BF)).astype(jnp.int32)
    key = jnp.where(named, rank, -2 * capacity)
    slot = iota((rows, 2 * capacity), 1)
    width = mixed.shape[1] // cuts
    for j in range(cuts):
        at = slice(j * width, (j + 1) * width)
        total_out, total_grad = (p[:, at] for p in partial) if partial else (None, None)
        for i in range(count):
            home = homes[i][j][...] if len(homes[i]) == cuts else homes[i][0][:, at]
            row_key = key[:, i : i + 1]
            pick_out = (row_key == slot).astype(F32).astype(BF)
            pick_grad = (row_key + capacity == slot).astype(F32).astype(BF)
            out = w_named[:, i : i + 1] * dot(pick_out, home)
            grad = dot(pick_grad, home)
            total_out = out if total_out is None else total_out + out
            total_grad = grad if total_grad is None else total_grad + grad
        mixed[:, at] = total_out.astype(mixed.dtype)
        grad_tokens[:, at] = total_grad.astype(mixed.dtype)


def final(ids, routes, weight, homes, sources, capacity, partial, dtype):
    parts = [len(home) for home in homes]
    shape = (routes.shape[0], homes[0][0].shape[1] * parts[0])
    return call(
        lambda *refs: final_kernel(capacity, sources, parts, *refs),
        "final",
        [jax.ShapeDtypeStruct(shape, dtype)] * 2,
        [ids],
        routes.T,
        weight.T,
        *[x for home in homes for x in home],
        *partial,
    )


def per_device_chunked(tokens, routes, route_weight, cotangent, w_in, w_out):
    tok_rows = tokens.shape[0]
    top_count = routes.shape[1]
    n_expert = lax.axis_size("expert")
    n_dp = lax.axis_size("dp")
    capacity = tok_rows * top_count * 5 // (4 * n_expert)
    w_in, w_out = w_in[0], w_out[0]
    units = w_out.shape[0]
    ids = jnp.stack([lax.axis_index("expert"), lax.axis_index("dp") % 2]).astype(jnp.int32)

    def across(x, s):
        return lax.ppermute(x, "expert", [(i, i ^ s) for i in range(n_expert)]) if s else x

    def beside(x, s):
        return lax.ppermute(x, "dp", [(i, i ^ s) for i in range(n_dp)])

    def after(x, *earlier):
        return lax.optimization_barrier((x, *earlier))[0]

    def after(x, *earlier):
        return lax.optimization_barrier((x, *earlier))[0]

    inside = lax.axis_index("expert") >= 0

    def stage(body, *args):
        shapes = jax.eval_shape(body, *args)
        return lax.cond(inside, body, lambda *_: jax.tree.map(lambda x: jnp.zeros(x.shape, x.dtype), shapes), *args)

    def up_part(blocks, weights, *earlier):
        first, *others = blocks
        return up_step(ids, [after(first, *earlier), *others], weights, capacity)

    def core_part(state, *earlier):
        rows, grads, send, keep = state
        return rows, grads, keep, beside(after(send, *earlier) if earlier else send, 1)

    def up_in_halves(blocks):
        rows, grads, send, *weights = other_half(ids, blocks, w_in, w_out, capacity)
        core = beside(send, 1)
        return (rows, grads, own_half(ids, after(rows, send), grads, weights), core), weights

    def sum_part(state, *earlier, cuts=1):
        rows, grads, keep, core = state
        return rows, grads, keep, core, sum_step(after(keep, *earlier), core, cuts)

    def x_part(state):
        rows, grads, keep, core, totals = state
        return rows, grads, keep, core, [beside(total, 2) for total in totals]

    def act_part(state, *earlier):
        rows, grads, keep, core, others = state
        own = act_step(after(keep, *earlier), core, others)
        return rows, grads, own, beside(own, 1)

    def down_part(group, weights, count):
        return down_step(ids, *group[2:], weights, count, capacity)

    def down_in_halves(group, weights, count):
        _, _, own, core = group
        sums = down_own(ids, own, weights)
        return down_other(ids, *sums, after(core, *sums), weights, count, capacity)

    def act_both(state, next_state, *earlier):
        rows, grads, keep, core, (other,) = state
        own, next_total = act_and_sum(after(keep, *earlier), core, other, *next_state[2:])
        return (rows, grads, own, beside(own, 1)), (*next_state, [next_total])

    def first_stage(blocks):
        state, _ = up_in_halves(blocks)
        return sum_part(state, cuts=2)

    def far_stage(blocks, before, before_count, next_blocks):
        state, held = up_in_halves(blocks)
        state = sum_part(state)
        before = act_part(before, *state[4])
        next_state = up_part(next_blocks, held, before[2])
        back = down_part((*before[:2], after(before[2], next_state[2]), before[3]), held, before_count)
        ends = [x for parts in back for x in parts]
        group, next_state = act_both(x_part(state), core_part(next_state, *ends), *ends)
        return group, down_in_halves(group, held, len(blocks)), next_state, before, back

    def rest_stage(state):
        group = act_part(state)
        _, _, own, core = group
        *sums, held_in, held_out = down_own_alone(ids, own, w_in, w_out)
        return group, down_other(ids, *sums, after(core, *sums), (held_in, held_out), size, capacity, 2)

    half, quarter = n_expert // 2, n_expert // 4
    size = quarter // 2
    near = [list(range(quarter)), list(range(quarter, quarter + size)), list(range(quarter + size, half))]
    far, last = list(range(half, half + quarter)), list(range(half + quarter, n_expert))
    sent = prep(ids, tokens, routes, route_weight, cotangent, n_expert, capacity)
    came, home = {0: sent[0]}, {}

    def blocks(sources, *earlier):
        first, *others = [came[s] for s in sources]
        return [after(first, *earlier), *others]

    def start(sources, *earlier):
        came.update({s: across(after(sent[s], *earlier) if earlier else sent[s], s) for s in sources if s})

    def start_back(sources, back, *earlier):
        for s, parts in zip(sources, back):
            home[s] = [across(after(x, *earlier) if earlier else x, s) for x in parts]

    def arrived(sources):
        return [x for s in sources for x in home[s]]

    start(far + near[0] + near[1])
    state_0 = stage(first_stage, blocks(near[0]))
    start(last, *blocks(far + near[1]), *state_0[4])
    state_0 = x_part(state_0)
    start(near[2], *blocks(far), *state_0[4])
    group_far, back_far, state_1, group_0, back_0 = stage(
        lambda a, b, c: far_stage(a, b, quarter, c), blocks(far), state_0, blocks(near[1])
    )
    start_back(far, back_far, *blocks(last))
    start_back(near[0], back_0, *blocks(last))
    group_last, back_last, state_2, group_1, back_1 = stage(
        lambda a, b, c: far_stage(a, b, size, c), blocks(last, group_far[3]), x_part(state_1), blocks(near[2])
    )
    start_back(last, back_last, *arrived(far))
    start_back(near[1], back_1)
    group_2, back_2 = stage(rest_stage, x_part(state_2))
    start_back(near[2], back_2)

    def add(sources, partial, dtype):
        return final(ids, routes, route_weight, [home[s] for s in sources], sources, capacity, partial, dtype)

    groups = [group_0, group_far, group_1, group_last, group_2]
    grad_in, grad_out = grads_step(ids, groups, units)
    partial = add(near[0] + far, [], F32)
    partial = add(last, partial, F32)
    mixed, grad_tokens = add(near[1] + near[2], partial, BF)
    return mixed, grad_tokens, grad_in[None], grad_out[None]


def activate(pre_act, grad_hidden):
    units = pre_act.shape[1] // 2
    gate_part = pre_act[:, :units]
    up_part = pre_act[:, units:]
    sigmoid_gate = jax.nn.sigmoid(gate_part)
    silu_gate = gate_part * sigmoid_gate
    hidden = (silu_gate * up_part).astype(jnp.bfloat16)
    grad_gate = grad_hidden * up_part * sigmoid_gate * (1.0 + gate_part * (1.0 - sigmoid_gate))
    grad_up = grad_hidden * silu_gate
    return (hidden, jnp.concatenate([grad_gate, grad_up], axis=1).astype(jnp.bfloat16))


def per_device(tokens, routes, route_weight, cotangent, w_in, w_out):
    tok_rows, features = tokens.shape
    top_count = routes.shape[1]
    n_expert = lax.axis_size("expert")
    local_experts = w_in.shape[0]
    hidden_units = w_out.shape[1]
    experts = n_expert * local_experts
    capacity = tok_rows * top_count * 5 // (4 * experts)
    slot_count = experts * capacity
    flat_routes = routes.reshape(-1)
    onehot = (flat_routes[:, None] == jnp.arange(experts, dtype=jnp.int32)[None, :]).astype(
        jnp.int32
    )
    slot_rank = jnp.sum((jnp.cumsum(onehot, axis=0) - onehot) * onehot, axis=1)
    target = flat_routes * capacity + slot_rank
    placing = (target[None, :] == jnp.arange(slot_count, dtype=jnp.int32)[:, None]).astype(
        jnp.bfloat16
    )
    choose_token = jnp.sum(placing.reshape(slot_count, tok_rows, top_count), axis=2)
    scaled_grads = (route_weight[:, :, None] * cotangent[:, None, :].astype(jnp.float32)).astype(
        jnp.bfloat16
    )
    scaled_grads = scaled_grads.reshape(tok_rows * top_count, features)
    send_rows = jnp.dot(choose_token, tokens, preferred_element_type=jnp.float32).astype(
        jnp.bfloat16
    )
    send_grads = jnp.dot(placing, scaled_grads, preferred_element_type=jnp.float32).astype(
        jnp.bfloat16
    )
    send_rows = send_rows.reshape(n_expert, local_experts * capacity, features)
    send_grads = send_grads.reshape(n_expert, local_experts * capacity, features)
    routed_rows, routed_grads = (
        lax.all_to_all(send_rows, "expert", split_axis=0, concat_axis=0, tiled=True),
        lax.all_to_all(send_grads, "expert", split_axis=0, concat_axis=0, tiled=True),
    )
    rows_four = routed_rows.reshape(n_expert, local_experts, capacity, features)
    grads_four = routed_grads.reshape(n_expert, local_experts, capacity, features)
    total_rows = n_expert * local_experts * capacity
    pre_part = jnp.einsum("secd,edf->secf", rows_four, w_in, preferred_element_type=jnp.float32)
    back_part = jnp.einsum("secd,efd->secf", grads_four, w_out, preferred_element_type=jnp.float32)
    pre_flat = pre_part.reshape(total_rows, 2 * hidden_units)
    back_flat = back_part.reshape(total_rows, hidden_units)
    pre_share, back_share = (
        lax.psum_scatter(pre_flat, "dp", scatter_dimension=0, tiled=True),
        lax.psum_scatter(back_flat, "dp", scatter_dimension=0, tiled=True),
    )
    hidden_share, both_share = activate(pre_share, back_share)
    hidden, grad_both = (
        lax.all_gather(hidden_share, "dp", axis=0, tiled=True),
        lax.all_gather(both_share, "dp", axis=0, tiled=True),
    )
    hidden_four = hidden.reshape(n_expert, local_experts, capacity, hidden_units)
    both_four = grad_both.reshape(n_expert, local_experts, capacity, 2 * hidden_units)
    out_rows = jnp.einsum(
        "secf,efd->secd", hidden_four, w_out, preferred_element_type=jnp.float32
    ).astype(jnp.bfloat16)
    grad_rows = jnp.einsum(
        "secf,edf->secd", both_four, w_in, preferred_element_type=jnp.float32
    ).astype(jnp.bfloat16)
    grad_out = jnp.einsum(
        "secf,secd->efd", hidden_four, grads_four, preferred_element_type=jnp.float32
    ).astype(jnp.bfloat16)
    grad_in = jnp.einsum(
        "secd,secf->edf", rows_four, both_four, preferred_element_type=jnp.float32
    ).astype(jnp.bfloat16)
    home_out, home_grad = (
        lax.all_to_all(
            out_rows.reshape(n_expert, local_experts * capacity, features),
            "expert",
            split_axis=0,
            concat_axis=0,
            tiled=True,
        ),
        lax.all_to_all(
            grad_rows.reshape(n_expert, local_experts * capacity, features),
            "expert",
            split_axis=0,
            concat_axis=0,
            tiled=True,
        ),
    )
    route_out = jnp.dot(
        placing.T, home_out.reshape(slot_count, features), preferred_element_type=jnp.float32
    )
    route_out = route_out.reshape(tok_rows, top_count, features)
    mixed = jnp.sum(route_weight[:, :, None] * route_out, axis=1).astype(jnp.bfloat16)
    grad_tokens = jnp.dot(
        choose_token.T, home_grad.reshape(slot_count, features), preferred_element_type=jnp.float32
    )
    return (mixed, grad_tokens.astype(jnp.bfloat16), grad_in, grad_out)


def solution(mesh):
    placed = (
        P("expert", "dp"),
        P("expert", None),
        P("expert", None),
        P("expert", "dp"),
        P("expert", "dp", None),
        P("expert", None, "dp"),
    )
    sizes = dict(mesh.shape)
    chunked = sizes["dp"] == 4 and sizes["expert"] in (8, 16)
    return jax.shard_map(
        per_device_chunked if chunked else per_device,
        mesh=mesh,
        in_specs=placed,
        out_specs=(
            P("expert", "dp"),
            P("expert", "dp"),
            P("expert", "dp", None),
            P("expert", None, "dp"),
        ),
        check_vma=False,
    )
```
